32 devices in a mesh: fsdp: 8 (over z, y), dp: 4 (over x, core).
Axes of the slice: x: 2, y: 2, z: 4, core: 2. Of those that a mesh axis runs over, the one named last changes fastest.
Arguments:
- image: bfloat16 [128, 16, 16, 256], P(('fsdp', 'dp')), may hold values from -6 to 6
- timesteps: int32 [128], P(('fsdp', 'dp')), may hold values from 0 to 999
- time_table: float32 [1000, 512], replicated, may hold values from -6 to 6
- conv_first: bfloat16 [2304, 256], P('fsdp'), may hold values from -0.125 to 0.125
- embed_weight: bfloat16 [512, 256], P('fsdp'), may hold values from -0.25 to 0.25
- conv_second: bfloat16 [2304, 256], P('fsdp'), may hold values from -0.125 to 0.125
- qkv_weight: bfloat16 [256, 768], P('fsdp'), may hold values from -0.375 to 0.375
- out_weight: bfloat16 [256, 256], P('fsdp'), may hold values from -1 to 1
- vectors: bfloat16 [12, 256], P(None, 'fsdp'), may hold values from -2.5 to 2.5
- cotangent: bfloat16 [128, 16, 16, 256], P(('fsdp', 'dp')), may hold values from -6 to 6
Outputs:
- output: bfloat16 [128, 16, 16, 256], P(('fsdp', 'dp'))
- image_grad: bfloat16 [128, 16, 16, 256], P(('fsdp', 'dp'))
- table_grad: float32 [1000, 512], replicated
- conv_first_grad: float32 [2304, 256], P('fsdp')
- embed_grad: float32 [512, 256], P('fsdp')
- conv_second_grad: float32 [2304, 256], P('fsdp')
- qkv_grad: float32 [256, 768], P('fsdp')
- out_grad: float32 [256, 256], P('fsdp')
- vectors_grad: float32 [12, 256], P(None, 'fsdp')
The draws below stay inside these ranges and needn't reach their ends.
All inputs are finite; a program needn't handle non-finite values.
Results may differ from the reference program's by a relative error of at most 0.018.
Values may be sent and summed in bfloat16 or wider, within the bound.
A program may use at most 128 MiB of HBM per device.

```python
import jax
import jax.numpy as jnp
from jax import lax

C = 256
TEMB = 512
GROUPS = 32
SIDE = 16
TSTEPS = 1000
BATCH = 128


def with_ends(entries, key, smallest, top_value):
    dims = entries.shape
    spot = [jax.random.randint(jax.random.fold_in(key, axis), (), 0, dims[axis]) for axis in range(len(dims))]
    entries = entries.at[tuple(spot)].set(smallest)
    longest = dims.index(max(dims))
    spot[longest] = (spot[longest] + 1) % dims[longest]
    return entries.at[tuple(spot)].set(top_value)


def steps_of(own_key, shape, pieces, least, top_value):
    def one(dim, parts):
        steps = jax.random.uniform(jax.random.fold_in(jax.random.fold_in(own_key, 6), dim), (parts,), jnp.float32, least / len(pieces), top_value / len(pieces))
        return jnp.repeat(jnp.exp(steps), shape[dim] // parts).reshape((-1,) + (1,) * (len(shape) - dim - 1))

    level = one(*pieces[0])
    for cut in pieces[1:]:
        level = level * one(*cut)
    return level


def noise(rng, dims, width, limit, split=(), held_as=jnp.bfloat16):
    factor_of = steps_of(rng, dims, split, -0.22, 0.18) if split else 1.0
    values = jax.random.normal(rng, dims, jnp.float32) * width * factor_of
    return jnp.minimum(jnp.maximum(values, -limit), limit).astype(held_as)


def setup_inputs(seed: int = 0) -> dict:
    splits = jax.random.split(jax.random.key(seed), 11)
    image = noise(splits[0], (BATCH, SIDE, SIDE, C), 1.0, 6.0, ((0, 32),))
    timesteps = with_ends(jax.random.randint(splits[1], (BATCH,), 0, TSTEPS), jax.random.fold_in(splits[1], 1), 0, TSTEPS - 1).astype(jnp.int32)
    time_table = noise(splits[2], (TSTEPS, TEMB), 1.0, 6.0, (), jnp.float32)
    conv_first = noise(splits[3], (9 * C, C), (9 * C) ** -0.5, 0.125, ((0, 8),))
    embed_weight = noise(splits[4], (TEMB, C), TEMB ** -0.5, 0.25, ((0, 8),))
    conv_second = noise(splits[5], (9 * C, C), (9 * C) ** -0.5, 0.125, ((0, 8),))
    qkv_weight = noise(splits[6], (C, 3 * C), C ** -0.5, 0.375, ((0, 8),))
    out_weight = noise(splits[7], (C, C), (C // 8) ** -0.5, 1.0, ((0, 8),))
    vectors = noise(splits[8], (12, C), 0.3, 2.5, ((1, 8),))
    cotangent = noise(splits[9], (BATCH, SIDE, SIDE, C), 1.0, 6.0, ((0, 32),))
    return {"image": image, "timesteps": timesteps, "time_table": time_table, "conv_first": conv_first, "embed_weight": embed_weight, "conv_second": conv_second, "qkv_weight": qkv_weight, "out_weight": out_weight, "vectors": vectors, "cotangent": cotangent}


@jax.custom_vjp
def low(v):
    return lax.optimization_barrier(v.astype(jnp.bfloat16)).astype(jnp.float32)

@jax.custom_vjp
def low_back(v):
    return v

def low_keep(v):
    return (low(v), None)

def low_pass(kept, grad):
    return (grad,)

def back_keep(v):
    return (v, None)

def back_low(kept, grad):
    return (low(grad),)
low.defvjp(low_keep, low_pass)
low_back.defvjp(back_keep, back_low)
EPS = 1e-06
HIGH = lax.Precision.HIGHEST

def swish(v):
    return v * jax.nn.sigmoid(v)

def spread_groups(chan):
    count = chan.shape[0]
    grouped = lax.optimization_barrier(jnp.mean(chan.reshape(count, GROUPS, C // GROUPS), axis=2))
    return jnp.repeat(grouped, C // GROUPS, axis=1)[:, None, None, :]

def group_norm(u, gain, shift):
    mean = spread_groups(lax.optimization_barrier(jnp.mean(u, axis=(1, 2))))
    centered = u - mean
    var = spread_groups(lax.optimization_barrier(jnp.mean(centered * centered, axis=(1, 2))))
    return centered * lax.rsqrt(var + EPS) * (1.0 + gain) + shift

def convolve(a, w):
    kernel = w.reshape(3, 3, C, C)
    return lax.conv_general_dilated(a, kernel, (1, 1), ((1, 1), (1, 1)), dimension_numbers=('NHWC', 'HWIO', 'NHWC'), precision=HIGH)

def layer(x, table, w_first, w_embed, w_second, w_mixed, w_out, vec, steps):
    count = x.shape[0]
    a1 = low(swish(group_norm(x, vec[0], vec[1])))
    e = low(swish(table[steps]))
    proj = low_back(jnp.dot(e, w_embed, precision=HIGH) + vec[3])
    h1 = low_back(convolve(a1, w_first) + vec[2] + proj[:, None, None, :])
    a2 = low(swish(group_norm(h1, vec[4], vec[5])))
    resid = x + low_back(convolve(a2, w_second) + vec[6])
    nrm = low(group_norm(resid, vec[7], vec[8])).reshape(count, SIDE * SIDE, C)
    mixed = jnp.einsum('npc,cd->npd', nrm, w_mixed, precision=HIGH)
    query = low(low_back(mixed[..., :C] + vec[9]))
    key_part = low(low_back(mixed[..., C:2 * C]))
    value = low(low_back(mixed[..., 2 * C:] + vec[10]))
    scores = low_back(jnp.einsum('nqc,nkc->nqk', query, key_part, precision=HIGH) * C ** (-0.5))
    probs = jax.nn.softmax(scores, axis=-1)
    att = low(low_back(jnp.einsum('nqk,nkc->nqc', low(probs), value, precision=HIGH)))
    branch = jnp.einsum('npc,cd->npd', att, w_out, precision=HIGH) + vec[11]
    return resid + branch.reshape(x.shape)

def reference(image, timesteps, time_table, conv_first, embed_weight, conv_second, qkv_weight, out_weight, vectors, cotangent):
    count = BATCH // 16
    images = image.reshape(count, 16, SIDE, SIDE, C)
    steps_all = timesteps.reshape(count, 16)
    cots = cotangent.reshape(count, 16, SIDE, SIDE, C)
    params = (time_table, conv_first.astype(jnp.float32), embed_weight.astype(jnp.float32), conv_second.astype(jnp.float32), qkv_weight.astype(jnp.float32), out_weight.astype(jnp.float32), vectors.astype(jnp.float32))

    def step(totals, item):
        x_group, step_group, cot_group = item

        def forward(x32, table, w_first, w_embed, w_second, w_mixed, w_out, vec):
            return layer(x32, table, w_first, w_embed, w_second, w_mixed, w_out, vec, step_group)
        result, pull = jax.vjp(forward, x_group.astype(jnp.float32), *params)
        grads = pull(cot_group.astype(jnp.float32))
        totals = tuple((a + b for a, b in zip(totals, grads[1:])))
        return (totals, (result.astype(jnp.bfloat16), grads[0].astype(jnp.bfloat16)))
    zeros = tuple((jnp.zeros_like(p) for p in params))
    totals, (outputs, image_grads) = lax.scan(step, zeros, (images, steps_all, cots))
    return (outputs.reshape(image.shape), image_grads.reshape(image.shape), totals[0], totals[1], totals[2], totals[3], totals[4], totals[5], totals[6])
```

```python
import functools

import jax
import jax.numpy as jnp
from jax import lax
from jax.experimental import pallas as pl
from jax.experimental.pallas import tpu as pltpu
from jax.sharding import PartitionSpec as P

F32 = jnp.float32
BF16 = jnp.bfloat16
MESH = pl.DeviceIdType.MESH
EPS = 1e-06
WIDTH = 256
GROUP = 8
TEMB = 512
TAPS = 9 * WIDTH
EXTRA = TEMB + 128
VMEM_BYTES = 56 * 2**20
NT = (((1,), (1,)), ((), ()))
TN = (((0,), (0,)), ((), ()))


def dot(a, b):
    return jnp.dot(a, b, preferred_element_type=F32)


def dot_nt(a, b):
    return lax.dot_general(a, b, NT, preferred_element_type=F32)


def split3(v):
    high = v.astype(BF16)
    rest = v - high.astype(F32)
    mid = rest.astype(BF16)
    return high, mid, (rest - mid.astype(F32)).astype(BF16)


def colsum(v):
    return jnp.sum(v, axis=0, keepdims=True)


def group_mean(row, averager):
    high, mid, low = split3(row)
    return dot(high, averager) + dot(mid, averager) + dot(low, averager)


class Refs:
    def __init__(self, names, refs, count, side):
        for name, ref in zip(names, refs):
            setattr(self, name, ref)
        self.count, self.side, self.places = count, side, side * side

    def rows(self, m):
        return pl.ds(m * self.places, self.places)


def scratch_of(count, side):
    places = side * side
    total = count * places
    padded = places + 2 * side
    return {
        "averager": ((WIDTH, WIDTH), BF16),
        "shifted_a": ((count, padded, 3 * WIDTH), BF16),
        "shifted_g": ((count, padded, 3 * WIDTH), BF16),
        "unit1": ((total, WIDTH), F32),
        "slope1": ((total, WIDTH), F32),
        "inv1": ((count, 1, WIDTH), F32),
        "unit2": ((total, WIDTH), F32),
        "slope2": ((total, WIDTH), F32),
        "inv2": ((count, 1, WIDTH), F32),
        "unit3": ((total, WIDTH), F32),
        "inv3": ((count, 1, WIDTH), F32),
        "a1_t": ((WIDTH, total), BF16),
        "a2_t": ((WIDTH, total), BF16),
        "nrm_t": ((WIDTH, total), BF16),
        "att_t": ((WIDTH, total), BF16),
        "conv_out": ((total, WIDTH), F32),
        "resid": ((total, WIDTH), F32),
        "g_mixed": ((total, 3 * WIDTH), BF16),
        "proj": ((8, WIDTH), F32),
        "sums": ((16, WIDTH), F32),
        "g_proj": ((8, WIDTH), F32),
    }


def start_compute(k):
    rows = lax.broadcasted_iota(jnp.int32, (WIDTH, WIDTH), 0) // GROUP
    cols = lax.broadcasted_iota(jnp.int32, (WIDTH, WIDTH), 1) // GROUP
    k.averager[...] = jnp.where(rows == cols, 1.0 / (k.places * GROUP), 0.0).astype(BF16)
    edge = jnp.zeros((k.count, k.side, 3 * WIDTH), BF16)
    for ref in (k.shifted_a, k.shifted_g):
        ref[:, 0 : k.side, :] = edge
        ref[:, k.places + k.side : k.places + 2 * k.side, :] = edge
    k.sums[...] = jnp.zeros(k.sums.shape, F32)
    k.g_proj[...] = jnp.zeros(k.g_proj.shape, F32)


def store_shifted(k, ref, m, a):
    column = lax.broadcasted_iota(jnp.int32, a.shape, 0) % k.side
    inner = slice(k.side, k.side + k.places)
    left = jnp.where(column == 0, 0.0, pltpu.roll(a, 1, 0))
    right = jnp.where(column == k.side - 1, 0.0, pltpu.roll(a, k.places - 1, 0))
    ref[m, inner, 0:WIDTH] = left.astype(BF16)
    ref[m, inner, WIDTH : 2 * WIDTH] = a.astype(BF16)
    ref[m, inner, 2 * WIDTH : 3 * WIDTH] = right.astype(BF16)


def normalize(k, u):
    averager = k.averager[...]
    centered = u - group_mean(colsum(u), averager)
    inverse = lax.rsqrt(group_mean(colsum(centered * centered), averager) + EPS)
    return centered * inverse, inverse


def norm_swish(k, u, m, j, unit_ref, slope_ref, inv_ref):
    unit, inverse = normalize(k, u)
    unit_ref[k.rows(m), :] = unit
    inv_ref[m] = inverse
    h = unit * (1.0 + k.vec[j : j + 1, :]) + k.vec[j + 1 : j + 2, :]
    sig = jax.nn.sigmoid(h)
    a = h * sig
    slope_ref[k.rows(m), :] = sig + a * (1.0 - sig)
    return a


def norm_back(k, upstream, unit, inverse, j):
    averager = k.averager[...]
    g_gain = colsum(upstream * unit)
    g_shift = colsum(upstream)
    k.sums[j : j + 1, :] += g_gain
    k.sums[j + 1 : j + 2, :] += g_shift
    gain = 1.0 + k.vec[j : j + 1, :]
    first = group_mean(g_shift * gain, averager)
    second = group_mean(g_gain * gain, averager)
    return inverse * (upstream * gain - first - unit * second)


def convolve(k, ref, w, m):
    total = None
    for ky in range(3):
        window = ref[m, ky * k.side : ky * k.side + k.places, :]
        term = dot(window, w[ky * 3 * WIDTH : (ky + 1) * 3 * WIDTH, :])
        total = term if total is None else total + term
    return total


def convolve_back(k, ref, w, m):
    total = None
    for ky in range(3):
        for kx in range(3):
            window = ref[
                m,
                (2 - ky) * k.side : (2 - ky) * k.side + k.places,
                (2 - kx) * WIDTH : (3 - kx) * WIDTH,
            ]
            tap = 3 * ky + kx
            term = dot_nt(window, w[tap * WIDTH : (tap + 1) * WIDTH, :])
            total = term if total is None else total + term
    return total


def kernel_grad(k, a_t, g_w):
    for ky in range(3):
        window = k.shifted_g[:, (2 - ky) * k.side : (2 - ky) * k.side + k.places, :]
        term = dot(a_t[...], window.reshape(k.count * k.places, 3 * WIDTH))
        for kx in range(3):
            tap = 3 * ky + kx
            g_w[tap * WIDTH : (tap + 1) * WIDTH, :] = term[
                :, (2 - kx) * WIDTH : (3 - kx) * WIDTH
            ].astype(BF16)


def first_norm(k, m):
    a = norm_swish(k, k.x[k.rows(m), :].astype(F32), m, 0, k.unit1, k.slope1, k.inv1)
    store_shifted(k, k.shifted_a, m, a)
    k.a1_t[:, k.rows(m)] = a.astype(BF16).T


def embed(k, pre):
    e = (pre * jax.nn.sigmoid(pre)).astype(BF16)
    k.proj[...] = dot(e, k.w_embed[...]) + k.vec[3:4, :]


def first_conv(k, m):
    k.conv_out[k.rows(m), :] = convolve(k, k.shifted_a, k.w_first, m) + (
        k.vec[2:3, :] + k.proj[m : m + 1, :]
    )


def second_norm(k, m):
    a = norm_swish(k, k.conv_out[k.rows(m), :], m, 4, k.unit2, k.slope2, k.inv2)
    store_shifted(k, k.shifted_a, m, a)
    k.a2_t[:, k.rows(m)] = a.astype(BF16).T


def second_conv(k, m):
    x = k.x[k.rows(m), :].astype(F32)
    k.resid[k.rows(m), :] = x + convolve(k, k.shifted_a, k.w_second, m) + k.vec[6:7, :]


def attention(k, m):
    rows = k.rows(m)
    scale = WIDTH**-0.5
    resid = k.resid[rows, :]
    unit, inverse = normalize(k, resid)
    k.unit3[rows, :] = unit
    k.inv3[m] = inverse
    nrm = (unit * (1.0 + k.vec[7:8, :]) + k.vec[8:9, :]).astype(BF16)
    k.nrm_t[:, rows] = nrm.T
    mixed = dot(nrm, k.w_mixed[...])
    query = (mixed[:, :WIDTH] + k.vec[9:10, :]).astype(BF16)
    key_part = mixed[:, WIDTH : 2 * WIDTH].astype(BF16)
    value = (mixed[:, 2 * WIDTH :] + k.vec[10:11, :]).astype(BF16)
    scores = dot_nt(query, key_part) * scale
    raised = jnp.exp(scores - jnp.max(scores, axis=1, keepdims=True))
    probs = raised * (1.0 / jnp.sum(raised, axis=1, keepdims=True))
    probs_low = probs.astype(BF16)
    att = dot(probs_low, value).astype(BF16)
    k.att_t[:, rows] = att.T
    k.out[rows, :] = (resid + dot(att, k.w_out[...]) + k.vec[11:12, :]).astype(BF16)
    cot = k.cot[rows, :]
    k.sums[11:12, :] += colsum(cot.astype(F32))
    g_att = dot_nt(cot, k.w_out[...]).astype(BF16)
    g_probs = dot_nt(g_att, value)
    g_value = dot(probs_low.T, g_att).astype(BF16)
    weighted = jnp.sum(probs * g_probs, axis=1, keepdims=True)
    g_scores = (probs * (g_probs - weighted)).astype(BF16)
    g_query = (dot(g_scores, key_part) * scale).astype(BF16)
    g_key = (dot(g_scores.T, query) * scale).astype(BF16)
    k.sums[9:10, :] += colsum(g_query.astype(F32))
    k.sums[10:11, :] += colsum(g_value.astype(F32))
    k.g_mixed[rows, 0:WIDTH] = g_query
    k.g_mixed[rows, WIDTH : 2 * WIDTH] = g_key
    k.g_mixed[rows, 2 * WIDTH : 3 * WIDTH] = g_value


def third_norm_back(k, m):
    rows = k.rows(m)
    g_nrm = dot_nt(k.g_mixed[rows, :], k.w_mixed[...])
    g_resid = k.cot[rows, :].astype(F32) + norm_back(
        k, g_nrm, k.unit3[rows, :], k.inv3[m], 7
    )
    k.resid[rows, :] = g_resid
    g_conv = g_resid.astype(BF16).astype(F32)
    k.sums[6:7, :] += colsum(g_conv)
    store_shifted(k, k.shifted_g, m, g_conv)


def second_conv_back(k, m):
    rows = k.rows(m)
    k.conv_out[rows, :] = convolve_back(k, k.shifted_g, k.w_second, m) * k.slope2[rows, :]


def second_norm_back(k, m):
    rows = k.rows(m)
    g_h1 = norm_back(k, k.conv_out[rows, :], k.unit2[rows, :], k.inv2[m], 4)
    g_h1 = g_h1.astype(BF16).astype(F32)
    per_map = colsum(g_h1)
    k.sums[2:3, :] += per_map
    g_proj = per_map.astype(BF16).astype(F32)
    k.sums[3:4, :] += g_proj
    k.g_proj[m : m + 1, :] = g_proj
    store_shifted(k, k.shifted_g, m, g_h1)


def first_conv_back(k, m):
    rows = k.rows(m)
    k.conv_out[rows, :] = convolve_back(k, k.shifted_g, k.w_first, m) * k.slope1[rows, :]


def first_norm_back(k, m):
    rows = k.rows(m)
    g_x = norm_back(k, k.conv_out[rows, :], k.unit1[rows, :], k.inv1[m], 0)
    k.image_grad[rows, :] = (k.resid[rows, :] + g_x).astype(BF16)


def each_map(k, *steps):
    for step in steps:
        for m in range(k.count):
            step(k, m)


class Links:
    def __init__(self, send_sems, recv_sems, local_sems, z_size):
        f, d = lax.axis_index("fsdp"), lax.axis_index("dp")
        self.f, self.z_size = f, z_size
        self.z, self.y = f // 2, f % 2
        self.x, self.c = d // 2, d % 2
        self.send_sems, self.recv_sems, self.local_sems = send_sems, recv_sems, local_sems
        self.started, self.n_sent, self.n_local = [], 0, 0

    def device(self, z=None, y=None, x=None, c=None):
        z = self.z if z is None else z
        y = self.y if y is None else y
        x = self.x if x is None else x
        c = self.c if c is None else c
        return (z * 2 + y, x * 2 + c)

    def ahead(self, offset):
        return lax.rem(self.z + offset, self.z_size)

    def behind(self, offset):
        return lax.rem(self.z + self.z_size - offset, self.z_size)

    @property
    def x_peer(self):
        return self.device(x=1 - self.x)

    @property
    def y_peer(self):
        return self.device(y=1 - self.y)

    @property
    def core_peer(self):
        return self.device(c=1 - self.c)

    def send(self, src, dst, device):
        spot = self.n_sent
        self.n_sent += 1
        copy = pltpu.make_async_remote_copy(
            src_ref=src,
            dst_ref=dst,
            send_sem=self.send_sems.at[spot],
            recv_sem=self.recv_sems.at[spot],
            device_id=device,
            device_id_type=MESH,
        )
        copy.start()
        self.started.append(copy)
        return copy

    def local(self, src, dst):
        copy = pltpu.make_async_copy(src, dst, self.local_sems.at[self.n_local])
        self.n_local += 1
        copy.start()
        return copy

    def finish(self):
        for copy in self.started:
            copy.wait_send()

    def greet(self):
        barrier = pltpu.get_barrier_semaphore()
        peers = [
            self.device(z=self.ahead(o), y=y)
            for o in range(self.z_size)
            for y in (self.y, 1 - self.y)
            if not (o == 0 and y is self.y)
        ]
        peers += [self.x_peer, self.core_peer, self.device(x=1 - self.x, c=1 - self.c)]
        peers += [self.device(x=1 - self.x, y=1 - self.y)]
        for peer in peers:
            pl.semaphore_signal(barrier, inc=1, device_id=peer, device_id_type=MESH)
        return lambda: pl.semaphore_wait(barrier, len(peers))


class Box:
    def __init__(self, rows, lanes, by_rows=None, by_lanes=None):
        self.rows, self.lanes = rows, lanes
        self.half_rows, self.half_lanes = rows // 2, lanes // 2
        cut_r = self.half_rows if by_rows is None else by_rows
        cut_l = self.half_lanes if by_lanes is None else by_lanes
        if by_rows is not None:
            self.colors = [(0, cut_r, 0, self.half_lanes), (cut_r, self.half_rows - cut_r, 0, self.half_lanes)]
        elif by_lanes is not None:
            self.colors = [(0, self.half_rows, 0, cut_l), (0, self.half_rows, cut_l, self.half_lanes - cut_l)]
        else:
            self.colors = [None, (0, self.half_rows, 0, self.half_lanes)]

    def rows_of(self, c, color=None):
        first, size = (0, self.half_rows) if color is None else self.colors[color][:2]
        return pl.ds(pl.multiple_of(c * self.half_rows + first, 16), size)

    def lanes_of(self, x, color=None):
        first, size = (0, self.half_lanes) if color is None else self.colors[color][2:]
        return pl.ds(pl.multiple_of(x * self.half_lanes + first, 128), size)

    def inner(self, color):
        r0, rn, l0, ln = self.colors[color]
        return slice(r0, r0 + rn), slice(l0, l0 + ln)


class Gather:
    def __init__(self, links, box, shard, full):
        self.n, self.box, self.shard, self.full = links, box, shard, full
        self.z_copies, self.parts, self.diag, self.core = {}, {}, {}, []

    def start(self):
        n, box = self.n, self.box
        src = self.shard.at[box.rows_of(n.c), box.lanes_of(n.x)]
        dst = self.full.at[n.z, n.y, box.rows_of(n.c), box.lanes_of(n.x)]
        for o in (1, 3, 2):
            self.z_copies[o] = n.send(src, dst, n.device(z=n.ahead(o)))
        self.own = n.local(src, dst)

    def part(self, o, y, x, color=None):
        n, box = self.n, self.box
        p = slice(None) if o is None else n.behind(o)
        return self.full.at[p, y, box.rows_of(n.c, color), box.lanes_of(x, color)]

    def spread(self, o):
        n = self.n
        if o is None:
            for copy in self.z_copies.values():
                copy.wait_recv()
            self.own.wait()
        elif o == 0:
            self.own.wait()
        else:
            self.z_copies[o].wait_recv()
        mine = self.part(o, n.y, n.x)
        self.parts[o] = (n.send(mine, mine, n.x_peer), n.send(mine, mine, n.y_peer))

    def cross(self, o):
        n = self.n
        from_x, from_y = self.parts[o]
        copies = []
        if self.box.colors[0] is not None:
            from_y.wait_recv()
            block = self.part(o, 1 - n.y, n.x, 0)
            copies.append(n.send(block, block, n.x_peer))
        from_x.wait_recv()
        block = self.part(o, n.y, 1 - n.x, 1)
        copies.append(n.send(block, block, n.y_peer))
        if self.box.colors[0] is None:
            from_y.wait_recv()
        self.diag[o] = copies

    def share(self, o):
        n, box = self.n, self.box
        for copy in self.diag[o]:
            copy.wait_recv()
        p = slice(None) if o is None else n.behind(o)
        block = self.full.at[p, :, box.rows_of(n.c), :]
        self.core.append(n.send(block, block, n.core_peer))

    def finish(self):
        for copy in self.core:
            copy.wait_recv()


class SmallGather:
    def __init__(self, links, block, full):
        self.n, self.block, self.full = links, block, full

    def start(self):
        n = self.n
        dst = self.full.at[n.z, n.y, n.x, n.c]
        self.z_copies = [n.send(self.block, dst, n.device(z=n.ahead(o))) for o in (1, 3, 2)]
        self.own = n.local(self.block, dst)

    def spread(self):
        n = self.n
        for copy in self.z_copies:
            copy.wait_recv()
        self.own.wait()
        mine = self.full.at[:, n.y, n.x, n.c]
        self.from_x, self.from_y = n.send(mine, mine, n.x_peer), n.send(mine, mine, n.y_peer)

    def cross(self):
        n = self.n
        self.from_y.wait_recv()
        block = self.full.at[:, 1 - n.y, n.x, n.c]
        self.diag = n.send(block, block, n.x_peer)

    def share(self):
        n = self.n
        self.from_x.wait_recv()
        self.diag.wait_recv()
        block = self.full.at[:, :, :, n.c]
        self.core = n.send(block, block, n.core_peer)

    def finish(self):
        self.core.wait_recv()


class Reduce:
    def __init__(self, links, box, grad, bufs):
        self.n, self.box, self.grad = links, box, grad
        self.from_core, self.held, self.diag0, self.diag1, self.from_x, self.from_y, self.from_z, self.total = bufs
        self.core, self.diag, self.sides, self.z_copies = {}, {}, {}, {}

    @staticmethod
    def buffers(box, z):
        h, w = box.half_rows, box.half_lanes
        color0 = (16, 128) if box.colors[0] is None else (box.colors[0][1], box.colors[0][3])
        color1 = (box.colors[1][1], box.colors[1][3])
        return [
            ((z, 2, h, box.lanes), BF16),
            ((z, 2, h, box.lanes), BF16),
            ((z,) + color0, BF16),
            ((z,) + color1, BF16),
            ((z, h, w), BF16),
            ((z, h, w), BF16),
            ((3, h, w), BF16),
            ((box.rows, box.lanes), BF16),
        ]

    def spot(self, o):
        return slice(None) if o is None else self.n.ahead(o)

    def start(self, o):
        n, box, p = self.n, self.box, self.spot(o)
        src = self.grad.at[p, :, box.rows_of(1 - n.c), :]
        self.core[o] = n.send(src, self.from_core.at[p], n.core_peer)

    def pair(self, o):
        n, box, p = self.n, self.box, self.spot(o)
        self.core[o].wait_recv()
        mine = self.grad[p, :, box.rows_of(n.c), :].astype(F32)
        self.held[p] = (mine + self.from_core[p].astype(F32)).astype(BF16)
        copies = []
        for color, (land, peer) in enumerate(((self.diag0, n.x_peer), (self.diag1, n.y_peer))):
            if box.colors[color] is not None:
                src = self.held.at[p, 1 - n.y, box.rows_of(0, color), box.lanes_of(1 - n.x, color)]
                copies.append(n.send(src, land.at[p], peer))
            else:
                copies.append(None)
        self.diag[o] = copies

    def side(self, o):
        n, box, p = self.n, self.box, self.spot(o)
        first, second = self.diag[o]
        if first is not None:
            first.wait_recv()
            at = (p, 1 - n.y, box.rows_of(0, 0), box.lanes_of(n.x, 0))
            self.held[at] = (self.held[at].astype(F32) + self.diag0[p].astype(F32)).astype(BF16)
        to_y = n.send(
            self.held.at[p, 1 - n.y, :, box.lanes_of(n.x)], self.from_y.at[p], n.y_peer
        )
        second.wait_recv()
        at = (p, n.y, box.rows_of(0, 1), box.lanes_of(1 - n.x, 1))
        self.held[at] = (self.held[at].astype(F32) + self.diag1[p].astype(F32)).astype(BF16)
        to_x = n.send(
            self.held.at[p, n.y, :, box.lanes_of(1 - n.x)], self.from_x.at[p], n.x_peer
        )
        self.sides[o] = (to_y, to_x)

    def column(self, o):
        n, box, p = self.n, self.box, self.spot(o)
        for copy in self.sides[o]:
            copy.wait_recv()
        at = (p, n.y, slice(None), box.lanes_of(n.x))
        summed = (
            self.held[at].astype(F32)
            + self.from_x[p].astype(F32)
            + self.from_y[p].astype(F32)
        )
        self.held[at] = summed.astype(BF16)
        for off in (1, 3, 2) if o is None else (o,):
            if off != 0:
                src = self.held.at[n.ahead(off), n.y, :, box.lanes_of(n.x)]
                self.z_copies[off] = n.send(
                    src, self.from_z.at[off - 1], n.device(z=n.ahead(off))
                )

    def owner(self):
        n, box = self.n, self.box
        for copy in self.z_copies.values():
            copy.wait_recv()
        summed = self.held[n.z, n.y, :, box.lanes_of(n.x)].astype(F32)
        for i in range(3):
            summed = summed + self.from_z[i].astype(F32)
        self.total[box.rows_of(n.c), box.lanes_of(n.x)] = summed.astype(BF16)
        mine = self.total.at[box.rows_of(n.c), box.lanes_of(n.x)]
        self.replicas = [
            n.send(mine, mine, n.core_peer),
            n.send(mine, mine, n.x_peer),
            n.send(mine, mine, n.device(x=1 - n.x, c=1 - n.c)),
        ]

    def finish(self, out):
        for copy in self.replicas:
            copy.wait_recv()
        out[...] = self.total[...].astype(F32)


class SmallSum:
    def __init__(self, links, block, land):
        self.n, self.block, self.land = links, block, land

    def exchange(self, first, peers, mate=0):
        self.mate = mate
        self.copies = [
            (self.n.send(self.block, self.land.at[first + i], peer), first + i)
            for i, peer in enumerate(peers)
        ]

    def add(self):
        for copy, _ in self.copies:
            copy.wait_recv()
        parts = [self.land[slot] for _, slot in self.copies]
        total = self.block[...] + parts[self.mate]
        if len(parts) == 3:
            others = [part for i, part in enumerate(parts) if i != self.mate]
            total = total + (others[0] + others[1])
        for copy, _ in self.copies:
            copy.wait_send()
            self.n.started = [c for c in self.n.started if c is not copy]
        self.block[...] = total


BOXES = {
    "first": Box(288, 256, by_rows=80),
    "embed": Box(64, 256, by_rows=16),
    "second": Box(288, 256, by_rows=80),
    "mixed": Box(32, 768, by_lanes=256),
    "out": Box(32, 256),
}
COPIES = 288


def whole_kernel(names, count, side, z_size, steps, *refs):
    k = Refs(names, refs, count, side)
    n = Links(k.send_sems, k.recv_sems, k.local_sems, z_size)
    arrived = n.greet()
    table_copy = n.local(k.time_table, k.table)
    start_compute(k)

    width = k.vectors.shape[1]
    lane = lax.broadcasted_iota(jnp.int32, (width, WIDTH), 1)
    row = lax.broadcasted_iota(jnp.int32, (width, WIDTH), 0)
    place = jnp.where(lane == row + n.f * width, 1.0, 0.0).astype(BF16)
    own_vec = dot(k.vectors[...], place).astype(BF16)
    k.vec_own[...] = jnp.concatenate([own_vec, jnp.zeros((4, WIDTH), BF16)], axis=0)

    arrived()
    gathers = {
        name: Gather(n, box, getattr(k, "shard_" + name), getattr(k, "full_" + name))
        for name, box in BOXES.items()
    }
    first = gathers["first"]
    first.start()
    vec_copies = [
        n.send(k.vec_own, k.vec_all.at[n.z, n.y], n.device(z=n.ahead(o), y=y))
        for o in range(z_size)
        for y in (n.y, 1 - n.y)
        if not (o == 0 and y is n.y)
    ]
    vec_own = n.local(k.vec_own, k.vec_all.at[n.z, n.y])
    first.spread(0)
    gathers["embed"].start()
    table_copy.wait()
    k.extra[...] = jnp.full(k.extra.shape, -1.0, F32)
    for m in range(count):
        k.extra[m : m + 1, 0:TEMB] = k.table[pl.ds(k.steps[m], 1), :]
        k.extra[m : m + 1, TEMB:EXTRA] = jnp.full((1, EXTRA - TEMB), k.steps[m].astype(F32), F32)
    for copy in vec_copies:
        copy.wait_recv()
    vec_own.wait()
    total = k.vec_all[0, 0].astype(F32)
    for i in range(1, 2 * z_size):
        total = total + k.vec_all[i // 2, i % 2].astype(F32)
    k.vec[...] = total

    first_norm(k, 0)
    first.spread(1)
    first.cross(0)
    first_norm(k, 1)
    first.spread(3)
    first.cross(1)
    first_norm(k, 2)
    first.spread(2)
    first_norm(k, 3)
    gathers["second"].start()
    first.cross(3)
    first.share(0)
    first.cross(2)
    first.share(1)
    gathers["embed"].spread(None)
    first.share(3)
    first.share(2)
    gathers["embed"].cross(None)
    gathers["mixed"].start()
    gathers["out"].start()
    gathers["second"].spread(None)
    gathers["embed"].share(None)
    first.finish()
    gathers["embed"].finish()
    k.w_first = k.full_first.reshape(TAPS, WIDTH)
    k.w_second = k.full_second.reshape(TAPS, WIDTH)
    k.w_embed = k.full_embed.reshape(TEMB, WIDTH)
    k.w_mixed = k.full_mixed.reshape(WIDTH, 3 * WIDTH)
    k.w_out = k.full_out.reshape(WIDTH, WIDTH)
    embed(k, k.extra[:, 0:TEMB])
    each_map(k, first_conv)
    gathers["second"].cross(None)
    gathers["mixed"].spread(None)
    gathers["out"].spread(None)
    extras = SmallGather(n, k.extra, k.extra_all)
    extras.start()
    each_map(k, second_norm)
    gathers["second"].share(None)
    gathers["mixed"].cross(None)
    gathers["out"].cross(None)
    gathers["second"].finish()
    each_map(k, second_conv)
    gathers["mixed"].share(None)
    gathers["out"].share(None)
    gathers["mixed"].finish()
    gathers["out"].finish()
    for m in range(count):
        attention(k, m)
        if m == 0:
            extras.spread()
        elif m == 1:
            extras.cross()
        elif m == 2:
            extras.share()
    extras.finish()

    reduces = {}
    for name in ("first", "second", "mixed", "out"):
        bufs = [getattr(k, f"reduce_{name}_{i}") for i in range(8)]
        reduces[name] = Reduce(n, BOXES[name], getattr(k, "grad_" + name), bufs)
    g_out = k.grad_out.reshape(WIDTH, WIDTH)
    g_mixed = k.grad_mixed.reshape(WIDTH, 3 * WIDTH)
    g_second = k.grad_second.reshape(TAPS, WIDTH)
    g_first = k.grad_first.reshape(TAPS, WIDTH)
    small = [reduces["out"], reduces["mixed"]]
    g_out[...] = dot(k.att_t[...], k.cot[...]).astype(BF16)
    reduces["out"].start(None)
    g_mixed[...] = dot(k.nrm_t[...], k.g_mixed[...]).astype(BF16)
    reduces["mixed"].start(None)
    each_map(k, third_norm_back)
    for r in small:
        r.pair(None)
    kernel_grad(k, k.a2_t, g_second)
    reduces["second"].start(None)
    for r in small:
        r.side(None)
    each_map(k, second_conv_back)
    reduces["second"].pair(None)
    for r in small:
        r.column(None)
    each_map(k, second_norm_back)
    reduces["second"].side(None)
    sends = SmallGather(n, k.g_proj, k.g_proj_all)
    sends.start()
    kernel_grad(k, k.a1_t, g_first)
    first = reduces["first"]
    order = (2, 1, 3, 0)
    for o in order:
        first.start(o)
    for r in small:
        r.owner()
    first_conv_back(k, 0)
    first_conv_back(k, 1)
    for o in order:
        first.pair(o)
    reduces["second"].column(None)
    first_conv_back(k, 2)
    first_conv_back(k, 3)
    sends.spread()
    each_map(k, first_norm_back)
    sums = SmallSum(n, k.sums, k.sums_land)
    sums.exchange(0, [n.core_peer])
    for o in order:
        first.side(o)
    sends.cross()
    sums.add()
    sums.exchange(1, [n.x_peer, n.y_peer, n.device(x=1 - n.x, y=1 - n.y)])
    reduces["second"].owner()
    for o in order:
        first.column(o)
    sends.share()
    sums.add()
    sums.exchange(4, [n.device(z=n.ahead(o)) for o in range(1, z_size)], mate=1)
    first.owner()
    sends.finish()

    devices = 4 * 2 * z_size
    g_proj = k.g_proj_all[...].reshape(devices * 8, WIDTH).astype(BF16)
    extra = k.extra_all[...].reshape(devices * 8, EXTRA)
    pre = extra[:, 0:TEMB]
    sig = jax.nn.sigmoid(pre)
    e = pre * sig
    g_embed = dot(e.astype(BF16).T, g_proj)
    k.g_embed_all[...] = g_embed
    rows = TEMB // (2 * z_size)
    k.embed_grad[...] = k.g_embed_all[pl.ds(pl.multiple_of(n.f * rows, rows), rows), :]
    g_pre = dot_nt(g_proj, k.w_embed[...]) * (sig + e * (1.0 - sig))
    when = extra[:, TEMB:EXTRA].T[0:1, :]
    t = lax.broadcasted_iota(jnp.int32, (steps, devices * 8), 0).astype(F32)
    selector = jnp.where(t == when, 1.0, 0.0).astype(BF16)
    high, mid, low = split3(g_pre)
    k.table_grad[...] = dot(selector, high) + dot(selector, mid) + dot(selector, low)
    sums.add()
    k.vec_grad[...] = k.sums[...]
    reduces["out"].finish(k.out_grad)
    reduces["mixed"].finish(k.mixed_grad)
    reduces["second"].finish(k.second_grad)
    first.finish(k.first_grad)
    n.finish()


def fused(image, timesteps, time_table, conv_first, embed_weight, conv_second, qkv_weight, out_weight, vectors, cotangent):
    count, side = image.shape[:2]
    total = count * side * side
    steps = time_table.shape[0]
    z_size = lax.axis_size("fsdp") // 2
    inputs = {
        "x": image.reshape(total, WIDTH),
        "cot": cotangent.reshape(total, WIDTH),
        "steps": timesteps,
        "time_table": time_table,
        "shard_first": conv_first,
        "shard_embed": embed_weight,
        "shard_second": conv_second,
        "shard_mixed": qkv_weight,
        "shard_out": out_weight,
        "vectors": vectors,
    }
    outputs = {
        "out": ((total, WIDTH), BF16),
        "image_grad": ((total, WIDTH), BF16),
        "table_grad": (time_table.shape, F32),
        "first_grad": (conv_first.shape, F32),
        "embed_grad": (embed_weight.shape, F32),
        "second_grad": (conv_second.shape, F32),
        "mixed_grad": (qkv_weight.shape, F32),
        "out_grad": (out_weight.shape, F32),
        "vec_grad": ((16, WIDTH), F32),
    }
    scratch = scratch_of(count, side)
    for name, box in BOXES.items():
        scratch["full_" + name] = ((z_size, 2, box.rows, box.lanes), BF16)
    for name in ("first", "second", "mixed", "out"):
        box = BOXES[name]
        scratch["grad_" + name] = ((z_size, 2, box.rows, box.lanes), BF16)
        for i, buf in enumerate(Reduce.buffers(box, z_size)):
            scratch[f"reduce_{name}_{i}"] = buf
    scratch["table"] = (time_table.shape, F32)
    scratch["extra"] = ((8, EXTRA), F32)
    scratch["extra_all"] = ((z_size, 2, 2, 2, 8, EXTRA), F32)
    scratch["g_proj_all"] = ((z_size, 2, 2, 2, 8, WIDTH), F32)
    scratch["g_embed_all"] = ((TEMB, WIDTH), F32)
    scratch["vec_own"] = ((16, WIDTH), BF16)
    scratch["vec_all"] = ((z_size, 2, 16, WIDTH), BF16)
    scratch["vec"] = ((16, WIDTH), F32)
    scratch["sums_land"] = ((7, 16, WIDTH), F32)
    sems = {"send_sems": COPIES, "recv_sems": COPIES, "local_sems": 16}
    names = list(inputs) + list(outputs) + list(scratch) + list(sems)
    vmem = pl.BlockSpec(memory_space=pltpu.VMEM)
    places = {
        "steps": pl.BlockSpec(memory_space=pltpu.SMEM),
        "time_table": pl.BlockSpec(memory_space=pl.ANY),
    }
    results = pl.pallas_call(
        functools.partial(whole_kernel, names, count, side, z_size, steps),
        out_shape=[jax.ShapeDtypeStruct(*v) for v in outputs.values()],
        in_specs=[places.get(name, vmem) for name in inputs],
        out_specs=[vmem] * len(outputs),
        scratch_shapes=[pltpu.VMEM(*v) for v in scratch.values()]
        + [pltpu.SemaphoreType.DMA((size,)) for size in sems.values()],
        compiler_params=pltpu.CompilerParams(
            collective_id=0, has_side_effects=True, vmem_limit_bytes=VMEM_BYTES
        ),
        name="block",
    )(*inputs.values())
    out, image_grad, table_grad, g_first, g_embed, g_second, g_mixed, g_out, g_vec = results
    wide = vectors.shape[1]
    g_vec = lax.dynamic_slice(
        g_vec, (0, lax.axis_index("fsdp") * wide), vectors.shape
    )
    return (
        out.reshape(image.shape),
        image_grad.reshape(image.shape),
        table_grad,
        g_first,
        g_embed,
        g_second,
        g_mixed,
        g_out,
        g_vec,
    )


def local_kernel(names, count, side, *refs):
    k = Refs(names, refs, count, side)
    start_compute(k)
    embed(k, k.pre[...])
    each_map(k, first_norm, first_conv, second_norm, second_conv, attention)
    k.grad_out[...] = dot(k.att_t[...], k.cot[...]).astype(BF16)
    k.grad_mixed[...] = dot(k.nrm_t[...], k.g_mixed[...]).astype(BF16)
    each_map(k, third_norm_back)
    kernel_grad(k, k.a2_t, k.grad_second)
    each_map(k, second_conv_back, second_norm_back)
    kernel_grad(k, k.a1_t, k.grad_first)
    each_map(k, first_conv_back, first_norm_back)
    k.vec_grad[...] = k.sums[...]
    k.g_proj_out[...] = k.g_proj[...]


def plain(image, timesteps, time_table, conv_first, embed_weight, conv_second, qkv_weight, out_weight, vectors, cotangent):
    count, side = image.shape[:2]
    total = count * side * side

    def whole(w, axis=0):
        return lax.all_gather(w, "fsdp", axis=axis, tiled=True)

    pre = time_table[timesteps]
    w_embed = whole(embed_weight)
    inputs = {
        "x": image.reshape(total, WIDTH),
        "cot": cotangent.reshape(total, WIDTH),
        "w_first": whole(conv_first),
        "w_embed": w_embed,
        "w_second": whole(conv_second),
        "w_mixed": whole(qkv_weight),
        "w_out": whole(out_weight),
        "vec": jnp.pad(whole(vectors, 1).astype(F32), ((0, 4), (0, 0))),
        "pre": jnp.pad(pre, ((0, 8 - count), (0, 0))),
    }
    outputs = {
        "out": ((total, WIDTH), BF16),
        "image_grad": ((total, WIDTH), BF16),
        "grad_first": ((TAPS, WIDTH), BF16),
        "grad_second": ((TAPS, WIDTH), BF16),
        "grad_mixed": ((WIDTH, 3 * WIDTH), BF16),
        "grad_out": ((WIDTH, WIDTH), BF16),
        "vec_grad": ((16, WIDTH), F32),
        "g_proj_out": ((8, WIDTH), F32),
    }
    scratch = scratch_of(count, side)
    names = list(inputs) + list(outputs) + list(scratch)
    vmem = pl.BlockSpec(memory_space=pltpu.VMEM)
    results = pl.pallas_call(
        functools.partial(local_kernel, names, count, side),
        out_shape=[jax.ShapeDtypeStruct(*v) for v in outputs.values()],
        in_specs=[vmem] * len(inputs),
        out_specs=[vmem] * len(outputs),
        scratch_shapes=[pltpu.VMEM(*v) for v in scratch.values()],
        compiler_params=pltpu.CompilerParams(vmem_limit_bytes=VMEM_BYTES),
        name="block_alone",
    )(*inputs.values())
    out, image_grad, g_first, g_second, g_mixed, g_out, g_vec, g_proj = results
    g_proj = g_proj[:count].astype(BF16)

    def owned(g, axis=0):
        own = lax.psum_scatter(g.astype(BF16), "fsdp", scatter_dimension=axis, tiled=True)
        return lax.psum(own, "dp").astype(F32)

    e = (pre * jax.nn.sigmoid(pre)).astype(BF16)
    g_embed = lax.dot_general(e, g_proj, TN, preferred_element_type=F32)
    sig = jax.nn.sigmoid(pre)
    g_pre = dot_nt(g_proj, w_embed) * (sig * (1.0 + pre * (1.0 - sig)))
    rows = lax.all_gather(g_pre, ("fsdp", "dp"), axis=0, tiled=True)
    where = lax.all_gather(timesteps, ("fsdp", "dp"), axis=0, tiled=True)
    table_grad = jnp.zeros(time_table.shape, F32).at[where].add(rows)
    return (
        out.reshape(image.shape),
        image_grad.reshape(image.shape),
        table_grad,
        owned(g_first),
        owned(g_embed),
        owned(g_second),
        owned(g_mixed),
        owned(g_out),
        owned(g_vec[: vectors.shape[0]], 1),
    )


def solution(mesh):
    placed = (
        P(("fsdp", "dp"), None, None, None),
        P(("fsdp", "dp")),
        P(),
        P("fsdp", None),
        P("fsdp", None),
        P("fsdp", None),
        P("fsdp", None),
        P("fsdp", None),
        P(None, "fsdp"),
        P(("fsdp", "dp"), None, None, None),
    )
    grid = (mesh.shape["fsdp"], mesh.shape["dp"])
    return jax.shard_map(
        fused if grid == (8, 4) else plain,
        mesh=mesh,
        in_specs=placed,
        out_specs=(
            P(("fsdp", "dp"), None, None, None),
            P(("fsdp", "dp"), None, None, None),
            P(),
            P("fsdp", None),
            P("fsdp", None),
            P("fsdp", None),
            P("fsdp", None),
            P("fsdp", None),
            P(None, "fsdp"),
        ),
        check_vma=False,
    )
```

```python
import functools
from types import SimpleNamespace

import jax
import jax.numpy as jnp
from jax import lax
from jax.experimental import pallas as pl
from jax.experimental.pallas import tpu as pltpu
from jax.sharding import PartitionSpec as P

FSDP, DP = "fsdp", "dp"
F32 = jnp.float32
BF16 = jnp.bfloat16
MESH = pl.DeviceIdType.MESH
EPS = 1e-06
WIDTH = 256
GROUP = 8
TEMB = 512
TAPS = 9 * WIDTH
HALF = TEMB // 2
EXTRA = HALF + 128
VMEM_BYTES = 56 * 2**20
NT = (((1,), (1,)), ((), ()))
TN = (((0,), (0,)), ((), ()))


def dot(a, b):
    return jnp.dot(a, b, preferred_element_type=F32)


def dot_nt(a, b):
    return lax.dot_general(a, b, NT, preferred_element_type=F32)


def split3(v):
    high = v.astype(BF16)
    rest = v - high.astype(F32)
    mid = rest.astype(BF16)
    return high, mid, (rest - mid.astype(F32)).astype(BF16)


def colsum(v):
    return jnp.sum(v, axis=0, keepdims=True)


def group_mean(row, averager):
    high, mid, low = split3(row)
    return dot(high, averager) + dot(mid, averager) + dot(low, averager)


class Refs:
    def __init__(self, names, refs, count, side):
        for name, ref in zip(names, refs):
            setattr(self, name, ref)
        self.count, self.side, self.places = count, side, side * side

    def rows(self, m):
        return pl.ds(m * self.places, self.places)


def scratch_of(count, side):
    places = side * side
    total = count * places
    padded = places + 2 * side
    return dict(
        averager=((WIDTH, WIDTH), BF16),
        shifted_a=((count, padded, 3 * WIDTH), BF16),
        shifted_g=((count, padded, 3 * WIDTH), BF16),
        unit1=((total, WIDTH), F32),
        slope1=((total, WIDTH), F32),
        inv1=((count, 1, WIDTH), F32),
        unit2=((total, WIDTH), F32),
        slope2=((total, WIDTH), F32),
        inv2=((count, 1, WIDTH), F32),
        unit3=((total, WIDTH), F32),
        inv3=((count, 1, WIDTH), F32),
        a1_t=((WIDTH, total), BF16),
        a2_t=((WIDTH, total), BF16),
        nrm_t=((WIDTH, total), BF16),
        att_t=((WIDTH, total), BF16),
        nrm=((total, WIDTH), BF16),
        mixed=((total, 3 * WIDTH), BF16),
        g_att=((total, WIDTH), BF16),
        probs=((total, places), F32),
        probs_low=((total, places), BF16),
        probs_t=((places, total), BF16),
        att=((total, WIDTH), BF16),
        g_probs=((total, places), F32),
        g_scores=((total, places), BF16),
        g_scores_t=((places, total), BF16),
        conv_out=((total, WIDTH), F32),
        resid=((total, WIDTH), F32),
        g_mixed=((total, 3 * WIDTH), BF16),
        proj=((8, WIDTH), F32),
        sums=((16, WIDTH), F32),
        g_proj=((8, WIDTH), F32),
    )


def start_compute(k):
    rows = lax.broadcasted_iota(jnp.int32, (WIDTH, WIDTH), 0) // GROUP
    cols = lax.broadcasted_iota(jnp.int32, (WIDTH, WIDTH), 1) // GROUP
    k.averager[...] = jnp.where(rows == cols, 1.0 / (k.places * GROUP), 0.0).astype(BF16)
    edge = jnp.zeros((k.count, k.side, 3 * WIDTH), BF16)
    for ref in (k.shifted_a, k.shifted_g):
        ref[:, 0 : k.side, :] = edge
        ref[:, k.places + k.side : k.places + 2 * k.side, :] = edge
    k.sums[...] = jnp.zeros(k.sums.shape, F32)
    k.g_proj[...] = jnp.zeros(k.g_proj.shape, F32)


def store_shifted(k, ref, m, a):
    column = lax.broadcasted_iota(jnp.int32, a.shape, 0) % k.side
    inner = slice(k.side, k.side + k.places)
    left = jnp.where(column == 0, 0.0, pltpu.roll(a, 1, 0))
    right = jnp.where(column == k.side - 1, 0.0, pltpu.roll(a, k.places - 1, 0))
    ref[m, inner, 0:WIDTH] = left.astype(BF16)
    ref[m, inner, WIDTH : 2 * WIDTH] = a.astype(BF16)
    ref[m, inner, 2 * WIDTH : 3 * WIDTH] = right.astype(BF16)


def normalize(k, u):
    averager = k.averager[...]
    centered = u - group_mean(colsum(u), averager)
    inverse = lax.rsqrt(group_mean(colsum(centered * centered), averager) + EPS)
    return centered * inverse, inverse


def norm_swish(k, u, m, j, unit_ref, slope_ref, inv_ref):
    unit, inverse = normalize(k, u)
    unit_ref[k.rows(m), :] = unit
    inv_ref[m] = inverse
    h = unit * (1.0 + k.vec[j : j + 1, :]) + k.vec[j + 1 : j + 2, :]
    sig = jax.nn.sigmoid(h)
    a = h * sig
    slope_ref[k.rows(m), :] = sig + a * (1.0 - sig)
    return a


def norm_back(k, upstream, unit, inverse, j):
    averager = k.averager[...]
    g_gain = colsum(upstream * unit)
    g_shift = colsum(upstream)
    k.sums[j : j + 1, :] += g_gain
    k.sums[j + 1 : j + 2, :] += g_shift
    gain = 1.0 + k.vec[j : j + 1, :]
    first = group_mean(g_shift * gain, averager)
    second = group_mean(g_gain * gain, averager)
    return inverse * (upstream * gain - first - unit * second)


def convolve(k, ref, w, m):
    total = None
    for ky in range(3):
        window = ref[m, ky * k.side : ky * k.side + k.places, :]
        term = dot(window, w[ky * 3 * WIDTH : (ky + 1) * 3 * WIDTH, :])
        total = term if total is None else total + term
    return total


def convolve_back(k, ref, w, m):
    total = None
    for ky in range(3):
        for kx in range(3):
            window = ref[
                m,
                (2 - ky) * k.side : (2 - ky) * k.side + k.places,
                (2 - kx) * WIDTH : (3 - kx) * WIDTH,
            ]
            tap = 3 * ky + kx
            term = dot_nt(window, w[tap * WIDTH : (tap + 1) * WIDTH, :])
            total = term if total is None else total + term
    return total


def kernel_grad(k, a_t, g_w):
    for ky in range(3):
        window = k.shifted_g[:, (2 - ky) * k.side : (2 - ky) * k.side + k.places, :]
        term = dot(a_t[...], window.reshape(k.count * k.places, 3 * WIDTH))
        for kx in range(3):
            tap = 3 * ky + kx
            g_w[tap * WIDTH : (tap + 1) * WIDTH, :] = term[
                :, (2 - kx) * WIDTH : (3 - kx) * WIDTH
            ].astype(BF16)


def first_norm(k, m):
    a = norm_swish(k, k.x[k.rows(m), :].astype(F32), m, 0, k.unit1, k.slope1, k.inv1)
    store_shifted(k, k.shifted_a, m, a)
    k.a1_t[:, k.rows(m)] = a.astype(BF16).T


def embed(k, pre):
    e = (pre * jax.nn.sigmoid(pre)).astype(BF16)
    k.proj[...] = dot(e, k.w_embed[...]) + k.vec[3:4, :]


def first_conv(k, m):
    k.conv_out[k.rows(m), :] = convolve(k, k.shifted_a, k.w_first, m)


def second_norm(k, m):
    h1 = k.conv_out[k.rows(m), :] + (k.vec[2:3, :] + k.proj[m : m + 1, :])
    a = norm_swish(k, h1, m, 4, k.unit2, k.slope2, k.inv2)
    store_shifted(k, k.shifted_a, m, a)
    k.a2_t[:, k.rows(m)] = a.astype(BF16).T


def second_conv(k, m):
    x = k.x[k.rows(m), :].astype(F32)
    k.resid[k.rows(m), :] = x + convolve(k, k.shifted_a, k.w_second, m) + k.vec[6:7, :]


def third_norm(k, m):
    rows = k.rows(m)
    unit, inverse = normalize(k, k.resid[rows, :])
    k.unit3[rows, :] = unit
    k.inv3[m] = inverse
    nrm = (unit * (1.0 + k.vec[7:8, :]) + k.vec[8:9, :]).astype(BF16)
    k.nrm[rows, :] = nrm
    k.nrm_t[:, rows] = nrm.T


def project(k, m):
    rows = k.rows(m)
    mixed = dot(k.nrm[rows, :], k.w_mixed[...])
    k.mixed[rows, 0:WIDTH] = (mixed[:, :WIDTH] + k.vec[9:10, :]).astype(BF16)
    k.mixed[rows, WIDTH : 2 * WIDTH] = mixed[:, WIDTH : 2 * WIDTH].astype(BF16)
    k.mixed[rows, 2 * WIDTH :] = (mixed[:, 2 * WIDTH :] + k.vec[10:11, :]).astype(BF16)


def upstream(k, m):
    cot = k.cot[k.rows(m), :]
    k.sums[11:12, :] += colsum(cot.astype(F32))
    k.g_att[k.rows(m), :] = dot_nt(cot, k.w_out[...]).astype(BF16)


def softmax(k, m):
    rows = k.rows(m)
    scores = dot_nt(k.mixed[rows, 0:WIDTH], k.mixed[rows, WIDTH : 2 * WIDTH]) * WIDTH**-0.5
    raised = jnp.exp(scores - jnp.max(scores, axis=1, keepdims=True))
    probs = raised * (1.0 / jnp.sum(raised, axis=1, keepdims=True))
    k.probs[rows, :] = probs
    low = probs.astype(BF16)
    k.probs_low[rows, :] = low
    k.probs_t[:, rows] = low.T


def attend(k, m):
    rows = k.rows(m)
    value = k.mixed[rows, 2 * WIDTH :]
    att = dot(k.probs_low[rows, :], value).astype(BF16)
    k.att[rows, :] = att
    k.att_t[:, rows] = att.T
    k.g_probs[rows, :] = dot_nt(k.g_att[rows, :], value)


def emit(k, m):
    rows = k.rows(m)
    branch = dot(k.att[rows, :], k.w_out[...])
    k.out[rows, :] = (k.resid[rows, :] + branch + k.vec[11:12, :]).astype(BF16)


def softmax_back(k, m):
    rows = k.rows(m)
    probs, g_probs = k.probs[rows, :], k.g_probs[rows, :]
    weighted = jnp.sum(probs * g_probs, axis=1, keepdims=True)
    g_scores = (probs * (g_probs - weighted)).astype(BF16)
    k.g_scores[rows, :] = g_scores
    k.g_scores_t[:, rows] = g_scores.T
    g_value = dot(k.probs_t[:, rows], k.g_att[rows, :]).astype(BF16)
    k.sums[10:11, :] += colsum(g_value.astype(F32))
    k.g_mixed[rows, 2 * WIDTH :] = g_value


def project_back(k, m):
    rows = k.rows(m)
    scale = WIDTH**-0.5
    g_query = (dot(k.g_scores[rows, :], k.mixed[rows, WIDTH : 2 * WIDTH]) * scale).astype(BF16)
    g_key = (dot(k.g_scores_t[:, rows], k.mixed[rows, 0:WIDTH]) * scale).astype(BF16)
    k.sums[9:10, :] += colsum(g_query.astype(F32))
    k.g_mixed[rows, 0:WIDTH] = g_query
    k.g_mixed[rows, WIDTH : 2 * WIDTH] = g_key


ATTENTION = (third_norm, project, upstream, softmax, attend, emit, softmax_back, project_back)


def third_norm_back(k, m):
    rows = k.rows(m)
    g_nrm = dot_nt(k.g_mixed[rows, :], k.w_mixed[...])
    g_resid = k.cot[rows, :].astype(F32) + norm_back(
        k, g_nrm, k.unit3[rows, :], k.inv3[m], 7
    )
    k.resid[rows, :] = g_resid
    g_conv = g_resid.astype(BF16).astype(F32)
    k.sums[6:7, :] += colsum(g_conv)
    store_shifted(k, k.shifted_g, m, g_conv)


def second_conv_back(k, m):
    rows = k.rows(m)
    k.conv_out[rows, :] = convolve_back(k, k.shifted_g, k.w_second, m) * k.slope2[rows, :]


def second_norm_back(k, m):
    rows = k.rows(m)
    g_h1 = norm_back(k, k.conv_out[rows, :], k.unit2[rows, :], k.inv2[m], 4)
    g_h1 = g_h1.astype(BF16).astype(F32)
    per_map = colsum(g_h1)
    k.sums[2:3, :] += per_map
    g_proj = per_map.astype(BF16).astype(F32)
    k.sums[3:4, :] += g_proj
    k.g_proj[m : m + 1, :] = g_proj
    k.g_proj[m + 4 : m + 5, :] = g_proj
    store_shifted(k, k.shifted_g, m, g_h1)


def first_conv_back(k, m):
    rows = k.rows(m)
    k.conv_out[rows, :] = convolve_back(k, k.shifted_g, k.w_first, m) * k.slope1[rows, :]


def first_norm_back(k, m):
    rows = k.rows(m)
    g_x = norm_back(k, k.conv_out[rows, :], k.unit1[rows, :], k.inv1[m], 0)
    k.image_grad[rows, :] = (k.resid[rows, :] + g_x).astype(BF16)


def each_map(k, *steps):
    for step in steps:
        for m in range(k.count):
            step(k, m)


class Links:
    def __init__(self, send_sems, recv_sems, local_sems, z_size):
        f, d = lax.axis_index(FSDP), lax.axis_index(DP)
        self.f, self.z_size = f, z_size
        self.z, self.y = f // 2, f % 2
        self.x, self.c = d // 2, d % 2
        self.send_sems, self.recv_sems, self.local_sems = send_sems, recv_sems, local_sems
        self.started, self.n_sent, self.n_local = [], 0, 0
        self.n_received, self.left = 0, set()

    def device(self, z=None, y=None, x=None, c=None):
        z = self.z if z is None else z
        y = self.y if y is None else y
        x = self.x if x is None else x
        c = self.c if c is None else c
        return (z * 2 + y, x * 2 + c)

    def partner(self, k):
        return (self.z, self.z + 1 - 2 * (self.z % 2), (self.z + 2) % 4, 3 - self.z)[k]

    @property
    def x_peer(self):
        return self.device(x=1 - self.x)

    @property
    def y_peer(self):
        return self.device(y=1 - self.y)

    @property
    def core_peer(self):
        return self.device(c=1 - self.c)

    def send(self, src, dst, device, landing=None):
        if self.n_sent >= SENDS:
            self.sent(self.started[self.n_sent - SENDS])
        if landing is None:
            landing = self.landing()
        copy = pltpu.make_async_remote_copy(
            src_ref=src,
            dst_ref=dst,
            send_sem=self.send_sems.at[self.n_sent % SENDS],
            recv_sem=self.recv_sems.at[landing],
            device_id=device,
            device_id_type=MESH,
        )
        copy.start()
        self.n_sent += 1
        self.started.append(copy)
        return copy

    def landing(self):
        self.n_received += 1
        return self.n_received - 1

    def send_all(self, triples, room):
        landing = self.landing()
        for src, dst, device in triples:
            self.send(src, dst, device, landing)
        return pltpu.make_async_copy(room, room, self.recv_sems.at[landing])

    def sent(self, copy):
        spot = [c is copy for c in self.started].index(True)
        if spot not in self.left:
            copy.wait_send()
            self.left.add(spot)

    def local(self, src, dst):
        copy = pltpu.make_async_copy(src, dst, self.local_sems.at[self.n_local])
        self.n_local += 1
        copy.start()
        return copy

    def finish(self):
        for copy in self.started:
            self.sent(copy)

    def greet(self):
        barrier = pltpu.get_barrier_semaphore()
        peers = [
            self.device(z=self.partner(o), y=y)
            for o in range(4)
            for y in (self.y, 1 - self.y)
            if not (o == 0 and y is self.y)
        ]
        peers += [self.x_peer, self.core_peer, self.device(x=1 - self.x, c=1 - self.c)]
        peers += [self.device(x=1 - self.x, y=1 - self.y)]
        for peer in peers:
            pl.semaphore_signal(barrier, inc=1, device_id=peer, device_id_type=MESH)
        return lambda: pl.semaphore_wait(barrier, len(peers))


class Box:
    def __init__(self, rows, lanes):
        self.rows, self.lanes = rows, lanes
        self.half_rows, self.half_lanes = rows // 2, lanes // 2

    def rows_of(self, c):
        return pl.ds(pl.multiple_of(c * self.half_rows, 16), self.half_rows)

    def lanes_of(self, x):
        return pl.ds(pl.multiple_of(x * self.half_lanes, 128), self.half_lanes)


class Gather:
    def __init__(self, links, box, shard, full, parts=False):
        self.n, self.box, self.shard, self.full = links, box, shard, full
        self.by_parts = parts
        self.sides, self.core = {}, []

    def start(self):
        n, box = self.n, self.box
        src = self.shard.at[box.rows_of(n.c), box.lanes_of(n.x)]
        dst = self.full.at[n.z, n.y, box.rows_of(n.c), box.lanes_of(n.x)]
        routes = [(src, dst, n.device(z=n.partner(o))) for o in (1, 2, 3)]
        if self.by_parts:
            self.z_copies = {o: n.send(*route) for o, route in zip((1, 2, 3), routes)}
        else:
            self.z_copies = n.send_all(routes, self.room(1))
            self.own = n.local(src, dst)

    def room(self, o):
        rows, w = self.box.rows if o is None else self.box.half_rows, self.box.half_lanes
        return self.full.at[0:3, 0 : 2 if o is None else 1, 0:rows, 0:w]

    def start_own(self):
        n, box = self.n, self.box
        src = self.shard.at[box.rows_of(n.c), :]
        self.own_y = n.send(src, self.full.at[n.z, n.y, box.rows_of(n.c), :], n.y_peer)
        self.own = n.local(self.shard, self.full.at[n.z, n.y])

    def part(self, o, y, x):
        n, box = self.n, self.box
        p = slice(None) if o is None else n.partner(o)
        return self.full.at[p, y, box.rows_of(n.c), box.lanes_of(x)]

    def spread(self, *parts):
        n = self.n
        for o in parts or (None,):
            if o is None:
                self.z_copies.wait()
                self.own.wait()
            else:
                self.z_copies[o].wait_recv()
            mine = self.part(o, n.y, n.x)
            peers = (n.x_peer, n.y_peer, n.device(x=1 - n.x, y=1 - n.y))
            room = self.room(o)
            self.sides[o] = n.send_all([(mine, mine, peer) for peer in peers], room)

    def share_own(self):
        n, box = self.n, self.box
        self.own_y.wait_recv()
        block = self.full.at[n.z, 1 - n.y, box.rows_of(n.c), :]
        self.core.append(n.send(block, block, n.core_peer))

    def share(self, o=None):
        n, box = self.n, self.box
        self.sides[o].wait()
        p = slice(None) if o is None else n.partner(o)
        block = self.full.at[p, :, box.rows_of(n.c), :]
        self.core.append(n.send(block, block, n.core_peer))

    def finish(self):
        for copy in self.core:
            copy.wait_recv()
        if self.by_parts:
            self.own.wait()


class SmallGather:
    def __init__(self, links, block, full):
        self.n, self.block, self.full = links, block, full

    def start(self):
        n = self.n
        dst = self.full.at[n.z, n.y, n.x, n.c]
        routes = [(self.block, dst, n.device(z=n.partner(o))) for o in (1, 2, 3)]
        self.z_copies = n.send_all(routes, self.full.at[0:3, 0, 0, 0])
        self.own = n.local(self.block, dst)

    def spread(self):
        n = self.n
        self.z_copies.wait()
        self.own.wait()
        mine = self.full.at[:, n.y, n.x, n.c]
        peers = (n.x_peer, n.y_peer, n.device(x=1 - n.x, y=1 - n.y))
        self.sides = n.send_all([(mine, mine, peer) for peer in peers], self.full.at[0:3, :, :, 0])

    def share(self):
        n = self.n
        self.sides.wait()
        block = self.full.at[:, :, :, n.c]
        self.core = n.send(block, block, n.core_peer)

    def finish(self):
        self.core.wait_recv()


class Reduce:
    def __init__(self, links, box, early, grad, bufs):
        self.n, self.box, self.early, self.grad = links, box, early, grad
        self.from_core, self.held, self.z_early, self.sides_early, self.sides_late, self.z_late, self.total = bufs
        self.core, self.sides = {}, {}
        self.early_landing = self.late_landing = None

    @staticmethod
    def buffers(box, early, z):
        w, late = box.half_lanes, max(box.half_rows - early, 16)
        return [
            ((z, 2, box.half_rows, box.lanes), BF16),
            ((z, 2, box.half_rows, box.lanes), BF16),
            ((3, 2, max(early, 16), box.lanes), BF16),
            ((3, max(early, 16), w), BF16),
            ((3, z, late, w), BF16),
            ((3, late, w), BF16),
            ((box.rows, box.lanes), BF16),
        ]

    def spot(self, o):
        return slice(None) if o is None else self.n.partner(o)

    def rows(self, late):
        return slice(self.early, self.box.half_rows) if late else slice(0, self.early)

    def around(self):
        n = self.n
        return (
            (1 - n.y, 1 - n.x, n.device(x=1 - n.x, y=1 - n.y)),
            (1 - n.y, n.x, n.y_peer),
            (n.y, 1 - n.x, n.x_peer),
        )

    def start(self, o=None):
        n, box, p = self.n, self.box, self.spot(o)
        src = self.grad.at[p, :, box.rows_of(1 - n.c), :]
        self.core[o] = n.send(src, self.from_core.at[p], n.core_peer)

    def pair(self, o=None):
        n, box, p = self.n, self.box, self.spot(o)
        self.core[o].wait_recv()
        mine = self.grad[p, :, box.rows_of(n.c), :].astype(F32)
        self.held[p] = (mine + self.from_core[p].astype(F32)).astype(BF16)
        if self.early and self.early_landing is None:
            self.early_landing = n.landing()
        for k in (3, 2, 1) if o is None else (o,):
            if k != 0 and self.early:
                z = n.partner(k)
                src = self.held.at[z, :, self.rows(False), :]
                n.send(src, self.z_early.at[k - 1], n.device(z=z), self.early_landing)
        if self.early < box.half_rows:
            routes = [
                (
                    self.held.at[p, y, self.rows(True), box.lanes_of(x)],
                    self.sides_late.at[i, p],
                    peer,
                )
                for i, (y, x, peer) in enumerate(self.around())
            ]
            self.sides[o] = n.send_all(routes, self.sides_late.at[:, slice(None) if o is None else 0])

    def wait(self, landing, room):
        pltpu.make_async_copy(room, room, self.n.recv_sems.at[landing]).wait()

    def middle_early(self):
        n, box = self.n, self.box
        self.wait(self.early_landing, self.z_early)
        at = (n.z, slice(None), self.rows(False), slice(None))
        summed = self.held[at].astype(F32)
        for i in range(3):
            summed = summed + self.z_early[i].astype(F32)
        self.held[at] = summed.astype(BF16)
        routes = [
            (self.held.at[n.z, y, self.rows(False), box.lanes_of(x)], self.sides_early.at[i], peer)
            for i, (y, x, peer) in enumerate(self.around())
        ]
        self.early_sides = n.send_all(routes, self.sides_early)

    def middle_late(self, o=None):
        n, box, p = self.n, self.box, self.spot(o)
        self.sides[o].wait()
        at = (p, n.y, self.rows(True), box.lanes_of(n.x))
        summed = self.held[at].astype(F32)
        for i in range(3):
            summed = summed + self.sides_late[i, p].astype(F32)
        self.held[at] = summed.astype(BF16)
        if self.late_landing is None:
            self.late_landing = n.landing()
        for k in (3, 2, 1) if o is None else (o,):
            if k != 0:
                z = n.partner(k)
                src = self.held.at[z, n.y, self.rows(True), box.lanes_of(n.x)]
                n.send(src, self.z_late.at[k - 1], n.device(z=z), self.late_landing)

    def owner(self):
        n, box = self.n, self.box
        if self.early:
            self.early_sides.wait()
        if self.early < box.half_rows:
            self.wait(self.late_landing, self.z_late)
        for late, lands in ((False, self.sides_early), (True, self.z_late)):
            rows = self.rows(late)
            size = rows.stop - rows.start
            if size:
                summed = self.held[n.z, n.y, rows, box.lanes_of(n.x)].astype(F32)
                for i in range(3):
                    summed = summed + lands[i].astype(F32)
                first = pl.multiple_of(n.c * box.half_rows + rows.start, 16)
                self.total[pl.ds(first, size), box.lanes_of(n.x)] = summed.astype(BF16)
        mine = self.total.at[box.rows_of(n.c), box.lanes_of(n.x)]
        peers = (n.x_peer, n.device(x=1 - n.x, c=1 - n.c), n.core_peer)
        self.replicas = n.send_all(
            [(mine, mine, peer) for peer in peers],
            self.from_core.at[0:3, 0, :, 0 : box.half_lanes],
        )

    def finish(self, out):
        self.replicas.wait()
        return self.n.local(self.total, out)


class SmallSum:
    def __init__(self, links, block, land):
        self.n, self.block, self.land = links, block, land

    def exchange(self, first, peers):
        self.slots = range(first, first + len(peers))
        routes = [(self.block, self.land.at[i], peer) for i, peer in zip(self.slots, peers)]
        self.arrivals = self.n.send_all(routes, self.land.at[first : first + len(peers)])
        self.copies = self.n.started[-len(peers) :]

    def add(self):
        self.arrivals.wait()
        parts = [self.land[slot] for slot in self.slots]
        total = self.block[...] + parts[0]
        if len(parts) == 3:
            total = total + (parts[1] + parts[2])
        for copy in self.copies:
            self.n.sent(copy)
        self.block[...] = total


BOXES = dict(
    first=Box(288, 256),
    embed=Box(64, 256),
    second=Box(288, 256),
    mixed=Box(32, 768),
    out=Box(32, 256),
)
EARLY = dict(first=0, second=32, mixed=0, out=0)
SENDS = 32
LANDINGS = 65


def whole_kernel(names, count, side, z_size, *refs):
    k = Refs(names, refs, count, side)
    n = Links(k.send_sems, k.recv_sems, k.local_sems, z_size)
    arrived = n.greet()
    vectors_copy = n.local(k.vectors_in, k.vectors)
    steps_copy = n.local(k.steps_in, k.steps)
    x_copy = n.local(k.x_in, k.x)
    table_copy = n.local(k.time_table, k.table)
    cot_copy = n.local(k.cot_in, k.cot)

    arrived()
    gathers = SimpleNamespace(**{
        name: Gather(
            n,
            box,
            getattr(k, "shard_" + name),
            getattr(k, "full_" + name),
            parts=name in ("first", "second"),
        )
        for name, box in BOXES.items()
    })
    first, second = gathers.first, gathers.second
    first.start()
    first.start_own()
    vectors_copy.wait()
    width = k.vectors.shape[1]
    lane = lax.broadcasted_iota(jnp.int32, (width, 128), 1)
    row = lax.broadcasted_iota(jnp.int32, (width, 128), 0)
    place = jnp.where(lane == row + lax.rem(n.f * width, 128), 1.0, 0.0).astype(BF16)
    own_vec = dot(k.vectors[...], place).astype(BF16)
    k.vec_own[...] = jnp.concatenate([own_vec, jnp.zeros((4, 128), BF16)], axis=0)

    gathers.embed.start()
    to_all = [
        (k.vec_own, k.vec_all.at[n.z, n.y], n.device(z=n.partner(o), y=y))
        for o in range(4)
        for y in (n.y, 1 - n.y)
        if not (o == 0 and y is n.y)
    ]
    vec_copies = n.send_all(to_all, k.vec_room)
    second.start_own()
    vec_own = n.local(k.vec_own, k.vec_all.at[n.z, n.y])
    start_compute(k)
    steps_copy.wait()
    table_copy.wait()
    for m in range(count):
        row = k.table[pl.ds(k.steps[m], 1), :]
        k.pre[m : m + 1, :] = row
        k.extra[m : m + 1, 0:HALF] = row[:, 0:HALF]
        k.extra[m + 4 : m + 5, 0:HALF] = row[:, HALF:TEMB]
        when = jnp.full((1, EXTRA - HALF), k.steps[m].astype(F32), F32)
        k.extra[m : m + 1, HALF:EXTRA] = when
        k.extra[m + 4 : m + 5, HALF:EXTRA] = when
    extras = SmallGather(n, k.extra, k.extra_all)
    first.spread(1)
    second.start()
    for o in (2, 3):
        first.spread(o)
    vec_own.wait()
    x_copy.wait()
    vec_copies.wait()
    per_half = 2 * z_size // 2
    for half in range(2):
        total = k.vec_all[half * per_half // 2, 0].astype(F32)
        for i in range(half * per_half + 1, (half + 1) * per_half):
            total = total + k.vec_all[i // 2, i % 2].astype(F32)
        k.vec[:, half * 128 : (half + 1) * 128] = total
    gathers.embed.spread()
    gathers.mixed.start()
    gathers.out.start()
    extras.start()
    each_map(k, first_norm)
    first.share_own()
    for o in (1, 2, 3):
        first.share(o)
    second.spread(1, 2, 3)
    first.finish()
    k.w_first = k.full_first.reshape(TAPS, WIDTH)
    k.w_second = k.full_second.reshape(TAPS, WIDTH)
    k.w_embed = k.full_embed.reshape(TEMB, WIDTH)
    k.w_mixed = k.full_mixed.reshape(WIDTH, 3 * WIDTH)
    k.w_out = k.full_out.reshape(WIDTH, WIDTH)
    each_map(k, first_conv)
    for gather in (gathers.mixed, gathers.out):
        gather.spread()
    gathers.embed.share()
    second.share_own()
    second.share(1)
    gathers.embed.finish()
    embed(k, k.pre[...])
    each_map(k, second_norm)
    second.share(2)
    second.share(3)
    second.finish()
    each_map(k, second_conv)
    gathers.mixed.share()
    gathers.out.share()
    extras.spread()
    each_map(k, third_norm)
    cot_copy.wait()
    gathers.mixed.finish()
    gathers.out.finish()
    each_map(k, *ATTENTION[1:])
    out_copy = n.local(k.out, k.out_done)

    reduces = SimpleNamespace()
    for name in EARLY:
        bufs = [getattr(k, f"reduce_{name}_{i}") for i in range(7)]
        setattr(reduces, name, Reduce(n, BOXES[name], EARLY[name], getattr(k, "grad_" + name), bufs))
    g_out = k.grad_out.reshape(WIDTH, WIDTH)
    g_mixed = k.grad_mixed.reshape(WIDTH, 3 * WIDTH)
    g_second = k.grad_second.reshape(TAPS, WIDTH)
    g_first = k.grad_first.reshape(TAPS, WIDTH)
    small = [reduces.out, reduces.mixed]
    first, second = reduces.first, reduces.second
    g_out[...] = dot(k.att_t[...], k.cot[...]).astype(BF16)
    g_mixed[...] = dot(k.nrm_t[...], k.g_mixed[...]).astype(BF16)
    for r in small:
        r.start()
    each_map(k, third_norm_back)
    for r in small:
        r.pair()
    extras.share()
    kernel_grad(k, k.a2_t, g_second)
    second.start()
    each_map(k, second_conv_back)
    second.pair()
    each_map(k, second_norm_back)
    sends = SmallGather(n, k.g_proj, k.g_proj_all)
    sends.start()
    for r in small:
        r.middle_late()
    kernel_grad(k, k.a1_t, g_first)
    order = (3, 2, 1, 0)
    for o in order:
        first.start(o)
    each_map(k, first_conv_back, first_norm_back)
    for o in order:
        first.pair(o)
    image_copy = n.local(k.image_grad, k.image_grad_done)
    sums = SmallSum(n, k.sums, k.sums_land)
    sums.exchange(0, [n.core_peer])
    sends.spread()
    second.middle_early()
    for r in small:
        r.owner()
    second.middle_late()
    sums.add()
    sums.exchange(1, [n.device(z=n.partner(o)) for o in (1, 2, 3)])
    for o in order[:2]:
        first.middle_late(o)
    if first.early:
        first.middle_early()
    for o in order[2:]:
        first.middle_late(o)
    sums.add()
    sums.exchange(4, [n.x_peer, n.y_peer, n.device(x=1 - n.x, y=1 - n.y)])
    first.owner()
    sends.share()
    second.owner()
    sends.finish()
    extras.finish()

    devices = 4 * 2 * z_size
    g_proj = k.g_proj_all[...].reshape(devices * 8, WIDTH)
    upper = lax.broadcasted_iota(jnp.int32, (devices * 8, 1), 0) % 8 < 4
    extra = k.extra_all[...].reshape(devices * 8, EXTRA)
    pre = extra[:, 0:HALF]
    sig = jax.nn.sigmoid(pre)
    e = pre * sig
    e_t = e.astype(BF16).T
    k.g_embed_all[0:HALF, :] = dot(e_t, jnp.where(upper, g_proj, 0.0).astype(BF16))
    k.g_embed_all[HALF:TEMB, :] = dot(e_t, jnp.where(upper, 0.0, g_proj).astype(BF16))
    g_e = dot_nt(g_proj.astype(BF16), k.w_embed[...])
    g_e = jnp.where(upper, g_e[:, 0:HALF], g_e[:, HALF:TEMB])
    k.g_pre[...] = g_e * (sig + e * (1.0 - sig))
    k.when[...] = extra[:, HALF:EXTRA].T[0:8, :]
    rows = TEMB // (2 * z_size)
    own_rows = pl.ds(pl.multiple_of(n.f * rows, rows), rows)
    done = [
        out_copy,
        image_copy,
        n.local(k.g_embed_all.at[own_rows, :], k.embed_done),
        n.local(k.g_pre, k.g_pre_done),
        n.local(k.when, k.when_done),
    ]
    sums.add()
    done.append(n.local(k.sums, k.sums_done))
    done += [
        reduces.out.finish(k.out_total),
        reduces.mixed.finish(k.mixed_total),
        second.finish(k.second_total),
        first.finish(k.first_total),
    ]
    for copy in done:
        copy.wait()
    n.finish()


def finish_kernel(names, arrays, *refs):
    k = Refs(names, refs, 1, 1)
    copies = {
        name: pltpu.make_async_copy(getattr(k, name + "_done"), getattr(k, name), k.sems.at[i])
        for i, name in enumerate(arrays)
    }
    for copy in copies.values():
        copy.start()
    stores = []

    def store(src, dst):
        copy = pltpu.make_async_copy(src, dst, k.sems.at[len(copies) + len(stores)])
        copy.start()
        stores.append(copy)

    copies["g_pre"].wait()
    copies["when"].wait()
    high, mid, low = split3(k.g_pre[...])
    steps = k.table.shape[0]
    chunk = 256
    for begin in range(0, steps, chunk):
        size = min(chunk, steps - begin)
        t = lax.broadcasted_iota(jnp.int32, (size, k.when.shape[1]), 0).astype(F32) + begin
        hit = t == k.when[0:1, :]
        upper = lax.broadcasted_iota(jnp.int32, hit.shape, 1) % 8 < 4
        block = slice(begin, begin + size)
        for half, rows in enumerate((upper, jnp.logical_not(upper))):
            selector = jnp.where(jnp.logical_and(hit, rows), 1.0, 0.0).astype(BF16)
            k.table[block, half * HALF : (half + 1) * HALF] = (
                dot(selector, high) + dot(selector, mid) + dot(selector, low)
            )
        store(k.table.at[block, :], k.table_grad.at[block, :])
    for name, to in (("out", k.out_final), ("image_grad", k.image_final), ("embed", k.embed_grad)):
        copies[name].wait()
        store(getattr(k, name), to)
    for name in ("out_total", "mixed_total", "second_total", "first_total"):
        copies[name].wait()
        wide = getattr(k, name + "_wide")
        wide[...] = getattr(k, name)[...].astype(F32)
        store(wide, getattr(k, name + "_grad"))
    copies["sums"].wait()
    width = k.vec_grad.shape[1]
    moved = pltpu.roll(k.sums[...], lax.rem(WIDTH - lax.axis_index(FSDP) * width, WIDTH), 1)
    k.vec_wide[...] = moved[0:12, 0:width]
    store(k.vec_wide, k.vec_grad)
    for copy in stores:
        copy.wait()


def fused(image, timesteps, time_table, conv_first, embed_weight, conv_second, qkv_weight, out_weight, vectors, cotangent):
    count, side = image.shape[:2]
    total = count * side * side
    z_size = lax.axis_size(FSDP) // 2
    slots = 4 * 2 * z_size * 8
    inputs = dict(
        x_in=image.reshape(total, WIDTH),
        cot_in=cotangent.reshape(total, WIDTH),
        steps_in=timesteps,
        time_table=time_table,
        shard_first=conv_first,
        shard_embed=embed_weight,
        shard_second=conv_second,
        shard_mixed=qkv_weight,
        shard_out=out_weight,
        vectors_in=vectors,
    )
    between = dict(
        g_pre=((slots, HALF), F32),
        when=((8, slots), F32),
        out=((total, WIDTH), BF16),
        image_grad=((total, WIDTH), BF16),
        embed=(embed_weight.shape, F32),
        out_total=(out_weight.shape, BF16),
        mixed_total=(qkv_weight.shape, BF16),
        second_total=(conv_second.shape, BF16),
        first_total=(conv_first.shape, BF16),
        sums=((16, WIDTH), F32),
    )
    scratch = scratch_of(count, side)
    for name in ("x", "cot", "out", "image_grad"):
        scratch[name] = ((total, WIDTH), BF16)
    for name, box in BOXES.items():
        scratch["full_" + name] = ((z_size, 2, box.rows, box.lanes), BF16)
    for name in EARLY:
        box = BOXES[name]
        scratch["grad_" + name] = ((z_size, 2, box.rows, box.lanes), BF16)
        for i, buf in enumerate(Reduce.buffers(box, EARLY[name], z_size)):
            scratch[f"reduce_{name}_{i}"] = buf
    scratch.update(vectors=(vectors.shape, BF16))
    scratch.update(table=(time_table.shape, F32))
    scratch.update(pre=((8, TEMB), F32))
    scratch.update(extra=((8, EXTRA), F32))
    scratch.update(extra_all=((z_size, 2, 2, 2, 8, EXTRA), F32))
    scratch.update(g_proj_all=((z_size, 2, 2, 2, 8, WIDTH), F32))
    scratch.update(g_embed_all=((TEMB, WIDTH), F32))
    scratch.update(g_pre=between["g_pre"])
    scratch.update(when=between["when"])
    scratch.update(vec_own=((16, 128), BF16))
    scratch.update(vec_room=((2 * z_size - 1, 16, 128), BF16))
    scratch.update(vec_all=((z_size, 2, 16, 128), BF16))
    scratch.update(vec=((16, WIDTH), F32))
    scratch.update(sums_land=((7, 16, WIDTH), F32))
    sems = dict(send_sems=SENDS, recv_sems=LANDINGS, local_sems=23)
    names = list(inputs)
    names += [name if name.endswith("_total") else name + "_done" for name in between]
    names += list(scratch) + list(sems) + ["steps"]
    anywhere = pl.BlockSpec(memory_space=pl.ANY)
    results = pl.pallas_call(
        functools.partial(whole_kernel, names, count, side, z_size),
        out_shape=[jax.ShapeDtypeStruct(*v) for v in between.values()],
        in_specs=[anywhere] * len(inputs),
        out_specs=[anywhere] * len(between),
        scratch_shapes=[pltpu.VMEM(*v) for v in scratch.values()]
        + [pltpu.SemaphoreType.DMA((size,)) for size in sems.values()]
        + [pltpu.SMEM(timesteps.shape, jnp.int32)],
        compiler_params=pltpu.CompilerParams(
            collective_id=0, has_side_effects=True, vmem_limit_bytes=VMEM_BYTES
        ),
        name="block",
    )(*inputs.values())

    outputs = dict(
        out_final=((total, WIDTH), BF16),
        image_final=((total, WIDTH), BF16),
        table_grad=(time_table.shape, F32),
        first_total_grad=(conv_first.shape, F32),
        embed_grad=(embed_weight.shape, F32),
        second_total_grad=(conv_second.shape, F32),
        mixed_total_grad=(qkv_weight.shape, F32),
        out_total_grad=(out_weight.shape, F32),
        vec_grad=(vectors.shape, F32),
    )
    scratch = dict(between)
    scratch.update(table=(time_table.shape, F32))
    scratch.update(vec_wide=(vectors.shape, F32))
    for name in between:
        if name.endswith("_total"):
            scratch[name + "_wide"] = (between[name][0], F32)
    names = [name + "_done" for name in between] + list(outputs) + list(scratch) + ["sems"]
    results = pl.pallas_call(
        functools.partial(finish_kernel, names, list(between)),
        out_shape=[jax.ShapeDtypeStruct(*v) for v in outputs.values()],
        in_specs=[anywhere] * len(between),
        out_specs=[anywhere] * len(outputs),
        scratch_shapes=[pltpu.VMEM(*v) for v in scratch.values()]
        + [pltpu.SemaphoreType.DMA((32,))],
        compiler_params=pltpu.CompilerParams(vmem_limit_bytes=VMEM_BYTES),
        name="finish",
    )(*results)
    out, image_grad, *rest = results
    return (out.reshape(image.shape), image_grad.reshape(image.shape), *rest)


def local_kernel(names, count, side, *refs):
    k = Refs(names, refs, count, side)
    start_compute(k)
    embed(k, k.pre[...])
    each_map(k, first_norm, first_conv, second_norm, second_conv, *ATTENTION)
    k.grad_out[...] = dot(k.att_t[...], k.cot[...]).astype(BF16)
    k.grad_mixed[...] = dot(k.nrm_t[...], k.g_mixed[...]).astype(BF16)
    each_map(k, third_norm_back)
    kernel_grad(k, k.a2_t, k.grad_second)
    each_map(k, second_conv_back, second_norm_back)
    kernel_grad(k, k.a1_t, k.grad_first)
    each_map(k, first_conv_back, first_norm_back)
    k.vec_grad[...] = k.sums[...]
    k.g_proj_out[...] = k.g_proj[...]


def plain(image, timesteps, time_table, conv_first, embed_weight, conv_second, qkv_weight, out_weight, vectors, cotangent):
    count, side = image.shape[:2]
    total = count * side * side

    def whole(w, axis=0):
        return lax.all_gather(w, FSDP, axis=axis, tiled=True)

    pre = time_table[timesteps]
    w_embed = whole(embed_weight)
    inputs = dict(
        x=image.reshape(total, WIDTH),
        cot=cotangent.reshape(total, WIDTH),
        w_first=whole(conv_first),
        w_embed=w_embed,
        w_second=whole(conv_second),
        w_mixed=whole(qkv_weight),
        w_out=whole(out_weight),
        vec=jnp.pad(whole(vectors, 1).astype(F32), ((0, 4), (0, 0))),
        pre=jnp.pad(pre, ((0, 8 - count), (0, 0))),
    )
    outputs = dict(
        out=((total, WIDTH), BF16),
        image_grad=((total, WIDTH), BF16),
        grad_first=((TAPS, WIDTH), BF16),
        grad_second=((TAPS, WIDTH), BF16),
        grad_mixed=((WIDTH, 3 * WIDTH), BF16),
        grad_out=((WIDTH, WIDTH), BF16),
        vec_grad=((16, WIDTH), F32),
        g_proj_out=((8, WIDTH), F32),
    )
    scratch = scratch_of(count, side)
    names = list(inputs) + list(outputs) + list(scratch)
    vmem = pl.BlockSpec(memory_space=pltpu.VMEM)
    results = pl.pallas_call(
        functools.partial(local_kernel, names, count, side),
        out_shape=[jax.ShapeDtypeStruct(*v) for v in outputs.values()],
        in_specs=[vmem] * len(inputs),
        out_specs=[vmem] * len(outputs),
        scratch_shapes=[pltpu.VMEM(*v) for v in scratch.values()],
        compiler_params=pltpu.CompilerParams(vmem_limit_bytes=VMEM_BYTES),
        name="block_alone",
    )(*inputs.values())
    out, image_grad, g_first, g_second, g_mixed, g_out, g_vec, g_proj = results
    g_proj = g_proj[:count].astype(BF16)

    def owned(g, axis=0):
        own = lax.psum_scatter(g.astype(BF16), FSDP, scatter_dimension=axis, tiled=True)
        return lax.psum(own, DP).astype(F32)

    e = (pre * jax.nn.sigmoid(pre)).astype(BF16)
    g_embed = lax.dot_general(e, g_proj, TN, preferred_element_type=F32)
    sig = jax.nn.sigmoid(pre)
    g_pre = dot_nt(g_proj, w_embed) * (sig * (1.0 + pre * (1.0 - sig)))
    rows = lax.all_gather(g_pre, (FSDP, DP), axis=0, tiled=True)
    where = lax.all_gather(timesteps, (FSDP, DP), axis=0, tiled=True)
    table_grad = jnp.zeros(time_table.shape, F32).at[where].add(rows)
    return (
        out.reshape(image.shape),
        image_grad.reshape(image.shape),
        table_grad,
        owned(g_first),
        owned(g_embed),
        owned(g_second),
        owned(g_mixed),
        owned(g_out),
        owned(g_vec[: vectors.shape[0]], 1),
    )


def solution(mesh):
    placed = (
        P((FSDP, DP), None, None, None),
        P((FSDP, DP)),
        P(),
        P(FSDP, None),
        P(FSDP, None),
        P(FSDP, None),
        P(FSDP, None),
        P(FSDP, None),
        P(None, FSDP),
        P((FSDP, DP), None, None, None),
    )
    grid = (mesh.shape[FSDP], mesh.shape[DP])
    return jax.shard_map(
        fused if grid == (8, 4) else plain,
        mesh=mesh,
        in_specs=placed,
        out_specs=(
            P((FSDP, DP), None, None, None),
            P((FSDP, DP), None, None, None),
            P(),
            P(FSDP, None),
            P(FSDP, None),
            P(FSDP, None),
            P(FSDP, None),
            P(FSDP, None),
            P(None, FSDP),
        ),
        check_vma=False,
    )
```

```python
import functools
from types import SimpleNamespace

import jax
import jax.numpy as jnp
from jax import lax
from jax.experimental import pallas as pl
from jax.experimental.pallas import tpu as pltpu
from jax.sharding import PartitionSpec as P

FSDP, DP = "fsdp", "dp"
F32 = jnp.float32
BF16 = jnp.bfloat16
MESH = pl.DeviceIdType.MESH
EPS = 1e-06
WIDTH = 256
GROUP = 8
TEMB = 512
TAPS = 9 * WIDTH
HALF = TEMB // 2
EXTRA = HALF + 128
VMEM_BYTES = 56 * 2**20
NT = (((1,), (1,)), ((), ()))
TN = (((0,), (0,)), ((), ()))


def dot(a, b):
    return jnp.dot(a, b, preferred_element_type=F32)


def dot_nt(a, b):
    return lax.dot_general(a, b, NT, preferred_element_type=F32)


def split3(v):
    high = v.astype(BF16)
    rest = v - high.astype(F32)
    mid = rest.astype(BF16)
    return high, mid, (rest - mid.astype(F32)).astype(BF16)


def colsum(v):
    return jnp.sum(v, axis=0, keepdims=True)


def group_mean(row, averager):
    high, mid, low = split3(row)
    return dot(high, averager) + dot(mid, averager) + dot(low, averager)


class Refs:
    def __init__(self, names, refs, count, side):
        for name, ref in zip(names, refs):
            setattr(self, name, ref)
        self.count, self.side, self.places = count, side, side * side

    def rows(self, m):
        return pl.ds(m * self.places, self.places)


def scratch_of(count, side):
    places = side * side
    total = count * places
    padded = places + 2 * side
    return dict(
        averager=((WIDTH, WIDTH), BF16),
        shifted_a=((count, padded, 3 * WIDTH), BF16),
        shifted_g=((count, padded, 3 * WIDTH), BF16),
        unit1=((total, WIDTH), F32),
        slope1=((total, WIDTH), F32),
        inv1=((count, 1, WIDTH), F32),
        unit2=((total, WIDTH), F32),
        slope2=((total, WIDTH), F32),
        inv2=((count, 1, WIDTH), F32),
        unit3=((total, WIDTH), F32),
        inv3=((count, 1, WIDTH), F32),
        a1_t=((WIDTH, total), BF16),
        a2_t=((WIDTH, total), BF16),
        nrm_t=((WIDTH, total), BF16),
        att_t=((WIDTH, total), BF16),
        nrm=((total, WIDTH), BF16),
        mixed=((total, 3 * WIDTH), BF16),
        g_att=((total, WIDTH), BF16),
        probs=((total, places), F32),
        probs_low=((total, places), BF16),
        probs_t=((places, total), BF16),
        att=((total, WIDTH), BF16),
        g_probs=((total, places), F32),
        g_scores=((total, places), BF16),
        g_scores_t=((places, total), BF16),
        conv_out=((total, WIDTH), F32),
        resid=((total, WIDTH), F32),
        g_mixed=((total, 3 * WIDTH), BF16),
        proj=((8, WIDTH), F32),
        sums=((16, WIDTH), F32),
        g_proj=((8, WIDTH), F32),
    )


def start_compute(k):
    rows = lax.broadcasted_iota(jnp.int32, (WIDTH, WIDTH), 0) // GROUP
    cols = lax.broadcasted_iota(jnp.int32, (WIDTH, WIDTH), 1) // GROUP
    k.averager[...] = jnp.where(rows == cols, 1.0 / (k.places * GROUP), 0.0).astype(BF16)
    edge = jnp.zeros((k.count, k.side, 3 * WIDTH), BF16)
    for ref in (k.shifted_a, k.shifted_g):
        ref[:, 0 : k.side, :] = edge
        ref[:, k.places + k.side : k.places + 2 * k.side, :] = edge
    k.sums[...] = jnp.zeros(k.sums.shape, F32)
    k.g_proj[...] = jnp.zeros(k.g_proj.shape, F32)


def store_shifted(k, ref, m, a):
    column = lax.broadcasted_iota(jnp.int32, a.shape, 0) % k.side
    inner = slice(k.side, k.side + k.places)
    left = jnp.where(column == 0, 0.0, pltpu.roll(a, 1, 0))
    right = jnp.where(column == k.side - 1, 0.0, pltpu.roll(a, k.places - 1, 0))
    ref[m, inner, 0:WIDTH] = left.astype(BF16)
    ref[m, inner, WIDTH : 2 * WIDTH] = a.astype(BF16)
    ref[m, inner, 2 * WIDTH : 3 * WIDTH] = right.astype(BF16)


def normalize(k, u):
    averager = k.averager[...]
    centered = u - group_mean(colsum(u), averager)
    inverse = lax.rsqrt(group_mean(colsum(centered * centered), averager) + EPS)
    return centered * inverse, inverse


def norm_swish(k, u, m, j, unit_ref, slope_ref, inv_ref):
    unit, inverse = normalize(k, u)
    unit_ref[k.rows(m), :] = unit
    inv_ref[m] = inverse
    h = unit * (1.0 + k.vec[j : j + 1, :]) + k.vec[j + 1 : j + 2, :]
    sig = jax.nn.sigmoid(h)
    a = h * sig
    slope_ref[k.rows(m), :] = sig + a * (1.0 - sig)
    return a


def norm_back(k, upstream, unit, inverse, j):
    averager = k.averager[...]
    g_gain = colsum(upstream * unit)
    g_shift = colsum(upstream)
    k.sums[j : j + 1, :] += g_gain
    k.sums[j + 1 : j + 2, :] += g_shift
    gain = 1.0 + k.vec[j : j + 1, :]
    first = group_mean(g_shift * gain, averager)
    second = group_mean(g_gain * gain, averager)
    return inverse * (upstream * gain - first - unit * second)


def convolve(k, ref, w, m):
    total = None
    for ky in range(3):
        window = ref[m, ky * k.side : ky * k.side + k.places, :]
        term = dot(window, w[ky * 3 * WIDTH : (ky + 1) * 3 * WIDTH, :])
        total = term if total is None else total + term
    return total


def convolve_back(k, ref, w, m):
    total = None
    for ky in range(3):
        for kx in range(3):
            window = ref[
                m,
                (2 - ky) * k.side : (2 - ky) * k.side + k.places,
                (2 - kx) * WIDTH : (3 - kx) * WIDTH,
            ]
            tap = 3 * ky + kx
            term = dot_nt(window, w[tap * WIDTH : (tap + 1) * WIDTH, :])
            total = term if total is None else total + term
    return total


def kernel_grad(k, a_t, g_w, ky):
    start = (2 - ky) * k.side
    row = ky * 3 * WIDTH
    if not isinstance(ky, int):
        start, row = pl.multiple_of(start, k.side), pl.multiple_of(row, WIDTH)
    window = k.shifted_g[:, pl.ds(start, k.places), :]
    term = dot(a_t[...], window.reshape(k.count * k.places, 3 * WIDTH))
    for kx in range(3):
        g_w[pl.ds(row + kx * WIDTH, WIDTH), :] = term[
            :, (2 - kx) * WIDTH : (3 - kx) * WIDTH
        ].astype(BF16)


def first_norm(k, m):
    a = norm_swish(k, k.x[k.rows(m), :].astype(F32), m, 0, k.unit1, k.slope1, k.inv1)
    store_shifted(k, k.shifted_a, m, a)
    k.a1_t[:, k.rows(m)] = a.astype(BF16).T


def embed(k, pre):
    e = (pre * jax.nn.sigmoid(pre)).astype(BF16)
    k.proj[...] = dot(e, k.w_embed[...]) + k.vec[3:4, :]


def first_conv(k, m):
    k.conv_out[k.rows(m), :] = convolve(k, k.shifted_a, k.w_first, m)


def second_norm(k, m):
    h1 = k.conv_out[k.rows(m), :] + (k.vec[2:3, :] + k.proj[m : m + 1, :])
    a = norm_swish(k, h1, m, 4, k.unit2, k.slope2, k.inv2)
    store_shifted(k, k.shifted_a, m, a)
    k.a2_t[:, k.rows(m)] = a.astype(BF16).T


def second_conv(k, m):
    x = k.x[k.rows(m), :].astype(F32)
    k.resid[k.rows(m), :] = x + convolve(k, k.shifted_a, k.w_second, m) + k.vec[6:7, :]


def third_norm(k, m):
    rows = k.rows(m)
    unit, inverse = normalize(k, k.resid[rows, :])
    k.unit3[rows, :] = unit
    k.inv3[m] = inverse
    nrm = (unit * (1.0 + k.vec[7:8, :]) + k.vec[8:9, :]).astype(BF16)
    k.nrm[rows, :] = nrm
    k.nrm_t[:, rows] = nrm.T


def project(k, m):
    rows = k.rows(m)
    mixed = dot(k.nrm[rows, :], k.w_mixed[...])
    k.mixed[rows, 0:WIDTH] = (mixed[:, :WIDTH] + k.vec[9:10, :]).astype(BF16)
    k.mixed[rows, WIDTH : 2 * WIDTH] = mixed[:, WIDTH : 2 * WIDTH].astype(BF16)
    k.mixed[rows, 2 * WIDTH :] = (mixed[:, 2 * WIDTH :] + k.vec[10:11, :]).astype(BF16)


def upstream(k, m):
    cot = k.cot[k.rows(m), :]
    k.sums[11:12, :] += colsum(cot.astype(F32))
    k.g_att[k.rows(m), :] = dot_nt(cot, k.w_out[...]).astype(BF16)


def softmax(k, m):
    rows = k.rows(m)
    scores = dot_nt(k.mixed[rows, 0:WIDTH], k.mixed[rows, WIDTH : 2 * WIDTH]) * WIDTH**-0.5
    raised = jnp.exp(scores - jnp.max(scores, axis=1, keepdims=True))
    probs = raised * (1.0 / jnp.sum(raised, axis=1, keepdims=True))
    k.probs[rows, :] = probs
    low = probs.astype(BF16)
    k.probs_low[rows, :] = low
    k.probs_t[:, rows] = low.T


def attend(k, m):
    rows = k.rows(m)
    value = k.mixed[rows, 2 * WIDTH :]
    att = dot(k.probs_low[rows, :], value).astype(BF16)
    k.att[rows, :] = att
    k.att_t[:, rows] = att.T
    k.g_probs[rows, :] = dot_nt(k.g_att[rows, :], value)


def emit(k, m):
    rows = k.rows(m)
    branch = dot(k.att[rows, :], k.w_out[...])
    k.out[rows, :] = (k.resid[rows, :] + branch + k.vec[11:12, :]).astype(BF16)


def softmax_back(k, m):
    rows = k.rows(m)
    probs, g_probs = k.probs[rows, :], k.g_probs[rows, :]
    weighted = jnp.sum(probs * g_probs, axis=1, keepdims=True)
    g_scores = (probs * (g_probs - weighted)).astype(BF16)
    k.g_scores[rows, :] = g_scores
    k.g_scores_t[:, rows] = g_scores.T
    g_value = dot(k.probs_t[:, rows], k.g_att[rows, :]).astype(BF16)
    k.sums[10:11, :] += colsum(g_value.astype(F32))
    k.g_mixed[rows, 2 * WIDTH :] = g_value


def project_back(k, m):
    rows = k.rows(m)
    scale = WIDTH**-0.5
    g_query = (dot(k.g_scores[rows, :], k.mixed[rows, WIDTH : 2 * WIDTH]) * scale).astype(BF16)
    g_key = (dot(k.g_scores_t[:, rows], k.mixed[rows, 0:WIDTH]) * scale).astype(BF16)
    k.sums[9:10, :] += colsum(g_query.astype(F32))
    k.g_mixed[rows, 0:WIDTH] = g_query
    k.g_mixed[rows, WIDTH : 2 * WIDTH] = g_key


ATTENTION = (third_norm, project, upstream, softmax, attend, emit, softmax_back, project_back)


def third_norm_back(k, m):
    rows = k.rows(m)
    g_nrm = dot_nt(k.g_mixed[rows, :], k.w_mixed[...])
    g_resid = k.cot[rows, :].astype(F32) + norm_back(
        k, g_nrm, k.unit3[rows, :], k.inv3[m], 7
    )
    k.resid[rows, :] = g_resid
    g_conv = g_resid.astype(BF16).astype(F32)
    k.sums[6:7, :] += colsum(g_conv)
    store_shifted(k, k.shifted_g, m, g_conv)


def second_conv_back(k, m):
    rows = k.rows(m)
    k.conv_out[rows, :] = convolve_back(k, k.shifted_g, k.w_second, m) * k.slope2[rows, :]


def second_norm_back(k, m):
    rows = k.rows(m)
    g_h1 = norm_back(k, k.conv_out[rows, :], k.unit2[rows, :], k.inv2[m], 4)
    g_h1 = g_h1.astype(BF16).astype(F32)
    per_map = colsum(g_h1)
    k.sums[2:3, :] += per_map
    g_proj = per_map.astype(BF16).astype(F32)
    k.sums[3:4, :] += g_proj
    k.g_proj[m : m + 1, :] = g_proj
    k.g_proj[m + 4 : m + 5, :] = g_proj
    store_shifted(k, k.shifted_g, m, g_h1)


def first_conv_back(k, m):
    rows = k.rows(m)
    k.conv_out[rows, :] = convolve_back(k, k.shifted_g, k.w_first, m) * k.slope1[rows, :]


def first_norm_back(k, m):
    rows = k.rows(m)
    g_x = norm_back(k, k.conv_out[rows, :], k.unit1[rows, :], k.inv1[m], 0)
    k.image_grad[rows, :] = (k.resid[rows, :] + g_x).astype(BF16)


def each_map(k, *steps):
    for step in steps:
        for m in range(k.count):
            step(k, m)


class Links:
    def __init__(self, send_sems, recv_sems, local_sems, z_size):
        f, d = lax.axis_index(FSDP), lax.axis_index(DP)
        self.f, self.z_size = f, z_size
        self.z, self.y = f // 2, f % 2
        self.x, self.c = d // 2, d % 2
        self.send_sems, self.recv_sems, self.local_sems = send_sems, recv_sems, local_sems
        self.started, self.n_sent, self.n_local = [], 0, 0
        self.n_received, self.left = 0, set()

    def device(self, z=None, y=None, x=None, c=None):
        z = self.z if z is None else z
        y = self.y if y is None else y
        x = self.x if x is None else x
        c = self.c if c is None else c
        return (z * 2 + y, x * 2 + c)

    def partner(self, k):
        return (self.z, self.z + 1 - 2 * (self.z % 2), (self.z + 2) % 4, 3 - self.z)[k]

    def turn(self, o):
        upper = self.z // 2
        return ((1 - upper) * 3, 2 - upper, self.partner(1), self.z)[o]

    @property
    def x_peer(self):
        return self.device(x=1 - self.x)

    @property
    def y_peer(self):
        return self.device(y=1 - self.y)

    @property
    def core_peer(self):
        return self.device(c=1 - self.c)

    def send(self, src, dst, device, landing=None):
        if self.n_sent >= SENDS:
            self.sent(self.started[self.n_sent - SENDS])
        if landing is None:
            landing = self.landing()
        copy = pltpu.make_async_remote_copy(
            src_ref=src,
            dst_ref=dst,
            send_sem=self.send_sems.at[self.n_sent % SENDS],
            recv_sem=self.recv_sems.at[landing],
            device_id=device,
            device_id_type=MESH,
        )
        copy.start()
        self.n_sent += 1
        self.started.append(copy)
        return copy

    def landing(self):
        self.n_received += 1
        return self.n_received - 1

    def send_all(self, triples, room):
        landing = self.landing()
        for src, dst, device in triples:
            self.send(src, dst, device, landing)
        return pltpu.make_async_copy(room, room, self.recv_sems.at[landing])

    def sent(self, copy):
        spot = [c is copy for c in self.started].index(True)
        if spot not in self.left:
            copy.wait_send()
            self.left.add(spot)

    def local(self, src, dst):
        copy = pltpu.make_async_copy(src, dst, self.local_sems.at[self.n_local])
        self.n_local += 1
        copy.start()
        return copy

    def finish(self):
        for copy in self.started:
            self.sent(copy)

    def greet(self):
        barrier = pltpu.get_barrier_semaphore()
        peers = [
            self.device(z=self.partner(o), y=y)
            for o in range(4)
            for y in (self.y, 1 - self.y)
            if not (o == 0 and y is self.y)
        ]
        peers += [self.x_peer, self.core_peer, self.device(x=1 - self.x, c=1 - self.c)]
        peers += [self.device(x=1 - self.x, y=1 - self.y)]
        for peer in peers:
            pl.semaphore_signal(barrier, inc=1, device_id=peer, device_id_type=MESH)
        return lambda: pl.semaphore_wait(barrier, len(peers))


class Box:
    def __init__(self, rows, lanes):
        self.rows, self.lanes = rows, lanes
        self.half_rows, self.half_lanes = rows // 2, lanes // 2

    def rows_of(self, c):
        return pl.ds(pl.multiple_of(c * self.half_rows, 16), self.half_rows)

    def lanes_of(self, x):
        return pl.ds(pl.multiple_of(x * self.half_lanes, 128), self.half_lanes)


class Gather:
    def __init__(self, links, box, shard, full, parts=False):
        self.n, self.box, self.shard, self.full = links, box, shard, full
        self.by_parts = parts
        self.sides, self.core = {}, []

    def start(self):
        n, box = self.n, self.box
        src = self.shard.at[box.rows_of(n.c), box.lanes_of(n.x)]
        dst = self.full.at[n.z, n.y, box.rows_of(n.c), box.lanes_of(n.x)]
        routes = [(src, dst, n.device(z=n.partner(o))) for o in (1, 2, 3)]
        if self.by_parts:
            self.z_copies = {o: n.send(*route) for o, route in zip((1, 2, 3), routes)}
        else:
            self.z_copies = n.send_all(routes, self.room(1))
            self.own = n.local(src, dst)

    def room(self, o):
        rows, w = self.box.rows if o is None else self.box.half_rows, self.box.half_lanes
        return self.full.at[0:3, 0 : 2 if o is None else 1, 0:rows, 0:w]

    def start_own(self):
        n, box = self.n, self.box
        src = self.shard.at[box.rows_of(n.c), :]
        self.own_y = n.send(src, self.full.at[n.z, n.y, box.rows_of(n.c), :], n.y_peer)
        self.own = n.local(self.shard, self.full.at[n.z, n.y])

    def part(self, o, y, x):
        n, box = self.n, self.box
        p = slice(None) if o is None else n.partner(o)
        return self.full.at[p, y, box.rows_of(n.c), box.lanes_of(x)]

    def spread(self, *parts):
        n = self.n
        for o in parts or (None,):
            if o is None:
                self.z_copies.wait()
                self.own.wait()
            else:
                self.z_copies[o].wait_recv()
            mine = self.part(o, n.y, n.x)
            peers = (n.x_peer, n.y_peer, n.device(x=1 - n.x, y=1 - n.y))
            room = self.room(o)
            self.sides[o] = n.send_all([(mine, mine, peer) for peer in peers], room)

    def share_own(self):
        n, box = self.n, self.box
        self.own_y.wait_recv()
        block = self.full.at[n.z, 1 - n.y, box.rows_of(n.c), :]
        self.core.append(n.send(block, block, n.core_peer))

    def share(self, o=None):
        n, box = self.n, self.box
        self.sides[o].wait()
        p = slice(None) if o is None else n.partner(o)
        block = self.full.at[p, :, box.rows_of(n.c), :]
        self.core.append(n.send(block, block, n.core_peer))

    def finish(self):
        for copy in self.core:
            copy.wait_recv()
        if self.by_parts:
            self.own.wait()


class SmallGather:
    def __init__(self, links, block, full):
        self.n, self.block, self.full = links, block, full

    def start(self):
        n = self.n
        dst = self.full.at[n.z, n.y, n.x, n.c]
        routes = [(self.block, dst, n.device(z=n.partner(o))) for o in (1, 2, 3)]
        self.z_copies = n.send_all(routes, self.full.at[0:3, 0, 0, 0])
        self.own = n.local(self.block, dst)

    def spread(self):
        n = self.n
        self.z_copies.wait()
        self.own.wait()
        mine = self.full.at[:, n.y, n.x, n.c]
        peers = (n.x_peer, n.y_peer, n.device(x=1 - n.x, y=1 - n.y))
        self.sides = n.send_all([(mine, mine, peer) for peer in peers], self.full.at[0:3, :, :, 0])

    def share(self):
        n = self.n
        self.sides.wait()
        block = self.full.at[:, :, :, n.c]
        self.core = n.send(block, block, n.core_peer)

    def finish(self):
        self.core.wait_recv()


class Reduce:
    def __init__(self, links, box, early, grad, bufs):
        self.n, self.box, self.early, self.grad = links, box, early, grad
        self.from_core, self.held, self.z_early, self.sides_early, self.sides_late, self.z_late, self.total = bufs
        self.core, self.sides = {}, {}
        self.early_landing = self.late_landing = None

    @staticmethod
    def buffers(box, early, z):
        w, late = box.half_lanes, max(box.half_rows - early, 16)
        return [
            ((z, 2, box.half_rows, box.lanes), BF16),
            ((z, 2, box.half_rows, box.lanes), BF16),
            ((3, 2, max(early, 16), box.lanes), BF16),
            ((3, max(early, 16), w), BF16),
            ((3, z, late, w), BF16),
            ((3, late, w), BF16),
            ((box.rows, box.lanes), BF16),
        ]

    def spot(self, o):
        return slice(None) if o is None else self.n.turn(o)

    def to_z(self, o):
        n = self.n
        if o is None:
            return [(n.partner(k), k - 1) for k in (3, 2, 1)]
        z = n.turn(o)
        k = lax.rem(n.z + z, 2) + 2 * lax.rem(n.z // 2 + z // 2, 2)
        return [] if o == 3 else [(z, k - 1)]

    def rows(self, late):
        return slice(self.early, self.box.half_rows) if late else slice(0, self.early)

    def around(self):
        n = self.n
        return (
            (1 - n.y, 1 - n.x, n.device(x=1 - n.x, y=1 - n.y)),
            (1 - n.y, n.x, n.y_peer),
            (n.y, 1 - n.x, n.x_peer),
        )

    def start(self, o=None):
        n, box, p = self.n, self.box, self.spot(o)
        src = self.grad.at[p, :, box.rows_of(1 - n.c), :]
        self.core[o] = n.send(src, self.from_core.at[p], n.core_peer)

    def pair(self, o=None):
        n, box, p = self.n, self.box, self.spot(o)
        self.core[o].wait_recv()
        mine = self.grad[p, :, box.rows_of(n.c), :].astype(F32)
        self.held[p] = (mine + self.from_core[p].astype(F32)).astype(BF16)
        if self.early and self.early_landing is None:
            self.early_landing = n.landing()
        if self.early:
            for z, slot in self.to_z(o):
                src = self.held.at[z, :, self.rows(False), :]
                n.send(src, self.z_early.at[slot], n.device(z=z), self.early_landing)
        if self.early < box.half_rows:
            routes = [
                (
                    self.held.at[p, y, self.rows(True), box.lanes_of(x)],
                    self.sides_late.at[i, p],
                    peer,
                )
                for i, (y, x, peer) in enumerate(self.around())
            ]
            self.sides[o] = n.send_all(routes, self.sides_late.at[:, slice(None) if o is None else 0])

    def wait(self, landing, room):
        pltpu.make_async_copy(room, room, self.n.recv_sems.at[landing]).wait()

    def middle_early(self):
        n, box = self.n, self.box
        self.wait(self.early_landing, self.z_early)
        at = (n.z, slice(None), self.rows(False), slice(None))
        summed = self.held[at].astype(F32)
        for i in range(3):
            summed = summed + self.z_early[i].astype(F32)
        self.held[at] = summed.astype(BF16)
        routes = [
            (self.held.at[n.z, y, self.rows(False), box.lanes_of(x)], self.sides_early.at[i], peer)
            for i, (y, x, peer) in enumerate(self.around())
        ]
        self.early_sides = n.send_all(routes, self.sides_early)

    def middle_late(self, o=None):
        n, box, p = self.n, self.box, self.spot(o)
        self.sides[o].wait()
        at = (p, n.y, self.rows(True), box.lanes_of(n.x))
        summed = self.held[at].astype(F32)
        for i in range(3):
            summed = summed + self.sides_late[i, p].astype(F32)
        self.held[at] = summed.astype(BF16)
        if self.late_landing is None:
            self.late_landing = n.landing()
        for z, slot in self.to_z(o):
            src = self.held.at[z, n.y, self.rows(True), box.lanes_of(n.x)]
            n.send(src, self.z_late.at[slot], n.device(z=z), self.late_landing)

    def owner(self):
        n, box = self.n, self.box
        if self.early:
            self.early_sides.wait()
        if self.early < box.half_rows:
            self.wait(self.late_landing, self.z_late)
        for late, lands in ((False, self.sides_early), (True, self.z_late)):
            rows = self.rows(late)
            size = rows.stop - rows.start
            if size:
                summed = self.held[n.z, n.y, rows, box.lanes_of(n.x)].astype(F32)
                for i in range(3):
                    summed = summed + lands[i].astype(F32)
                first = pl.multiple_of(n.c * box.half_rows + rows.start, 16)
                self.total[pl.ds(first, size), box.lanes_of(n.x)] = summed.astype(BF16)
        mine = self.total.at[box.rows_of(n.c), box.lanes_of(n.x)]
        peers = (n.x_peer, n.device(x=1 - n.x, c=1 - n.c), n.core_peer)
        self.replicas = n.send_all(
            [(mine, mine, peer) for peer in peers],
            self.from_core.at[0:3, 0, :, 0 : box.half_lanes],
        )

    def finish(self, out):
        self.replicas.wait()
        out[...] = self.total[...]


class SmallSum:
    def __init__(self, links, block, land):
        self.n, self.block, self.land = links, block, land

    def exchange(self, first, peers):
        self.slots = range(first, first + len(peers))
        routes = [(self.block, self.land.at[i], peer) for i, peer in zip(self.slots, peers)]
        self.arrivals = self.n.send_all(routes, self.land.at[first : first + len(peers)])
        self.copies = self.n.started[-len(peers) :]

    def add(self):
        self.arrivals.wait()
        parts = [self.land[slot] for slot in self.slots]
        total = self.block[...] + parts[0]
        if len(parts) == 3:
            total = total + (parts[1] + parts[2])
        for copy in self.copies:
            self.n.sent(copy)
        self.block[...] = total


def grad_and_start(k, n, a_t, g_w, reduce):
    upper = n.z // 2
    for steps, ready in (((0, 1), (0, 1)), ((2,), (2, 3))):
        for step in steps:
            kernel_grad(k, a_t, g_w, (1 - upper) * (2 - step) + upper * step)
        for o in ready:
            reduce.start(o)


BOXES = dict(
    first=Box(288, 256),
    embed=Box(64, 256),
    second=Box(288, 256),
    mixed=Box(32, 768),
    out=Box(32, 256),
)
EARLY = dict(first=32, second=48, mixed=0, out=0)
SENDS = 32
LANDINGS = 73


def whole_kernel(names, count, side, z_size, *refs):
    k = Refs(names, refs, count, side)
    n = Links(k.send_sems, k.recv_sems, k.local_sems, z_size)
    arrived = n.greet()
    vectors_copy = n.local(k.vectors_in, k.vectors)
    steps_copy = n.local(k.steps_in, k.steps)
    x_copy = n.local(k.x_in, k.x)
    table_copy = n.local(k.time_table, k.table)
    cot_copy = n.local(k.cot_in, k.cot)

    arrived()
    gathers = SimpleNamespace(**{
        name: Gather(
            n,
            box,
            getattr(k, "shard_" + name),
            getattr(k, "full_" + name),
            parts=name in ("first", "second"),
        )
        for name, box in BOXES.items()
    })
    first, second = gathers.first, gathers.second
    first.start()
    first.start_own()
    vectors_copy.wait()
    width = k.vectors.shape[1]
    lane = lax.broadcasted_iota(jnp.int32, (width, 128), 1)
    row = lax.broadcasted_iota(jnp.int32, (width, 128), 0)
    place = jnp.where(lane == row + lax.rem(n.f * width, 128), 1.0, 0.0).astype(BF16)
    own_vec = dot(k.vectors[...], place).astype(BF16)
    k.vec_own[...] = jnp.concatenate([own_vec, jnp.zeros((4, 128), BF16)], axis=0)

    gathers.embed.start()
    to_all = [
        (k.vec_own, k.vec_all.at[n.z, n.y], n.device(z=n.partner(o), y=y))
        for o in range(4)
        for y in (n.y, 1 - n.y)
        if not (o == 0 and y is n.y)
    ]
    vec_copies = n.send_all(to_all, k.vec_room)
    second.start_own()
    vec_own = n.local(k.vec_own, k.vec_all.at[n.z, n.y])
    start_compute(k)
    steps_copy.wait()
    table_copy.wait()
    for m in range(count):
        row = k.table[pl.ds(k.steps[m], 1), :]
        k.pre[m : m + 1, :] = row
        k.extra[m : m + 1, 0:HALF] = row[:, 0:HALF]
        k.extra[m + 4 : m + 5, 0:HALF] = row[:, HALF:TEMB]
        when = jnp.full((1, EXTRA - HALF), k.steps[m].astype(F32), F32)
        k.extra[m : m + 1, HALF:EXTRA] = when
        k.extra[m + 4 : m + 5, HALF:EXTRA] = when
    extras = SmallGather(n, k.extra, k.extra_all)
    first.spread(1)
    second.start()
    for o in (2, 3):
        first.spread(o)
    vec_own.wait()
    x_copy.wait()
    vec_copies.wait()
    per_half = 2 * z_size // 2
    for half in range(2):
        total = k.vec_all[half * per_half // 2, 0].astype(F32)
        for i in range(half * per_half + 1, (half + 1) * per_half):
            total = total + k.vec_all[i // 2, i % 2].astype(F32)
        k.vec[:, half * 128 : (half + 1) * 128] = total
    gathers.embed.spread()
    gathers.mixed.start()
    gathers.out.start()
    extras.start()
    each_map(k, first_norm)
    first.share_own()
    for o in (1, 2, 3):
        first.share(o)
    second.spread(1, 2, 3)
    first.finish()
    k.w_first = k.full_first.reshape(TAPS, WIDTH)
    k.w_second = k.full_second.reshape(TAPS, WIDTH)
    k.w_embed = k.full_embed.reshape(TEMB, WIDTH)
    k.w_mixed = k.full_mixed.reshape(WIDTH, 3 * WIDTH)
    k.w_out = k.full_out.reshape(WIDTH, WIDTH)
    each_map(k, first_conv)
    for gather in (gathers.mixed, gathers.out):
        gather.spread()
    gathers.embed.share()
    second.share_own()
    second.share(1)
    gathers.embed.finish()
    embed(k, k.pre[...])
    each_map(k, second_norm)
    second.share(2)
    second.share(3)
    second.finish()
    each_map(k, second_conv)
    gathers.mixed.share()
    gathers.out.share()
    extras.spread()
    each_map(k, third_norm)
    cot_copy.wait()
    gathers.mixed.finish()
    gathers.out.finish()
    each_map(k, *ATTENTION[1:])

    reduces = SimpleNamespace()
    for name in EARLY:
        bufs = [getattr(k, f"reduce_{name}_{i}") for i in range(7)]
        setattr(reduces, name, Reduce(n, BOXES[name], EARLY[name], getattr(k, "grad_" + name), bufs))
    g_out = k.grad_out.reshape(WIDTH, WIDTH)
    g_mixed = k.grad_mixed.reshape(WIDTH, 3 * WIDTH)
    g_second = k.grad_second.reshape(TAPS, WIDTH)
    g_first = k.grad_first.reshape(TAPS, WIDTH)
    small = [reduces.out, reduces.mixed]
    first, second = reduces.first, reduces.second
    g_out[...] = dot(k.att_t[...], k.cot[...]).astype(BF16)
    g_mixed[...] = dot(k.nrm_t[...], k.g_mixed[...]).astype(BF16)
    for r in small:
        r.start()
    each_map(k, third_norm_back)
    for r in small:
        r.pair()
    extras.share()
    grad_and_start(k, n, k.a2_t, g_second, second)
    second.pair(0)
    second.pair(1)
    each_map(k, second_conv_back)
    second.pair(2)
    second.pair(3)
    each_map(k, second_norm_back)
    sends = SmallGather(n, k.g_proj, k.g_proj_all)
    sends.start()
    for r in small:
        r.middle_late()
    grad_and_start(k, n, k.a1_t, g_first, first)
    first.pair(0)
    first.pair(1)
    each_map(k, first_conv_back, first_norm_back)
    first.pair(2)
    first.pair(3)
    sums = SmallSum(n, k.sums, k.sums_land)
    sums.exchange(0, [n.core_peer])
    if second.early:
        second.middle_early()
    for o in range(4):
        second.middle_late(o)
    sums.add()
    sums.exchange(1, [n.device(z=n.partner(o)) for o in (1, 2, 3)])
    for r in small:
        r.owner()
    sends.spread()
    for o in (0, 1):
        first.middle_late(o)
    if first.early:
        first.middle_early()
    for o in (2, 3):
        first.middle_late(o)
    second.owner()
    sums.add()
    sums.exchange(4, [n.x_peer, n.y_peer, n.device(x=1 - n.x, y=1 - n.y)])
    first.owner()
    sends.share()
    sends.finish()
    extras.finish()

    devices = 4 * 2 * z_size
    g_proj = k.g_proj_all[...].reshape(devices * 8, WIDTH)
    upper = lax.broadcasted_iota(jnp.int32, (devices * 8, 1), 0) % 8 < 4
    extra = k.extra_all[...].reshape(devices * 8, EXTRA)
    pre = extra[:, 0:HALF]
    sig = jax.nn.sigmoid(pre)
    e = pre * sig
    e_t = e.astype(BF16).T
    k.g_embed_all[0:HALF, :] = dot(e_t, jnp.where(upper, g_proj, 0.0).astype(BF16))
    k.g_embed_all[HALF:TEMB, :] = dot(e_t, jnp.where(upper, 0.0, g_proj).astype(BF16))
    g_e = dot_nt(g_proj.astype(BF16), k.w_embed[...])
    g_e = jnp.where(upper, g_e[:, 0:HALF], g_e[:, HALF:TEMB])
    k.g_pre[...] = g_e * (sig + e * (1.0 - sig))
    k.when[...] = extra[:, HALF:EXTRA].T[0:8, :]
    rows = TEMB // (2 * z_size)
    k.embed[...] = k.g_embed_all[pl.ds(pl.multiple_of(n.f * rows, rows), rows), :]
    sums.add()
    k.sums_total[...] = k.sums[...]
    reduces.out.finish(k.out_total)
    reduces.mixed.finish(k.mixed_total)
    second.finish(k.second_total)
    first.finish(k.first_total)
    n.finish()


def finish_kernel(names, *refs):
    k = Refs(names, refs, 1, 1)
    stores = []

    def store(src, dst):
        copy = pltpu.make_async_copy(src, dst, k.sems.at[len(stores)])
        copy.start()
        stores.append(copy)

    store(k.out_done, k.out_final)
    store(k.image_grad_done, k.image_final)
    high, mid, low = split3(k.g_pre_done[...])
    when = k.when_done[0:1, :]
    steps = k.table.shape[0]
    chunk = 256
    for begin in range(0, steps, chunk):
        size = min(chunk, steps - begin)
        t = lax.broadcasted_iota(jnp.int32, (size, when.shape[1]), 0).astype(F32) + begin
        hit = t == when
        upper = lax.broadcasted_iota(jnp.int32, hit.shape, 1) % 8 < 4
        block = slice(begin, begin + size)
        for half, rows in enumerate((upper, jnp.logical_not(upper))):
            selector = jnp.where(jnp.logical_and(hit, rows), 1.0, 0.0).astype(BF16)
            k.table[block, half * HALF : (half + 1) * HALF] = (
                dot(selector, high) + dot(selector, mid) + dot(selector, low)
            )
        store(k.table.at[block, :], k.table_grad.at[block, :])
    store(k.embed_done, k.embed_grad)
    for total, wide, out in (
        (k.out_total_done, k.out_wide, k.out_total_grad),
        (k.mixed_total_done, k.mixed_wide, k.mixed_total_grad),
        (k.second_total_done, k.second_wide, k.second_total_grad),
        (k.first_total_done, k.first_wide, k.first_total_grad),
    ):
        wide[...] = total[...].astype(F32)
        store(wide, out)
    width = k.vec_grad.shape[1]
    shift = lax.rem(WIDTH - lax.axis_index(FSDP) * width, WIDTH)
    k.vec_wide[...] = pltpu.roll(k.sums_total_done[...], shift, 1)[0 : k.vec_grad.shape[0], 0:width]
    store(k.vec_wide, k.vec_grad)
    for copy in stores:
        copy.wait()


def fused(image, timesteps, time_table, conv_first, embed_weight, conv_second, qkv_weight, out_weight, vectors, cotangent):
    count, side = image.shape[:2]
    total = count * side * side
    z_size = lax.axis_size(FSDP) // 2
    slots = 4 * 2 * z_size * 8
    inputs = dict(
        x_in=image.reshape(total, WIDTH),
        cot_in=cotangent.reshape(total, WIDTH),
        steps_in=timesteps,
        time_table=time_table,
        shard_first=conv_first,
        shard_embed=embed_weight,
        shard_second=conv_second,
        shard_mixed=qkv_weight,
        shard_out=out_weight,
        vectors_in=vectors,
    )
    between = dict(
        g_pre=((slots, HALF), F32),
        when=((8, slots), F32),
        out=((total, WIDTH), BF16),
        image_grad=((total, WIDTH), BF16),
        embed=(embed_weight.shape, F32),
        out_total=(out_weight.shape, BF16),
        mixed_total=(qkv_weight.shape, BF16),
        second_total=(conv_second.shape, BF16),
        first_total=(conv_first.shape, BF16),
        sums_total=((16, WIDTH), F32),
    )
    scratch = scratch_of(count, side)
    for name in ("x", "cot"):
        scratch[name] = ((total, WIDTH), BF16)
    for name, box in BOXES.items():
        scratch["full_" + name] = ((z_size, 2, box.rows, box.lanes), BF16)
    for name in EARLY:
        box = BOXES[name]
        scratch["grad_" + name] = ((z_size, 2, box.rows, box.lanes), BF16)
        for i, buf in enumerate(Reduce.buffers(box, EARLY[name], z_size)):
            scratch[f"reduce_{name}_{i}"] = buf
    scratch.update(vectors=(vectors.shape, BF16))
    scratch.update(table=(time_table.shape, F32))
    scratch.update(pre=((8, TEMB), F32))
    scratch.update(extra=((8, EXTRA), F32))
    scratch.update(extra_all=((z_size, 2, 2, 2, 8, EXTRA), F32))
    scratch.update(g_proj_all=((z_size, 2, 2, 2, 8, WIDTH), F32))
    scratch.update(g_embed_all=((TEMB, WIDTH), F32))
    scratch.update(vec_own=((16, 128), BF16))
    scratch.update(vec_room=((2 * z_size - 1, 16, 128), BF16))
    scratch.update(vec_all=((z_size, 2, 16, 128), BF16))
    scratch.update(vec=((16, WIDTH), F32))
    scratch.update(sums_land=((7, 16, WIDTH), F32))
    sems = dict(send_sems=SENDS, recv_sems=LANDINGS, local_sems=13)
    names = list(inputs) + list(between) + list(scratch) + list(sems) + ["steps"]
    anywhere = pl.BlockSpec(memory_space=pl.ANY)
    results = pl.pallas_call(
        functools.partial(whole_kernel, names, count, side, z_size),
        out_shape=[pltpu.VMEM(*v) for v in between.values()],
        in_specs=[anywhere] * len(inputs),
        out_specs=[pl.BlockSpec(memory_space=pltpu.VMEM)] * len(between),
        scratch_shapes=[pltpu.VMEM(*v) for v in scratch.values()]
        + [pltpu.SemaphoreType.DMA((size,)) for size in sems.values()]
        + [pltpu.SMEM(timesteps.shape, jnp.int32)],
        compiler_params=pltpu.CompilerParams(
            collective_id=0, has_side_effects=True, vmem_limit_bytes=VMEM_BYTES
        ),
        name="block",
    )(*inputs.values())

    outputs = dict(
        out_final=((total, WIDTH), BF16),
        image_final=((total, WIDTH), BF16),
        table_grad=(time_table.shape, F32),
        first_total_grad=(conv_first.shape, F32),
        embed_grad=(embed_weight.shape, F32),
        second_total_grad=(conv_second.shape, F32),
        mixed_total_grad=(qkv_weight.shape, F32),
        out_total_grad=(out_weight.shape, F32),
        vec_grad=(vectors.shape, F32),
    )
    scratch = dict(
        table=(time_table.shape, F32),
        vec_wide=(vectors.shape, F32),
        out_wide=(out_weight.shape, F32),
        mixed_wide=(qkv_weight.shape, F32),
        second_wide=(conv_second.shape, F32),
        first_wide=(conv_first.shape, F32),
    )
    names = [name + "_done" for name in between] + list(outputs) + list(scratch) + ["sems"]
    results = pl.pallas_call(
        functools.partial(finish_kernel, names),
        out_shape=[jax.ShapeDtypeStruct(*v) for v in outputs.values()],
        in_specs=[pl.BlockSpec(memory_space=pltpu.VMEM)] * len(between),
        out_specs=[anywhere] * len(outputs),
        scratch_shapes=[pltpu.VMEM(*v) for v in scratch.values()]
        + [pltpu.SemaphoreType.DMA((16,))],
        compiler_params=pltpu.CompilerParams(vmem_limit_bytes=VMEM_BYTES),
        name="finish",
    )(*[pltpu.with_memory_space_constraint(r, pltpu.VMEM) for r in results])
    out, image_grad, *rest = results
    return (out.reshape(image.shape), image_grad.reshape(image.shape), *rest)


def local_kernel(names, count, side, *refs):
    k = Refs(names, refs, count, side)
    start_compute(k)
    embed(k, k.pre[...])
    each_map(k, first_norm, first_conv, second_norm, second_conv, *ATTENTION)
    k.grad_out[...] = dot(k.att_t[...], k.cot[...]).astype(BF16)
    k.grad_mixed[...] = dot(k.nrm_t[...], k.g_mixed[...]).astype(BF16)
    each_map(k, third_norm_back)
    for ky in range(3):
        kernel_grad(k, k.a2_t, k.grad_second, ky)
    each_map(k, second_conv_back, second_norm_back)
    for ky in range(3):
        kernel_grad(k, k.a1_t, k.grad_first, ky)
    each_map(k, first_conv_back, first_norm_back)
    k.vec_grad[...] = k.sums[...]
    k.g_proj_out[...] = k.g_proj[...]


def plain(image, timesteps, time_table, conv_first, embed_weight, conv_second, qkv_weight, out_weight, vectors, cotangent):
    count, side = image.shape[:2]
    total = count * side * side

    def whole(w, axis=0):
        return lax.all_gather(w, FSDP, axis=axis, tiled=True)

    pre = time_table[timesteps]
    w_embed = whole(embed_weight)
    inputs = dict(
        x=image.reshape(total, WIDTH),
        cot=cotangent.reshape(total, WIDTH),
        w_first=whole(conv_first),
        w_embed=w_embed,
        w_second=whole(conv_second),
        w_mixed=whole(qkv_weight),
        w_out=whole(out_weight),
        vec=jnp.pad(whole(vectors, 1).astype(F32), ((0, 4), (0, 0))),
        pre=jnp.pad(pre, ((0, 8 - count), (0, 0))),
    )
    outputs = dict(
        out=((total, WIDTH), BF16),
        image_grad=((total, WIDTH), BF16),
        grad_first=((TAPS, WIDTH), BF16),
        grad_second=((TAPS, WIDTH), BF16),
        grad_mixed=((WIDTH, 3 * WIDTH), BF16),
        grad_out=((WIDTH, WIDTH), BF16),
        vec_grad=((16, WIDTH), F32),
        g_proj_out=((8, WIDTH), F32),
    )
    scratch = scratch_of(count, side)
    names = list(inputs) + list(outputs) + list(scratch)
    vmem = pl.BlockSpec(memory_space=pltpu.VMEM)
    results = pl.pallas_call(
        functools.partial(local_kernel, names, count, side),
        out_shape=[jax.ShapeDtypeStruct(*v) for v in outputs.values()],
        in_specs=[vmem] * len(inputs),
        out_specs=[vmem] * len(outputs),
        scratch_shapes=[pltpu.VMEM(*v) for v in scratch.values()],
        compiler_params=pltpu.CompilerParams(vmem_limit_bytes=VMEM_BYTES),
        name="block_alone",
    )(*inputs.values())
    out, image_grad, g_first, g_second, g_mixed, g_out, g_vec, g_proj = results
    g_proj = g_proj[:count].astype(BF16)

    def owned(g, axis=0):
        own = lax.psum_scatter(g.astype(BF16), FSDP, scatter_dimension=axis, tiled=True)
        return lax.psum(own, DP).astype(F32)

    e = (pre * jax.nn.sigmoid(pre)).astype(BF16)
    g_embed = lax.dot_general(e, g_proj, TN, preferred_element_type=F32)
    sig = jax.nn.sigmoid(pre)
    g_pre = dot_nt(g_proj, w_embed) * (sig * (1.0 + pre * (1.0 - sig)))
    rows = lax.all_gather(g_pre, (FSDP, DP), axis=0, tiled=True)
    where = lax.all_gather(timesteps, (FSDP, DP), axis=0, tiled=True)
    table_grad = jnp.zeros(time_table.shape, F32).at[where].add(rows)
    return (
        out.reshape(image.shape),
        image_grad.reshape(image.shape),
        table_grad,
        owned(g_first),
        owned(g_embed),
        owned(g_second),
        owned(g_mixed),
        owned(g_out),
        owned(g_vec[: vectors.shape[0]], 1),
    )


def solution(mesh):
    placed = (
        P((FSDP, DP), None, None, None),
        P((FSDP, DP)),
        P(),
        P(FSDP, None),
        P(FSDP, None),
        P(FSDP, None),
        P(FSDP, None),
        P(FSDP, None),
        P(None, FSDP),
        P((FSDP, DP), None, None, None),
    )
    grid = (mesh.shape[FSDP], mesh.shape[DP])
    return jax.shard_map(
        fused if grid == (8, 4) else plain,
        mesh=mesh,
        in_specs=placed,
        out_specs=(
            P((FSDP, DP), None, None, None),
            P((FSDP, DP), None, None, None),
            P(),
            P(FSDP, None),
            P(FSDP, None),
            P(FSDP, None),
            P(FSDP, None),
            P(FSDP, None),
            P(None, FSDP),
        ),
        check_vma=False,
    )
```

```python
import functools
from types import SimpleNamespace

import jax
import jax.numpy as jnp
from jax import lax
from jax.experimental import pallas as pl
from jax.experimental.pallas import tpu as pltpu
from jax.sharding import PartitionSpec as P

FSDP, DP = "fsdp", "dp"
F32 = jnp.float32
BF16 = jnp.bfloat16
MESH = pl.DeviceIdType.MESH
EPS = 1e-06
WIDTH = 256
GROUP = 8
TEMB = 512
TAPS = 9 * WIDTH
HALF = TEMB // 2
EXTRA = HALF + 128
VMEM_BYTES = 56 * 2**20
NT = (((1,), (1,)), ((), ()))
TN = (((0,), (0,)), ((), ()))


def dot(a, b):
    return jnp.dot(a, b, preferred_element_type=F32)


def dot_nt(a, b):
    return lax.dot_general(a, b, NT, preferred_element_type=F32)


def split3(v):
    high = v.astype(BF16)
    rest = v - high.astype(F32)
    mid = rest.astype(BF16)
    return high, mid, (rest - mid.astype(F32)).astype(BF16)


def colsum(v):
    return jnp.sum(v, axis=0, keepdims=True)


def group_mean(row, averager):
    high, mid, low = split3(row)
    return dot(high, averager) + dot(mid, averager) + dot(low, averager)


class Refs:
    def __init__(self, names, refs, count, side):
        for name, ref in zip(names, refs):
            setattr(self, name, ref)
        self.count, self.side, self.places = count, side, side * side

    def rows(self, m):
        return pl.ds(m * self.places, self.places)


def scratch_of(count, side):
    places = side * side
    total = count * places
    padded = places + 2 * side
    return dict(
        averager=((WIDTH, WIDTH), BF16),
        shifted_a=((count, padded, 3 * WIDTH), BF16),
        shifted_g=((count, padded, 3 * WIDTH), BF16),
        unit1=((total, WIDTH), F32),
        slope1=((total, WIDTH), F32),
        inv1=((count, 1, WIDTH), F32),
        unit2=((total, WIDTH), F32),
        slope2=((total, WIDTH), F32),
        inv2=((count, 1, WIDTH), F32),
        unit3=((total, WIDTH), F32),
        inv3=((count, 1, WIDTH), F32),
        a1_t=((WIDTH, total), BF16),
        a2_t=((WIDTH, total), BF16),
        nrm_t=((WIDTH, total), BF16),
        att_t=((WIDTH, total), BF16),
        nrm=((total, WIDTH), BF16),
        mixed=((total, 3 * WIDTH), BF16),
        g_att=((total, WIDTH), BF16),
        probs=((total, places), F32),
        probs_low=((total, places), BF16),
        probs_t=((places, total), BF16),
        att=((total, WIDTH), BF16),
        g_probs=((total, places), F32),
        g_scores=((total, places), BF16),
        g_scores_t=((places, total), BF16),
        conv_out=((total, WIDTH), F32),
        resid=((total, WIDTH), F32),
        g_mixed=((total, 3 * WIDTH), BF16),
        proj=((8, WIDTH), F32),
        sums=((16, WIDTH), F32),
        g_proj=((8, WIDTH), F32),
    )


def start_compute(k):
    rows = lax.broadcasted_iota(jnp.int32, (WIDTH, WIDTH), 0) // GROUP
    cols = lax.broadcasted_iota(jnp.int32, (WIDTH, WIDTH), 1) // GROUP
    k.averager[...] = jnp.where(rows == cols, 1.0 / (k.places * GROUP), 0.0).astype(BF16)
    edge = jnp.zeros((k.count, k.side, 3 * WIDTH), BF16)
    for ref in (k.shifted_a, k.shifted_g):
        ref[:, 0 : k.side, :] = edge
        ref[:, k.places + k.side : k.places + 2 * k.side, :] = edge
    k.sums[...] = jnp.zeros(k.sums.shape, F32)
    k.g_proj[...] = jnp.zeros(k.g_proj.shape, F32)


def store_shifted(k, ref, m, a):
    column = lax.broadcasted_iota(jnp.int32, a.shape, 0) % k.side
    inner = slice(k.side, k.side + k.places)
    left = jnp.where(column == 0, 0.0, pltpu.roll(a, 1, 0))
    right = jnp.where(column == k.side - 1, 0.0, pltpu.roll(a, k.places - 1, 0))
    ref[m, inner, 0:WIDTH] = left.astype(BF16)
    ref[m, inner, WIDTH : 2 * WIDTH] = a.astype(BF16)
    ref[m, inner, 2 * WIDTH : 3 * WIDTH] = right.astype(BF16)


def normalize(k, u):
    averager = k.averager[...]
    centered = u - group_mean(colsum(u), averager)
    inverse = lax.rsqrt(group_mean(colsum(centered * centered), averager) + EPS)
    return centered * inverse, inverse


def norm_swish(k, u, m, j, unit_ref, slope_ref, inv_ref):
    unit, inverse = normalize(k, u)
    unit_ref[k.rows(m), :] = unit
    inv_ref[m] = inverse
    h = unit * (1.0 + k.vec[j : j + 1, :]) + k.vec[j + 1 : j + 2, :]
    sig = jax.nn.sigmoid(h)
    a = h * sig
    slope_ref[k.rows(m), :] = sig + a * (1.0 - sig)
    return a


def norm_back(k, upstream, unit, inverse, j):
    averager = k.averager[...]
    g_gain = colsum(upstream * unit)
    g_shift = colsum(upstream)
    k.sums[j : j + 1, :] += g_gain
    k.sums[j + 1 : j + 2, :] += g_shift
    gain = 1.0 + k.vec[j : j + 1, :]
    first = group_mean(g_shift * gain, averager)
    second = group_mean(g_gain * gain, averager)
    return inverse * (upstream * gain - first - unit * second)


def convolve(k, ref, w, m):
    total = None
    for ky in range(3):
        window = ref[m, ky * k.side : ky * k.side + k.places, :]
        term = dot(window, w[ky * 3 * WIDTH : (ky + 1) * 3 * WIDTH, :])
        total = term if total is None else total + term
    return total


def convolve_back(k, ref, w, m):
    total = None
    for ky in range(3):
        for kx in range(3):
            window = ref[
                m,
                (2 - ky) * k.side : (2 - ky) * k.side + k.places,
                (2 - kx) * WIDTH : (3 - kx) * WIDTH,
            ]
            tap = 3 * ky + kx
            term = dot_nt(window, w[tap * WIDTH : (tap + 1) * WIDTH, :])
            total = term if total is None else total + term
    return total


def kernel_grad(k, a_t, g_w, ky):
    start = (2 - ky) * k.side
    row = ky * 3 * WIDTH
    if not isinstance(ky, int):
        start, row = pl.multiple_of(start, k.side), pl.multiple_of(row, WIDTH)
    window = k.shifted_g[:, pl.ds(start, k.places), :]
    term = dot(a_t[...], window.reshape(k.count * k.places, 3 * WIDTH))
    for kx in range(3):
        g_w[pl.ds(row + kx * WIDTH, WIDTH), :] = term[
            :, (2 - kx) * WIDTH : (3 - kx) * WIDTH
        ].astype(BF16)


def first_norm(k, m):
    a = norm_swish(k, k.x[k.rows(m), :].astype(F32), m, 0, k.unit1, k.slope1, k.inv1)
    store_shifted(k, k.shifted_a, m, a)
    k.a1_t[:, k.rows(m)] = a.astype(BF16).T


def embed(k, pre):
    e = (pre * jax.nn.sigmoid(pre)).astype(BF16)
    k.proj[...] = dot(e, k.w_embed[...]) + k.vec[3:4, :]


def first_conv(k, m):
    k.conv_out[k.rows(m), :] = convolve(k, k.shifted_a, k.w_first, m)


def second_norm(k, m):
    h1 = k.conv_out[k.rows(m), :] + (k.vec[2:3, :] + k.proj[m : m + 1, :])
    a = norm_swish(k, h1, m, 4, k.unit2, k.slope2, k.inv2)
    store_shifted(k, k.shifted_a, m, a)
    k.a2_t[:, k.rows(m)] = a.astype(BF16).T


def second_conv(k, m):
    x = k.x[k.rows(m), :].astype(F32)
    k.resid[k.rows(m), :] = x + convolve(k, k.shifted_a, k.w_second, m) + k.vec[6:7, :]


def third_norm(k, m):
    rows = k.rows(m)
    unit, inverse = normalize(k, k.resid[rows, :])
    k.unit3[rows, :] = unit
    k.inv3[m] = inverse
    nrm = (unit * (1.0 + k.vec[7:8, :]) + k.vec[8:9, :]).astype(BF16)
    k.nrm[rows, :] = nrm
    k.nrm_t[:, rows] = nrm.T


def project(k, m):
    rows = k.rows(m)
    mixed = dot(k.nrm[rows, :], k.w_mixed[...])
    k.mixed[rows, 0:WIDTH] = (mixed[:, :WIDTH] + k.vec[9:10, :]).astype(BF16)
    k.mixed[rows, WIDTH : 2 * WIDTH] = mixed[:, WIDTH : 2 * WIDTH].astype(BF16)
    k.mixed[rows, 2 * WIDTH :] = (mixed[:, 2 * WIDTH :] + k.vec[10:11, :]).astype(BF16)


def upstream(k, m):
    cot = k.cot[k.rows(m), :]
    k.sums[11:12, :] += colsum(cot.astype(F32))
    k.g_att[k.rows(m), :] = dot_nt(cot, k.w_out[...]).astype(BF16)


def softmax(k, m):
    rows = k.rows(m)
    scores = dot_nt(k.mixed[rows, 0:WIDTH], k.mixed[rows, WIDTH : 2 * WIDTH]) * WIDTH**-0.5
    raised = jnp.exp(scores - jnp.max(scores, axis=1, keepdims=True))
    probs = raised * (1.0 / jnp.sum(raised, axis=1, keepdims=True))
    k.probs[rows, :] = probs
    low = probs.astype(BF16)
    k.probs_low[rows, :] = low
    k.probs_t[:, rows] = low.T


def attend(k, m):
    rows = k.rows(m)
    value = k.mixed[rows, 2 * WIDTH :]
    att = dot(k.probs_low[rows, :], value).astype(BF16)
    k.att[rows, :] = att
    k.att_t[:, rows] = att.T
    k.g_probs[rows, :] = dot_nt(k.g_att[rows, :], value)


def emit(k, m):
    rows = k.rows(m)
    branch = dot(k.att[rows, :], k.w_out[...])
    k.out[rows, :] = (k.resid[rows, :] + branch + k.vec[11:12, :]).astype(BF16)


def softmax_back(k, m):
    rows = k.rows(m)
    probs, g_probs = k.probs[rows, :], k.g_probs[rows, :]
    weighted = jnp.sum(probs * g_probs, axis=1, keepdims=True)
    g_scores = (probs * (g_probs - weighted)).astype(BF16)
    k.g_scores[rows, :] = g_scores
    k.g_scores_t[:, rows] = g_scores.T
    g_value = dot(k.probs_t[:, rows], k.g_att[rows, :]).astype(BF16)
    k.sums[10:11, :] += colsum(g_value.astype(F32))
    k.g_mixed[rows, 2 * WIDTH :] = g_value


def project_back(k, m):
    rows = k.rows(m)
    scale = WIDTH**-0.5
    g_query = (dot(k.g_scores[rows, :], k.mixed[rows, WIDTH : 2 * WIDTH]) * scale).astype(BF16)
    g_key = (dot(k.g_scores_t[:, rows], k.mixed[rows, 0:WIDTH]) * scale).astype(BF16)
    k.sums[9:10, :] += colsum(g_query.astype(F32))
    k.g_mixed[rows, 0:WIDTH] = g_query
    k.g_mixed[rows, WIDTH : 2 * WIDTH] = g_key


ATTENTION = (third_norm, project, upstream, softmax, attend, emit, softmax_back, project_back)


def third_norm_back(k, m):
    rows = k.rows(m)
    g_nrm = dot_nt(k.g_mixed[rows, :], k.w_mixed[...])
    g_resid = k.cot[rows, :].astype(F32) + norm_back(
        k, g_nrm, k.unit3[rows, :], k.inv3[m], 7
    )
    k.resid[rows, :] = g_resid
    g_conv = g_resid.astype(BF16).astype(F32)
    k.sums[6:7, :] += colsum(g_conv)
    store_shifted(k, k.shifted_g, m, g_conv)


def second_conv_back(k, m):
    rows = k.rows(m)
    k.conv_out[rows, :] = convolve_back(k, k.shifted_g, k.w_second, m) * k.slope2[rows, :]


def second_norm_back(k, m):
    rows = k.rows(m)
    g_h1 = norm_back(k, k.conv_out[rows, :], k.unit2[rows, :], k.inv2[m], 4)
    g_h1 = g_h1.astype(BF16).astype(F32)
    per_map = colsum(g_h1)
    k.sums[2:3, :] += per_map
    g_proj = per_map.astype(BF16).astype(F32)
    k.sums[3:4, :] += g_proj
    k.g_proj[m : m + 1, :] = g_proj
    k.g_proj[m + 4 : m + 5, :] = g_proj
    store_shifted(k, k.shifted_g, m, g_h1)


def first_conv_back(k, m):
    rows = k.rows(m)
    k.conv_out[rows, :] = convolve_back(k, k.shifted_g, k.w_first, m) * k.slope1[rows, :]


def first_norm_back(k, m):
    rows = k.rows(m)
    g_x = norm_back(k, k.conv_out[rows, :], k.unit1[rows, :], k.inv1[m], 0)
    k.image_grad[rows, :] = (k.resid[rows, :] + g_x).astype(BF16)


def each_map(k, *steps):
    for step in steps:
        for m in range(k.count):
            step(k, m)


class Links:
    def __init__(self, send_sems, recv_sems, local_sems):
        f, d = lax.axis_index(FSDP), lax.axis_index(DP)
        self.f = f
        self.z, self.y, self.x, self.c = f // 2, f % 2, d // 2, d % 2
        self.send_sems, self.recv_sems, self.local_sems = send_sems, recv_sems, local_sems
        self.n_local = 0
        self.core = None
        self.pools = {None: [], 0: [], 1: []}
        self.left = set()
        self.n_landings = {None: 0, 0: 0, 1: 0}
        z, y, x, c = self.z, self.y, self.x, self.c
        self.partners = (z, z + 1 - 2 * (z % 2), (z + 2) % 4, 3 - z)
        upper = z // 2
        self.upper = upper
        self.turns = ((1 - upper) * 3, 2 - upper, self.partners[1], z)
        self.slots = [lax.rem(z + t, 2) + 2 * lax.rem(upper + t // 2, 2) - 1 for t in self.turns[:3]]
        self.other_y, self.other_x = 1 - y, 1 - x
        here, over = (x * 2 + c), (1 - x) * 2 + c
        self.at_z = [(p * 2 + y, here) for p in self.partners]
        self.at_turn = [(p * 2 + y, here) for p in self.turns]
        self.across_z = [(p * 2 + 1 - y, here) for p in self.partners]
        self.x_peer, self.y_peer = (f, over), (z * 2 + 1 - y, here)
        self.diagonal = (z * 2 + 1 - y, over)
        self.core_peer, self.x_core_peer = (f, x * 2 + 1 - c), (f, (1 - x) * 2 + 1 - c)

    def on_core(self, core, *steps):
        def run():
            self.core = core
            for step in steps:
                step()
            self.core = None

        pl.when(self.c == core)(run)

    def landing(self, core=None):
        spot = self.n_landings[core]
        self.n_landings[core] += 1
        return spot if core is None else LANDINGS + spot

    def send(self, route, landing=None):
        core = self.core
        pool = self.pools[core]
        spot = len(pool)
        if spot >= SENDS:
            self.sent(pool[spot - SENDS])
        if landing is None:
            landing = self.landing(core)
        send_sem = spot % SENDS + (0 if core is None else SENDS)

        def copy():
            src, dst, device = route()
            return pltpu.make_async_remote_copy(
                src_ref=src,
                dst_ref=dst,
                send_sem=self.send_sems.at[send_sem],
                recv_sem=self.recv_sems.at[landing],
                device_id=device,
                device_id_type=MESH,
            )

        copy().start()
        pool.append(copy)
        return lambda: copy().wait_recv()

    def send_all(self, routes, room, landing=None):
        if landing is None:
            landing = self.landing(self.core)
        for route in routes:
            self.send(route, landing)
        return self.arrival(landing, room)

    def arrival(self, landing, room):
        def wait():
            block = room()
            pltpu.make_async_copy(block, block, self.recv_sems.at[landing]).wait()

        return wait

    def sent(self, copy):
        if id(copy) not in self.left:
            copy().wait_send()
            self.left.add(id(copy))

    def local(self, src, dst):
        copy = pltpu.make_async_copy(src, dst, self.local_sems.at[self.n_local])
        self.n_local += 1
        copy.start()
        return copy

    def keep(self, route):
        spot = self.n_local
        self.n_local += 1

        def copy():
            return pltpu.make_async_copy(*route(), self.local_sems.at[spot])

        copy().start()
        return lambda: copy().wait()

    def finish(self):
        for core in (0, 1):
            self.on_core(core, *[functools.partial(self.sent, copy) for copy in self.pools[core]])
        for copy in self.pools[None]:
            self.sent(copy)

    def greet(self):
        barrier = pltpu.get_barrier_semaphore()
        peers = self.at_z[1:] + self.across_z
        peers += [self.x_peer, self.core_peer, self.x_core_peer, self.diagonal]
        for peer in peers:
            pl.semaphore_signal(barrier, inc=1, device_id=peer, device_id_type=MESH)
        return lambda: pl.semaphore_wait(barrier, len(peers))


class Box:
    def __init__(self, core, first, rows, lanes):
        self.core, self.rows, self.lanes, self.half = core, rows, lanes, lanes // 2
        self.span = slice(first, first + rows)

    def lanes_of(self, x):
        return pl.ds(pl.multiple_of(x * self.half, 128), self.half)


class Gather:
    def __init__(self, links, box, shard, full, parts=False):
        self.n, self.box, self.shard, self.full = links, box, shard, full
        self.by_parts = parts
        self.mine = box.lanes_of(links.x)
        self.sides = {}
        self.shares = {}

    def start(self):
        n = self.n

        def route(o):
            return lambda: (
                self.shard.at[self.box.span, self.mine],
                self.full.at[n.z, n.y, self.box.span, self.mine],
                n.at_z[o],
            )

        if self.by_parts:
            self.z_arrivals = {o: n.send(route(o)) for o in (1, 2, 3)}
        else:
            self.z_arrivals = {None: n.send_all([route(o) for o in (1, 2, 3)], self.room(1))}
            self.own = n.keep(
                lambda: (self.shard.at[self.box.span, self.mine], self.full.at[n.z, n.y, self.box.span, self.mine])
            )

    def room(self, o):
        rows = slice(0, self.box.rows)
        if o is None:
            return lambda: self.full.at[0:3, :, rows, :]
        return lambda: self.full.at[0:3, 0, rows, 0 : self.box.half]

    def start_own(self):
        n = self.n
        self.own_y = n.send(
            lambda: (
                self.shard.at[self.box.span, :],
                self.full.at[n.z, n.y, self.box.span, :],
                n.y_peer,
            )
        )

    def spot(self, o):
        return slice(None) if o is None else self.n.partners[o]

    def spread(self, *parts):
        n = self.n

        def route(o, peer):
            def block():
                return self.full.at[self.spot(o), n.y, self.box.span, self.mine]

            return lambda: (block(), block(), peer)

        for o in parts or (None,):
            self.z_arrivals[o]()
            if o is None:
                self.own()
            routes = [route(o, peer) for peer in (n.x_peer, n.y_peer, n.diagonal)]
            self.sides[o] = n.send_all(routes, self.room(o))

    def share(self, *parts):
        n = self.n

        def route(o):
            def block():
                return self.full.at[self.spot(o), :, self.box.span, :]

            return lambda: (block(), block(), n.core_peer)

        for o in parts or (None,):
            self.sides[o]()
            self.shares[o] = n.send(route(o), n.landing(1 - self.box.core))

    def share_own(self):
        n = self.n

        def block():
            return self.full.at[n.z, n.other_y, self.box.span, :]

        self.own_y()
        self.shares[0] = n.send(
            lambda: (block(), block(), n.core_peer), n.landing(1 - self.box.core)
        )

    def finish(self):
        self.n.on_core(1 - self.box.core, *self.shares.values())


class SmallGather:
    def __init__(self, links, block, full):
        self.n, self.block, self.full = links, block, full

    def start(self):
        n = self.n

        def route(device):
            return lambda: (self.block, self.full.at[n.z, n.y, n.x, n.c], device)

        routes = [route(n.at_z[o]) for o in (1, 2, 3)]
        self.z_arrivals = n.send_all(routes, lambda: self.full.at[0:3, 0, 0, 0])
        self.own = n.local(self.block, self.full.at[n.z, n.y, n.x, n.c])

    def spread(self):
        n = self.n

        def block():
            return self.full.at[:, n.y, n.x, n.c]

        def route(peer):
            return lambda: (block(), block(), peer)

        self.z_arrivals()
        self.own.wait()
        routes = [route(peer) for peer in (n.x_peer, n.y_peer, n.diagonal)]
        self.sides = n.send_all(routes, lambda: self.full.at[0:3, :, :, 0])

    def share(self):
        n = self.n

        def block():
            return self.full.at[:, :, :, n.c]

        self.sides()
        self.core = n.send(lambda: (block(), block(), n.core_peer))

    def finish(self):
        self.core()


class Reduce:
    def __init__(self, links, box, early, grad, total, bufs):
        self.n, self.box, self.early, self.grad, self.total = links, box, early, grad, total
        self.from_core, self.held, self.z_early, self.sides_early, self.sides_late, self.z_late = bufs
        self.core, self.sides = {}, {}
        n = links
        self.mine, self.others = box.lanes_of(n.x), box.lanes_of(n.other_x)
        self.around = (
            (n.other_y, self.others, n.diagonal),
            (n.other_y, self.mine, n.y_peer),
            (n.y, self.others, n.x_peer),
        )
        self.early_landing = n.landing(box.core) if early else None
        self.late_landing = n.landing(box.core) if early < box.rows else None

    @staticmethod
    def buffers(box, early, z):
        w, late = box.half, max(box.rows - early, 16)
        return [
            ((z, 2, box.rows, box.lanes), BF16),
            ((z, 2, box.rows, box.lanes), BF16),
            ((3, 2, max(early, 16), box.lanes), BF16),
            ((3, max(early, 16), w), BF16),
            ((3, z, late, w), BF16),
            ((3, late, w), BF16),
        ]

    def spot(self, o):
        return slice(None) if o is None else self.n.turns[o]

    def to_z(self, o):
        n = self.n
        if o is None:
            return [(n.partners[k], k - 1, n.at_z[k]) for k in (3, 2, 1)]
        return [] if o == 3 else [(n.turns[o], n.slots[o], n.at_turn[o])]

    def rows(self, late):
        return slice(self.early, self.box.rows) if late else slice(0, self.early)

    def start(self, *parts):
        n = self.n

        def route(p):
            return lambda: (
                self.grad.at[p, :, self.box.span, :],
                self.from_core.at[p],
                n.core_peer,
            )

        for o in parts or (None,):
            self.core[o] = n.send(route(self.spot(o)), n.landing(self.box.core))

    def early_route(self, z, slot, device):
        return lambda: (self.held.at[z, :, self.rows(False), :], self.z_early.at[slot], device)

    def late_route(self, z, slot, device):
        return lambda: (
            self.held.at[z, self.n.y, self.rows(True), self.mine],
            self.z_late.at[slot],
            device,
        )

    def side_route(self, p, late, i):
        y, lanes, peer = self.around[i]
        land = self.sides_late if late else self.sides_early
        return lambda: (
            self.held.at[p, y, self.rows(late), lanes],
            land.at[i, p] if late else land.at[i],
            peer,
        )

    def pair(self, *parts):
        n = self.n
        for o in parts or (None,):
            p = self.spot(o)
            self.core[o]()
            self.held[p] = self.grad[p, :, self.box.span, :] + self.from_core[p]
            if self.early:
                for z, slot, device in self.to_z(o):
                    n.send(self.early_route(z, slot, device), self.early_landing)
            if self.early < self.box.rows:
                part = slice(None) if o is None else 0
                self.sides[o] = n.send_all(
                    [self.side_route(p, True, i) for i in range(3)],
                    lambda: self.sides_late.at[:, part],
                )

    def middle_early(self):
        n = self.n
        if not self.early:
            return
        n.arrival(self.early_landing, lambda: self.z_early)()
        at = (n.z, slice(None), self.rows(False), slice(None))
        summed = self.held[at].astype(F32)
        for i in range(3):
            summed = summed + self.z_early[i].astype(F32)
        self.held[at] = summed.astype(BF16)
        self.early_sides = n.send_all(
            [self.side_route(n.z, False, i) for i in range(3)], lambda: self.sides_early
        )

    def middle_late(self, *parts):
        n = self.n
        for o in parts or (None,):
            p = self.spot(o)
            self.sides[o]()
            at = (p, n.y, self.rows(True), self.mine)
            summed = self.held[at].astype(F32)
            for i in range(3):
                summed = summed + self.sides_late[i, p].astype(F32)
            self.held[at] = summed.astype(BF16)
            for z, slot, device in self.to_z(o):
                n.send(self.late_route(z, slot, device), self.late_landing)

    def owner(self):
        n, box = self.n, self.box
        if self.early:
            self.early_sides()
        if self.early < box.rows:
            n.arrival(self.late_landing, lambda: self.z_late)()
        for late, lands in ((False, self.sides_early), (True, self.z_late)):
            rows = self.rows(late)
            if rows.start < rows.stop:
                summed = self.held[n.z, n.y, rows, self.mine].astype(F32)
                for i in range(3):
                    summed = summed + lands[i].astype(F32)
                first = box.span.start
                at = (slice(first + rows.start, first + rows.stop), self.mine)
                self.total[at] = summed.astype(BF16)

        def route(peer):
            def block():
                return self.total.at[box.span, self.mine]

            return lambda: (block(), block(), peer)

        self.replica = n.send(route(n.x_peer))
        self.replicas = n.send_all(
            [route(n.x_core_peer), route(n.core_peer)],
            lambda: self.total.at[box.span, :],
            n.landing(1 - box.core),
        )

    def finish(self):
        n = self.n
        n.on_core(self.box.core, self.replica)
        n.on_core(1 - self.box.core, self.replicas)


class SmallSum:
    def __init__(self, links, block, land):
        self.n, self.block, self.land = links, block, land

    def half(self, z):
        return pl.ds(pl.multiple_of(z // 2 * 128, 128), 128)

    def cores(self):
        n = self.n
        self.arrivals = n.send(lambda: (self.block, self.land.at[0], n.core_peer))
        self.copies = n.pools[None][-1:]

    def add_core(self):
        self.arrivals()
        total = self.block[...] + self.land[0]
        self.n.sent(self.copies[0])
        self.block[...] = total

    def exchange(self, first, lanes, peers):
        n = self.n

        def route(i):
            return lambda: (
                self.block.at[:, lanes[i]],
                self.land.at[first + i, :, 0:128],
                peers[i],
            )

        self.arrivals = n.send_all(
            [route(i) for i in range(3)], lambda: self.land.at[first : first + 3, :, 0:128]
        )
        self.copies = n.pools[None][-3:]

    def over_z(self):
        n = self.n
        self.exchange(1, [self.half(z) for z in n.partners[1:]], n.at_z[1:])

    def over_sides(self):
        n = self.n
        self.exchange(4, [self.half(n.z)] * 3, (n.x_peer, n.y_peer, n.diagonal))

    def add(self, first):
        self.arrivals()
        parts = [self.land[i, :, 0:128] for i in range(first, first + 3)]
        mine = self.half(self.n.z)
        total = (self.block[:, mine] + parts[0]) + (parts[1] + parts[2])
        for copy in self.copies:
            self.n.sent(copy)
        self.block[:, mine] = total


def on_both(n, *steps):
    for core in (0, 1):
        n.on_core(
            core,
            *[functools.partial(getattr(pair[core], step), *rest) for pair, step, *rest in steps],
        )


def grad_and_start(k, n, a_t, g_w, pair):
    for steps, ready in (((0, 1), (0, 1)), ((2,), (2, 3))):
        for step in steps:
            kernel_grad(k, a_t, g_w, (1 - n.upper) * (2 - step) + n.upper * step)
        on_both(n, (pair[::-1], "start", *ready))


SHARDS = dict(
    first=(288, 256, 128),
    embed=(64, 256, 32),
    second=(288, 256, 128),
    mixed=(32, 768, 16),
    out=(32, 256, 16),
)
BOXES = {
    name: (Box(0, 0, cut, lanes), Box(1, cut, rows - cut, lanes))
    for name, (rows, lanes, cut) in SHARDS.items()
}
EARLY = dict(first=(32, 48), second=(32, 32), mixed=(0, 0), out=(0, 0))
SENDS = 24
LANDINGS = 10
CORE_LANDINGS = 67
LOCALS = 16


def whole_kernel(names, count, side, z_size, *refs):
    k = Refs(names, refs, count, side)
    n = Links(k.send_sems, k.recv_sems, k.local_sems)
    arrived = n.greet()
    vectors_copy = n.local(k.vectors_in, k.vectors)
    steps_copy = n.local(k.steps_in, k.steps)
    x_copy = n.local(k.x_in, k.x)
    table_copy = n.local(k.time_table, k.table)
    cot_copy = n.local(k.cot_in, k.cot)
    gathers = SimpleNamespace(**{
        name: tuple(
            Gather(
                n,
                box,
                getattr(k, "shard_" + name),
                getattr(k, "full_" + name),
                parts=name in ("first", "second"),
            )
            for box in boxes
        )
        for name, boxes in BOXES.items()
    })
    reduces = SimpleNamespace()
    for name, early in EARLY.items():
        pair = tuple(
            Reduce(
                n,
                box,
                early[box.core],
                getattr(k, "grad_" + name),
                getattr(k, "total_" + name),
                [getattr(k, f"reduce_{name}_{box.core}_{i}") for i in range(6)],
            )
            for box in BOXES[name]
        )
        setattr(reduces, name, pair)
    first, second = gathers.first, gathers.second

    arrived()
    on_both(n, (first, "start"), (first, "start_own"))
    vectors_copy.wait()
    width = k.vectors.shape[1]
    lane = lax.broadcasted_iota(jnp.int32, (width, 128), 1)
    row = lax.broadcasted_iota(jnp.int32, (width, 128), 0)
    place = jnp.where(lane == row + lax.rem(n.f * width, 128), 1.0, 0.0).astype(BF16)
    own_vec = dot(k.vectors[...], place).astype(BF16)
    k.vec_own[...] = jnp.concatenate([own_vec, jnp.zeros((4, 128), BF16)], axis=0)

    def vec_route(peer):
        return lambda: (k.vec_own, k.vec_all.at[n.z, n.y], peer)

    on_both(n, (gathers.embed, "start"))
    vec_arrival = n.send_all(
        [vec_route(peer) for peer in n.at_z[1:] + n.across_z], lambda: k.vec_room
    )
    on_both(n, (second, "start_own"))
    vec_own = n.local(k.vec_own, k.vec_all.at[n.z, n.y])
    own_first = n.local(k.shard_first, k.full_first.at[n.z, n.y])
    own_second = n.local(k.shard_second, k.full_second.at[n.z, n.y])
    start_compute(k)
    steps_copy.wait()
    table_copy.wait()
    for m in range(count):
        row = k.table[pl.ds(k.steps[m], 1), :]
        k.pre[m : m + 1, :] = row
        k.extra[m : m + 1, 0:HALF] = row[:, 0:HALF]
        k.extra[m + 4 : m + 5, 0:HALF] = row[:, HALF:TEMB]
        when = jnp.full((1, EXTRA - HALF), k.steps[m].astype(F32), F32)
        k.extra[m : m + 1, HALF:EXTRA] = when
        k.extra[m + 4 : m + 5, HALF:EXTRA] = when
    extras = SmallGather(n, k.extra, k.extra_all)
    on_both(n, (first, "spread", 1), (second, "start"), (first, "spread", 2, 3))
    vec_own.wait()
    x_copy.wait()
    vec_arrival()
    per_half = 2 * z_size // 2
    for half in range(2):
        total = k.vec_all[half * per_half // 2, 0].astype(F32)
        for i in range(half * per_half + 1, (half + 1) * per_half):
            total = total + k.vec_all[i // 2, i % 2].astype(F32)
        k.vec[:, half * 128 : (half + 1) * 128] = total
    on_both(n, (gathers.embed, "spread"), (gathers.mixed, "start"), (gathers.out, "start"))
    extras.start()
    on_both(n, (second, "spread", 1))
    each_map(k, first_norm)
    on_both(n, (first, "share_own"), (first, "share", 1, 2, 3), (second, "spread", 2, 3))
    for gather in first:
        gather.finish()
    own_first.wait()
    k.w_first = k.full_first.reshape(TAPS, WIDTH)
    k.w_second = k.full_second.reshape(TAPS, WIDTH)
    k.w_embed = k.full_embed.reshape(TEMB, WIDTH)
    k.w_mixed = k.full_mixed.reshape(WIDTH, 3 * WIDTH)
    k.w_out = k.full_out.reshape(WIDTH, WIDTH)
    each_map(k, first_conv)
    on_both(
        n,
        (gathers.mixed, "spread"),
        (gathers.out, "spread"),
        (gathers.embed, "share"),
        (second, "share_own"),
        (second, "share", 1),
    )
    for gather in gathers.embed:
        gather.finish()
    embed(k, k.pre[...])
    each_map(k, second_norm)
    on_both(n, (second, "share", 2, 3))
    for gather in second:
        gather.finish()
    own_second.wait()
    each_map(k, second_conv)
    on_both(n, (gathers.mixed, "share"), (gathers.out, "share"))
    extras.spread()
    each_map(k, third_norm)
    cot_copy.wait()
    for gather in gathers.mixed + gathers.out:
        gather.finish()
    each_map(k, *ATTENTION[1:])

    g_out = k.grad_out.reshape(WIDTH, WIDTH)
    g_mixed = k.grad_mixed.reshape(WIDTH, 3 * WIDTH)
    g_second = k.grad_second.reshape(TAPS, WIDTH)
    g_first = k.grad_first.reshape(TAPS, WIDTH)
    first, second, mixed, out = reduces.first, reduces.second, reduces.mixed, reduces.out
    g_out[...] = dot(k.att_t[...], k.cot[...]).astype(BF16)
    g_mixed[...] = dot(k.nrm_t[...], k.g_mixed[...]).astype(BF16)
    on_both(n, (out[::-1], "start"), (mixed[::-1], "start"))
    each_map(k, third_norm_back)
    on_both(n, (out, "pair"), (mixed, "pair"))
    extras.share()
    grad_and_start(k, n, k.a2_t, g_second, second)
    on_both(n, (second, "pair", 0, 1))
    each_map(k, second_conv_back)
    on_both(n, (second, "pair", 2, 3))
    each_map(k, second_norm_back)
    sends = SmallGather(n, k.g_proj, k.g_proj_all)
    sends.start()
    on_both(n, (out, "middle_late"), (mixed, "middle_late"))
    grad_and_start(k, n, k.a1_t, g_first, first)
    on_both(n, (first, "pair", 0, 1))
    each_map(k, first_conv_back)
    on_both(
        n,
        (first, "pair", 2, 3),
        (second, "middle_early"),
        (second, "middle_late", 0, 1, 2, 3),
    )
    each_map(k, first_norm_back)
    sums = SmallSum(n, k.sums, k.sums_land)
    sums.cores()
    on_both(n, (out, "owner"), (mixed, "owner"))
    sends.spread()
    sums.add_core()
    sums.over_z()
    on_both(
        n,
        (first, "middle_late", 0, 1),
        (first, "middle_early"),
        (first, "middle_late", 2, 3),
        (second, "owner"),
    )
    sums.add(1)
    sums.over_sides()
    on_both(n, (first, "owner"))
    sends.share()
    sends.finish()
    extras.finish()

    devices = 4 * 2 * z_size
    g_proj = k.g_proj_all[...].reshape(devices * 8, WIDTH)
    upper = lax.broadcasted_iota(jnp.int32, (devices * 8, 1), 0) % 8 < 4
    extra = k.extra_all[...].reshape(devices * 8, EXTRA)
    pre = extra[:, 0:HALF]
    sig = jax.nn.sigmoid(pre)
    e = pre * sig
    e_t = e.astype(BF16).T
    k.g_embed_all[0:HALF, :] = dot(e_t, jnp.where(upper, g_proj, 0.0).astype(BF16))
    k.g_embed_all[HALF:TEMB, :] = dot(e_t, jnp.where(upper, 0.0, g_proj).astype(BF16))
    g_e = dot_nt(g_proj.astype(BF16), k.w_embed[...])
    g_e = jnp.where(upper, g_e[:, 0:HALF], g_e[:, HALF:TEMB])
    k.g_pre[...] = g_e * (sig + e * (1.0 - sig))
    k.when[...] = extra[:, HALF:EXTRA].T[0:8, :]
    rows = TEMB // (2 * z_size)
    k.embed[...] = k.g_embed_all[pl.ds(pl.multiple_of(n.f * rows, rows), rows), :]
    sums.add(4)
    k.sums_total[...] = k.sums[...]
    for pair, total, result in (
        (out, k.total_out, k.out_total),
        (mixed, k.total_mixed, k.mixed_total),
        (second, k.total_second, k.second_total),
        (first, k.total_first, k.first_total),
    ):
        for part in pair:
            part.finish()
        result[...] = total[...]
    n.finish()


def finish_kernel(names, *refs):
    k = Refs(names, refs, 1, 1)
    stores = []

    def store(src, dst):
        copy = pltpu.make_async_copy(src, dst, k.sems.at[len(stores)])
        copy.start()
        stores.append(copy)

    store(k.out_done, k.out_final)
    store(k.image_grad_done, k.image_final)
    high, mid, low = split3(k.g_pre_done[...])
    when = k.when_done[0:1, :]
    steps = k.table.shape[0]
    chunk = 256
    for begin in range(0, steps, chunk):
        size = min(chunk, steps - begin)
        t = lax.broadcasted_iota(jnp.int32, (size, when.shape[1]), 0).astype(F32) + begin
        hit = t == when
        upper = lax.broadcasted_iota(jnp.int32, hit.shape, 1) % 8 < 4
        block = slice(begin, begin + size)
        for half, rows in enumerate((upper, jnp.logical_not(upper))):
            selector = jnp.where(jnp.logical_and(hit, rows), 1.0, 0.0).astype(BF16)
            k.table[block, half * HALF : (half + 1) * HALF] = (
                dot(selector, high) + dot(selector, mid) + dot(selector, low)
            )
        store(k.table.at[block, :], k.table_grad.at[block, :])
    store(k.embed_done, k.embed_grad)
    for total, wide, out in (
        (k.out_total_done, k.out_wide, k.out_total_grad),
        (k.mixed_total_done, k.mixed_wide, k.mixed_total_grad),
        (k.second_total_done, k.second_wide, k.second_total_grad),
        (k.first_total_done, k.first_wide, k.first_total_grad),
    ):
        wide[...] = total[...].astype(F32)
        store(wide, out)
    width = k.vec_grad.shape[1]
    shift = lax.rem(WIDTH - lax.axis_index(FSDP) * width, WIDTH)
    k.vec_wide[...] = pltpu.roll(k.sums_total_done[...], shift, 1)[0 : k.vec_grad.shape[0], 0:width]
    store(k.vec_wide, k.vec_grad)
    for copy in stores:
        copy.wait()


def fused(image, timesteps, time_table, conv_first, embed_weight, conv_second, qkv_weight, out_weight, vectors, cotangent):
    count, side = image.shape[:2]
    total = count * side * side
    z_size = lax.axis_size(FSDP) // 2
    slots = 4 * 2 * z_size * 8
    inputs = dict(
        x_in=image.reshape(total, WIDTH),
        cot_in=cotangent.reshape(total, WIDTH),
        steps_in=timesteps,
        time_table=time_table,
        shard_first=conv_first,
        shard_embed=embed_weight,
        shard_second=conv_second,
        shard_mixed=qkv_weight,
        shard_out=out_weight,
        vectors_in=vectors,
    )
    between = dict(
        g_pre=((slots, HALF), F32),
        when=((8, slots), F32),
        out=((total, WIDTH), BF16),
        image_grad=((total, WIDTH), BF16),
        embed=(embed_weight.shape, F32),
        out_total=(out_weight.shape, BF16),
        mixed_total=(qkv_weight.shape, BF16),
        second_total=(conv_second.shape, BF16),
        first_total=(conv_first.shape, BF16),
        sums_total=((16, WIDTH), F32),
    )
    scratch = scratch_of(count, side)
    for name in ("x", "cot"):
        scratch[name] = ((total, WIDTH), BF16)
    for name, (rows, lanes, _) in SHARDS.items():
        scratch["full_" + name] = ((z_size, 2, rows, lanes), BF16)
        if name not in EARLY:
            continue
        scratch["grad_" + name] = ((z_size, 2, rows, lanes), BF16)
        scratch["total_" + name] = ((rows, lanes), BF16)
        for box in BOXES[name]:
            bufs = Reduce.buffers(box, EARLY[name][box.core], z_size)
            for i, buf in enumerate(bufs):
                scratch[f"reduce_{name}_{box.core}_{i}"] = buf
    scratch.update(vectors=(vectors.shape, BF16))
    scratch.update(table=(time_table.shape, F32))
    scratch.update(pre=((8, TEMB), F32))
    scratch.update(extra=((8, EXTRA), F32))
    scratch.update(extra_all=((z_size, 2, 2, 2, 8, EXTRA), F32))
    scratch.update(g_proj_all=((z_size, 2, 2, 2, 8, WIDTH), F32))
    scratch.update(g_embed_all=((TEMB, WIDTH), F32))
    scratch.update(vec_own=((16, 128), BF16))
    scratch.update(vec_room=((2 * z_size - 1, 16, 128), BF16))
    scratch.update(vec_all=((z_size, 2, 16, 128), BF16))
    scratch.update(vec=((16, WIDTH), F32))
    scratch.update(sums_land=((7, 16, WIDTH), F32))
    sems = dict(send_sems=2 * SENDS, recv_sems=LANDINGS + CORE_LANDINGS, local_sems=LOCALS)
    names = list(inputs) + list(between) + list(scratch) + list(sems) + ["steps"]
    anywhere = pl.BlockSpec(memory_space=pl.ANY)
    results = pl.pallas_call(
        functools.partial(whole_kernel, names, count, side, z_size),
        out_shape=[pltpu.VMEM(*v) for v in between.values()],
        in_specs=[anywhere] * len(inputs),
        out_specs=[pl.BlockSpec(memory_space=pltpu.VMEM)] * len(between),
        scratch_shapes=[pltpu.VMEM(*v) for v in scratch.values()]
        + [pltpu.SemaphoreType.DMA((size,)) for size in sems.values()]
        + [pltpu.SMEM(timesteps.shape, jnp.int32)],
        compiler_params=pltpu.CompilerParams(
            collective_id=0, has_side_effects=True, vmem_limit_bytes=VMEM_BYTES
        ),
        name="block",
    )(*inputs.values())

    outputs = dict(
        out_final=((total, WIDTH), BF16),
        image_final=((total, WIDTH), BF16),
        table_grad=(time_table.shape, F32),
        first_total_grad=(conv_first.shape, F32),
        embed_grad=(embed_weight.shape, F32),
        second_total_grad=(conv_second.shape, F32),
        mixed_total_grad=(qkv_weight.shape, F32),
        out_total_grad=(out_weight.shape, F32),
        vec_grad=(vectors.shape, F32),
    )
    scratch = dict(
        table=(time_table.shape, F32),
        vec_wide=(vectors.shape, F32),
        out_wide=(out_weight.shape, F32),
        mixed_wide=(qkv_weight.shape, F32),
        second_wide=(conv_second.shape, F32),
        first_wide=(conv_first.shape, F32),
    )
    names = [name + "_done" for name in between] + list(outputs) + list(scratch) + ["sems"]
    results = pl.pallas_call(
        functools.partial(finish_kernel, names),
        out_shape=[jax.ShapeDtypeStruct(*v) for v in outputs.values()],
        in_specs=[pl.BlockSpec(memory_space=pltpu.VMEM)] * len(between),
        out_specs=[anywhere] * len(outputs),
        scratch_shapes=[pltpu.VMEM(*v) for v in scratch.values()]
        + [pltpu.SemaphoreType.DMA((16,))],
        compiler_params=pltpu.CompilerParams(vmem_limit_bytes=VMEM_BYTES),
        name="finish",
    )(*[pltpu.with_memory_space_constraint(r, pltpu.VMEM) for r in results])
    out, image_grad, *rest = results
    return (out.reshape(image.shape), image_grad.reshape(image.shape), *rest)


def local_kernel(names, count, side, *refs):
    k = Refs(names, refs, count, side)
    start_compute(k)
    embed(k, k.pre[...])
    each_map(k, first_norm, first_conv, second_norm, second_conv, *ATTENTION)
    k.grad_out[...] = dot(k.att_t[...], k.cot[...]).astype(BF16)
    k.grad_mixed[...] = dot(k.nrm_t[...], k.g_mixed[...]).astype(BF16)
    each_map(k, third_norm_back)
    for ky in range(3):
        kernel_grad(k, k.a2_t, k.grad_second, ky)
    each_map(k, second_conv_back, second_norm_back)
    for ky in range(3):
        kernel_grad(k, k.a1_t, k.grad_first, ky)
    each_map(k, first_conv_back, first_norm_back)
    k.vec_grad[...] = k.sums[...]
    k.g_proj_out[...] = k.g_proj[...]


def plain(image, timesteps, time_table, conv_first, embed_weight, conv_second, qkv_weight, out_weight, vectors, cotangent):
    count, side = image.shape[:2]
    total = count * side * side

    def whole(w, axis=0):
        return lax.all_gather(w, FSDP, axis=axis, tiled=True)

    pre = time_table[timesteps]
    w_embed = whole(embed_weight)
    inputs = dict(
        x=image.reshape(total, WIDTH),
        cot=cotangent.reshape(total, WIDTH),
        w_first=whole(conv_first),
        w_embed=w_embed,
        w_second=whole(conv_second),
        w_mixed=whole(qkv_weight),
        w_out=whole(out_weight),
        vec=jnp.pad(whole(vectors, 1).astype(F32), ((0, 4), (0, 0))),
        pre=jnp.pad(pre, ((0, 8 - count), (0, 0))),
    )
    outputs = dict(
        out=((total, WIDTH), BF16),
        image_grad=((total, WIDTH), BF16),
        grad_first=((TAPS, WIDTH), BF16),
        grad_second=((TAPS, WIDTH), BF16),
        grad_mixed=((WIDTH, 3 * WIDTH), BF16),
        grad_out=((WIDTH, WIDTH), BF16),
        vec_grad=((16, WIDTH), F32),
        g_proj_out=((8, WIDTH), F32),
    )
    scratch = scratch_of(count, side)
    names = list(inputs) + list(outputs) + list(scratch)
    vmem = pl.BlockSpec(memory_space=pltpu.VMEM)
    results = pl.pallas_call(
        functools.partial(local_kernel, names, count, side),
        out_shape=[jax.ShapeDtypeStruct(*v) for v in outputs.values()],
        in_specs=[vmem] * len(inputs),
        out_specs=[vmem] * len(outputs),
        scratch_shapes=[pltpu.VMEM(*v) for v in scratch.values()],
        compiler_params=pltpu.CompilerParams(vmem_limit_bytes=VMEM_BYTES),
        name="block_alone",
    )(*inputs.values())
    out, image_grad, g_first, g_second, g_mixed, g_out, g_vec, g_proj = results
    g_proj = g_proj[:count].astype(BF16)

    def owned(g, axis=0):
        own = lax.psum_scatter(g.astype(BF16), FSDP, scatter_dimension=axis, tiled=True)
        return lax.psum(own, DP).astype(F32)

    e = (pre * jax.nn.sigmoid(pre)).astype(BF16)
    g_embed = lax.dot_general(e, g_proj, TN, preferred_element_type=F32)
    sig = jax.nn.sigmoid(pre)
    g_pre = dot_nt(g_proj, w_embed) * (sig * (1.0 + pre * (1.0 - sig)))
    rows = lax.all_gather(g_pre, (FSDP, DP), axis=0, tiled=True)
    where = lax.all_gather(timesteps, (FSDP, DP), axis=0, tiled=True)
    table_grad = jnp.zeros(time_table.shape, F32).at[where].add(rows)
    return (
        out.reshape(image.shape),
        image_grad.reshape(image.shape),
        table_grad,
        owned(g_first),
        owned(g_embed),
        owned(g_second),
        owned(g_mixed),
        owned(g_out),
        owned(g_vec[: vectors.shape[0]], 1),
    )


def solution(mesh):
    placed = (
        P((FSDP, DP), None, None, None),
        P((FSDP, DP)),
        P(),
        P(FSDP, None),
        P(FSDP, None),
        P(FSDP, None),
        P(FSDP, None),
        P(FSDP, None),
        P(None, FSDP),
        P((FSDP, DP), None, None, None),
    )
    grid = (mesh.shape[FSDP], mesh.shape[DP])
    return jax.shard_map(
        fused if grid == (8, 4) else plain,
        mesh=mesh,
        in_specs=placed,
        out_specs=(
            P((FSDP, DP), None, None, None),
            P((FSDP, DP), None, None, None),
            P(),
            P(FSDP, None),
            P(FSDP, None),
            P(FSDP, None),
            P(FSDP, None),
            P(FSDP, None),
            P(None, FSDP),
        ),
        check_vma=False,
    )
```

```python
import functools
from types import SimpleNamespace

import jax
import jax.numpy as jnp
from jax import lax
from jax.experimental import pallas as pl
from jax.experimental.pallas import tpu as pltpu
from jax.sharding import PartitionSpec as P

FSDP, DP = "fsdp", "dp"
F32 = jnp.float32
BF16 = jnp.bfloat16
MESH = pl.DeviceIdType.MESH
EPS = 1e-06
WIDTH = 256
GROUP = 8
TEMB = 512
TAPS = 9 * WIDTH
HALF = TEMB // 2
EXTRA = HALF + 128
VMEM_BYTES = 56 * 2**20
NT = (((1,), (1,)), ((), ()))
TN = (((0,), (0,)), ((), ()))


def dot(a, b):
    return jnp.dot(a, b, preferred_element_type=F32)


def dot_nt(a, b):
    return lax.dot_general(a, b, NT, preferred_element_type=F32)


def split3(v):
    high = v.astype(BF16)
    rest = v - high.astype(F32)
    mid = rest.astype(BF16)
    return high, mid, (rest - mid.astype(F32)).astype(BF16)


def colsum(v):
    return jnp.sum(v, axis=0, keepdims=True)


def group_mean(row, averager):
    high, mid, low = split3(row)
    return dot(high, averager) + dot(mid, averager) + dot(low, averager)


class Refs:
    def __init__(self, names, refs, count, side):
        for name, ref in zip(names, refs):
            setattr(self, name, ref)
        self.count, self.side, self.places = count, side, side * side

    def rows(self, m):
        return pl.ds(m * self.places, self.places)


def scratch_of(count, side):
    places = side * side
    total = count * places
    padded = places + 2 * side
    return dict(
        averager=((WIDTH, WIDTH), BF16),
        shifted_a=((count, padded, 3 * WIDTH), BF16),
        shifted_g=((count, padded, 3 * WIDTH), BF16),
        unit1=((total, WIDTH), F32),
        slope1=((total, WIDTH), F32),
        inv1=((count, 1, WIDTH), F32),
        unit2=((total, WIDTH), F32),
        slope2=((total, WIDTH), F32),
        inv2=((count, 1, WIDTH), F32),
        unit3=((total, WIDTH), F32),
        inv3=((count, 1, WIDTH), F32),
        a1_t=((WIDTH, total), BF16),
        a2_t=((WIDTH, total), BF16),
        nrm_t=((WIDTH, total), BF16),
        att_t=((WIDTH, total), BF16),
        nrm=((total, WIDTH), BF16),
        mixed=((total, 3 * WIDTH), BF16),
        g_att=((total, WIDTH), BF16),
        probs=((total, places), F32),
        probs_low=((total, places), BF16),
        probs_t=((places, total), BF16),
        att=((total, WIDTH), BF16),
        g_probs=((total, places), F32),
        g_scores=((total, places), BF16),
        g_scores_t=((places, total), BF16),
        conv_out=((total, WIDTH), F32),
        resid=((total, WIDTH), F32),
        g_mixed=((total, 3 * WIDTH), BF16),
        proj=((8, WIDTH), F32),
        sums=((16, WIDTH), F32),
        g_proj=((8, WIDTH), F32),
    )


def start_compute(k):
    rows = lax.broadcasted_iota(jnp.int32, (WIDTH, WIDTH), 0) // GROUP
    cols = lax.broadcasted_iota(jnp.int32, (WIDTH, WIDTH), 1) // GROUP
    k.averager[...] = jnp.where(rows == cols, 1.0 / (k.places * GROUP), 0.0).astype(BF16)
    edge = jnp.zeros((k.count, k.side, 3 * WIDTH), BF16)
    for ref in (k.shifted_a, k.shifted_g):
        ref[:, 0 : k.side, :] = edge
        ref[:, k.places + k.side : k.places + 2 * k.side, :] = edge
    k.sums[...] = jnp.zeros(k.sums.shape, F32)
    k.g_proj[...] = jnp.zeros(k.g_proj.shape, F32)


def store_shifted(k, ref, m, a):
    column = lax.broadcasted_iota(jnp.int32, a.shape, 0) % k.side
    inner = slice(k.side, k.side + k.places)
    left = jnp.where(column == 0, 0.0, pltpu.roll(a, 1, 0))
    right = jnp.where(column == k.side - 1, 0.0, pltpu.roll(a, k.places - 1, 0))
    ref[m, inner, 0:WIDTH] = left.astype(BF16)
    ref[m, inner, WIDTH : 2 * WIDTH] = a.astype(BF16)
    ref[m, inner, 2 * WIDTH : 3 * WIDTH] = right.astype(BF16)


def normalize(k, u):
    averager = k.averager[...]
    centered = u - group_mean(colsum(u), averager)
    inverse = lax.rsqrt(group_mean(colsum(centered * centered), averager) + EPS)
    return centered * inverse, inverse


def norm_swish(k, u, m, j, unit_ref, slope_ref, inv_ref):
    unit, inverse = normalize(k, u)
    unit_ref[k.rows(m), :] = unit
    inv_ref[m] = inverse
    h = unit * (1.0 + k.vec[j : j + 1, :]) + k.vec[j + 1 : j + 2, :]
    sig = jax.nn.sigmoid(h)
    a = h * sig
    slope_ref[k.rows(m), :] = sig + a * (1.0 - sig)
    return a


def norm_back(k, upstream, unit, inverse, j):
    averager = k.averager[...]
    g_gain = colsum(upstream * unit)
    g_shift = colsum(upstream)
    k.sums[j : j + 1, :] += g_gain
    k.sums[j + 1 : j + 2, :] += g_shift
    gain = 1.0 + k.vec[j : j + 1, :]
    first = group_mean(g_shift * gain, averager)
    second = group_mean(g_gain * gain, averager)
    return inverse * (upstream * gain - first - unit * second)


def convolve(k, ref, w, m):
    total = None
    for ky in range(3):
        window = ref[m, ky * k.side : ky * k.side + k.places, :]
        term = dot(window, w[ky * 3 * WIDTH : (ky + 1) * 3 * WIDTH, :])
        total = term if total is None else total + term
    return total


def convolve_back(k, ref, w, m):
    total = None
    for ky in range(3):
        for kx in range(3):
            window = ref[
                m,
                (2 - ky) * k.side : (2 - ky) * k.side + k.places,
                (2 - kx) * WIDTH : (3 - kx) * WIDTH,
            ]
            tap = 3 * ky + kx
            term = dot_nt(window, w[tap * WIDTH : (tap + 1) * WIDTH, :])
            total = term if total is None else total + term
    return total


def kernel_grad(k, a_t, g_w, ky):
    start = (2 - ky) * k.side
    row = ky * 3 * WIDTH
    if not isinstance(ky, int):
        start, row = pl.multiple_of(start, k.side), pl.multiple_of(row, WIDTH)
    window = k.shifted_g[:, pl.ds(start, k.places), :]
    term = dot(a_t[...], window.reshape(k.count * k.places, 3 * WIDTH))
    for kx in range(3):
        g_w[pl.ds(row + kx * WIDTH, WIDTH), :] = term[
            :, (2 - kx) * WIDTH : (3 - kx) * WIDTH
        ].astype(BF16)


def first_norm(k, m):
    a = norm_swish(k, k.x[k.rows(m), :].astype(F32), m, 0, k.unit1, k.slope1, k.inv1)
    store_shifted(k, k.shifted_a, m, a)
    k.a1_t[:, k.rows(m)] = a.astype(BF16).T


def embed(k, pre):
    e = (pre * jax.nn.sigmoid(pre)).astype(BF16)
    k.proj[...] = dot(e, k.w_embed[...]) + k.vec[3:4, :]


def first_conv(k, m):
    k.conv_out[k.rows(m), :] = convolve(k, k.shifted_a, k.w_first, m)


def second_norm(k, m):
    h1 = k.conv_out[k.rows(m), :] + (k.vec[2:3, :] + k.proj[m : m + 1, :])
    a = norm_swish(k, h1, m, 4, k.unit2, k.slope2, k.inv2)
    store_shifted(k, k.shifted_a, m, a)
    k.a2_t[:, k.rows(m)] = a.astype(BF16).T


def second_conv(k, m):
    x = k.x[k.rows(m), :].astype(F32)
    k.resid[k.rows(m), :] = x + convolve(k, k.shifted_a, k.w_second, m) + k.vec[6:7, :]


def third_norm(k, m):
    rows = k.rows(m)
    unit, inverse = normalize(k, k.resid[rows, :])
    k.unit3[rows, :] = unit
    k.inv3[m] = inverse
    nrm = (unit * (1.0 + k.vec[7:8, :]) + k.vec[8:9, :]).astype(BF16)
    k.nrm[rows, :] = nrm
    k.nrm_t[:, rows] = nrm.T


def project(k, m):
    rows = k.rows(m)
    mixed = dot(k.nrm[rows, :], k.w_mixed[...])
    k.mixed[rows, 0:WIDTH] = (mixed[:, :WIDTH] + k.vec[9:10, :]).astype(BF16)
    k.mixed[rows, WIDTH : 2 * WIDTH] = mixed[:, WIDTH : 2 * WIDTH].astype(BF16)
    k.mixed[rows, 2 * WIDTH :] = (mixed[:, 2 * WIDTH :] + k.vec[10:11, :]).astype(BF16)


def upstream(k, m):
    cot = k.cot[k.rows(m), :]
    k.sums[11:12, :] += colsum(cot.astype(F32))
    k.g_att[k.rows(m), :] = dot_nt(cot, k.w_out[...]).astype(BF16)


def softmax(k, m):
    rows = k.rows(m)
    scores = dot_nt(k.mixed[rows, 0:WIDTH], k.mixed[rows, WIDTH : 2 * WIDTH]) * WIDTH**-0.5
    raised = jnp.exp(scores - jnp.max(scores, axis=1, keepdims=True))
    probs = raised * (1.0 / jnp.sum(raised, axis=1, keepdims=True))
    k.probs[rows, :] = probs
    low = probs.astype(BF16)
    k.probs_low[rows, :] = low
    k.probs_t[:, rows] = low.T


def attend(k, m):
    rows = k.rows(m)
    value = k.mixed[rows, 2 * WIDTH :]
    att = dot(k.probs_low[rows, :], value).astype(BF16)
    k.att[rows, :] = att
    k.att_t[:, rows] = att.T
    k.g_probs[rows, :] = dot_nt(k.g_att[rows, :], value)


def emit(k, m):
    rows = k.rows(m)
    branch = dot(k.att[rows, :], k.w_out[...])
    k.out[rows, :] = (k.resid[rows, :] + branch + k.vec[11:12, :]).astype(BF16)


def softmax_back(k, m):
    rows = k.rows(m)
    probs, g_probs = k.probs[rows, :], k.g_probs[rows, :]
    weighted = jnp.sum(probs * g_probs, axis=1, keepdims=True)
    g_scores = (probs * (g_probs - weighted)).astype(BF16)
    k.g_scores[rows, :] = g_scores
    k.g_scores_t[:, rows] = g_scores.T
    g_value = dot(k.probs_t[:, rows], k.g_att[rows, :]).astype(BF16)
    k.sums[10:11, :] += colsum(g_value.astype(F32))
    k.g_mixed[rows, 2 * WIDTH :] = g_value


def project_back(k, m):
    rows = k.rows(m)
    scale = WIDTH**-0.5
    g_query = (dot(k.g_scores[rows, :], k.mixed[rows, WIDTH : 2 * WIDTH]) * scale).astype(BF16)
    g_key = (dot(k.g_scores_t[:, rows], k.mixed[rows, 0:WIDTH]) * scale).astype(BF16)
    k.sums[9:10, :] += colsum(g_query.astype(F32))
    k.g_mixed[rows, 0:WIDTH] = g_query
    k.g_mixed[rows, WIDTH : 2 * WIDTH] = g_key


ATTENTION = (third_norm, project, upstream, softmax, attend, emit, softmax_back, project_back)


def third_norm_back(k, m):
    rows = k.rows(m)
    g_nrm = dot_nt(k.g_mixed[rows, :], k.w_mixed[...])
    g_resid = k.cot[rows, :].astype(F32) + norm_back(
        k, g_nrm, k.unit3[rows, :], k.inv3[m], 7
    )
    k.resid[rows, :] = g_resid
    g_conv = g_resid.astype(BF16).astype(F32)
    k.sums[6:7, :] += colsum(g_conv)
    store_shifted(k, k.shifted_g, m, g_conv)


def second_conv_back(k, m):
    rows = k.rows(m)
    k.conv_out[rows, :] = convolve_back(k, k.shifted_g, k.w_second, m) * k.slope2[rows, :]


def second_norm_back(k, m):
    rows = k.rows(m)
    g_h1 = norm_back(k, k.conv_out[rows, :], k.unit2[rows, :], k.inv2[m], 4)
    g_h1 = g_h1.astype(BF16).astype(F32)
    per_map = colsum(g_h1)
    k.sums[2:3, :] += per_map
    g_proj = per_map.astype(BF16).astype(F32)
    k.sums[3:4, :] += g_proj
    k.g_proj[m : m + 1, :] = g_proj
    k.g_proj[m + 4 : m + 5, :] = g_proj
    store_shifted(k, k.shifted_g, m, g_h1)


def first_conv_back(k, m):
    rows = k.rows(m)
    k.conv_out[rows, :] = convolve_back(k, k.shifted_g, k.w_first, m) * k.slope1[rows, :]


def first_norm_back(k, m):
    rows = k.rows(m)
    g_x = norm_back(k, k.conv_out[rows, :], k.unit1[rows, :], k.inv1[m], 0)
    k.image_grad[rows, :] = (k.resid[rows, :] + g_x).astype(BF16)


def each_map(k, *steps):
    for step in steps:
        for m in range(k.count):
            step(k, m)


class Links:
    def __init__(self, send_sems, recv_sems, local_sems):
        f, d = lax.axis_index(FSDP), lax.axis_index(DP)
        self.f = f
        self.z, self.y, self.x, self.c = f // 2, f % 2, d // 2, d % 2
        self.send_sems, self.recv_sems, self.local_sems = send_sems, recv_sems, local_sems
        self.n_local = 0
        self.core = None
        self.pools = {None: [], 0: [], 1: []}
        self.left = set()
        self.n_landings = {None: 0, 0: 0, 1: 0}
        z, y, x, c = self.z, self.y, self.x, self.c
        self.partners = (z, z + 1 - 2 * (z % 2), (z + 2) % 4, 3 - z)
        upper = z // 2
        self.upper = upper
        self.turns = ((1 - upper) * 3, 2 - upper, self.partners[1], z)
        self.slots = [lax.rem(z + t, 2) + 2 * lax.rem(upper + t // 2, 2) - 1 for t in self.turns[:3]]
        self.other_y, self.other_x = 1 - y, 1 - x
        here, over = (x * 2 + c), (1 - x) * 2 + c
        self.at_z = [(p * 2 + y, here) for p in self.partners]
        self.at_turn = [(p * 2 + y, here) for p in self.turns]
        self.across_z = [(p * 2 + 1 - y, here) for p in self.partners]
        self.x_peer, self.y_peer = (f, over), (z * 2 + 1 - y, here)
        self.diagonal = (z * 2 + 1 - y, over)
        self.core_peer, self.x_core_peer = (f, x * 2 + 1 - c), (f, (1 - x) * 2 + 1 - c)

    def on_core(self, core, *steps):
        def run():
            self.core = core
            for step in steps:
                step()
            self.core = None

        pl.when(self.c == core)(run)

    def landing(self, core=None):
        spot = self.n_landings[core]
        self.n_landings[core] += 1
        return spot if core is None else LANDINGS + spot

    def send(self, route, landing=None):
        core = self.core
        pool = self.pools[core]
        spot = len(pool)
        if spot >= SENDS:
            self.sent(pool[spot - SENDS])
        if landing is None:
            landing = self.landing(core)
        send_sem = spot % SENDS + (0 if core is None else SENDS)

        def copy():
            src, dst, device = route()
            return pltpu.make_async_remote_copy(
                src_ref=src,
                dst_ref=dst,
                send_sem=self.send_sems.at[send_sem],
                recv_sem=self.recv_sems.at[landing],
                device_id=device,
                device_id_type=MESH,
            )

        copy().start()
        pool.append(copy)
        return lambda: copy().wait_recv()

    def send_all(self, routes, room, landing=None):
        if landing is None:
            landing = self.landing(self.core)
        for route in routes:
            self.send(route, landing)
        return self.arrival(landing, room)

    def arrival(self, landing, room):
        def wait():
            block = room()
            pltpu.make_async_copy(block, block, self.recv_sems.at[landing]).wait()

        return wait

    def sent(self, copy):
        if id(copy) not in self.left:
            copy().wait_send()
            self.left.add(id(copy))

    def local(self, src, dst):
        copy = pltpu.make_async_copy(src, dst, self.local_sems.at[self.n_local])
        self.n_local += 1
        copy.start()
        return copy

    def keep(self, route):
        spot = self.n_local
        self.n_local += 1

        def copy():
            return pltpu.make_async_copy(*route(), self.local_sems.at[spot])

        copy().start()
        return lambda: copy().wait()

    def finish(self):
        for core in (0, 1):
            self.on_core(core, *[functools.partial(self.sent, copy) for copy in self.pools[core]])
        for copy in self.pools[None]:
            self.sent(copy)

    def greet(self):
        barrier = pltpu.get_barrier_semaphore()
        peers = self.at_z[1:] + self.across_z
        peers += [self.x_peer, self.core_peer, self.x_core_peer, self.diagonal]
        for peer in peers:
            pl.semaphore_signal(barrier, inc=1, device_id=peer, device_id_type=MESH)
        return lambda: pl.semaphore_wait(barrier, len(peers))


class Box:
    def __init__(self, core, first, rows, lanes):
        self.core, self.rows, self.lanes, self.half = core, rows, lanes, lanes // 2
        self.span = slice(first, first + rows)

    def lanes_of(self, x):
        return pl.ds(pl.multiple_of(x * self.half, 128), self.half)


class Gather:
    def __init__(self, links, box, shard, full, parts=False):
        self.n, self.box, self.shard, self.full = links, box, shard, full
        self.by_parts = parts
        self.mine = box.lanes_of(links.x)
        self.sides = {}
        self.shares = {}

    def start(self):
        n = self.n

        def route(o):
            return lambda: (
                self.shard.at[self.box.span, self.mine],
                self.full.at[n.z, n.y, self.box.span, self.mine],
                n.at_z[o],
            )

        if self.by_parts:
            self.z_arrivals = {o: n.send(route(o)) for o in (1, 2, 3)}
        else:
            self.z_arrivals = {None: n.send_all([route(o) for o in (1, 2, 3)], self.room(1))}
            self.own = n.keep(
                lambda: (self.shard.at[self.box.span, self.mine], self.full.at[n.z, n.y, self.box.span, self.mine])
            )

    def room(self, o):
        rows = slice(0, self.box.rows)
        if o is None:
            return lambda: self.full.at[0:3, :, rows, :]
        return lambda: self.full.at[0:3, 0, rows, 0 : self.box.half]

    def start_own(self):
        n = self.n
        self.own_y = n.send(
            lambda: (
                self.shard.at[self.box.span, :],
                self.full.at[n.z, n.y, self.box.span, :],
                n.y_peer,
            )
        )

    def spot(self, o):
        return slice(None) if o is None else self.n.partners[o]

    def spread(self, *parts):
        n = self.n

        def route(o, peer):
            def block():
                return self.full.at[self.spot(o), n.y, self.box.span, self.mine]

            return lambda: (block(), block(), peer)

        for o in parts or (None,):
            self.z_arrivals[o]()
            if o is None:
                self.own()
            routes = [route(o, peer) for peer in (n.x_peer, n.y_peer, n.diagonal)]
            self.sides[o] = n.send_all(routes, self.room(o))

    def share(self, *parts):
        n = self.n

        def route(o):
            def block():
                return self.full.at[self.spot(o), :, self.box.span, :]

            return lambda: (block(), block(), n.core_peer)

        for o in parts or (None,):
            self.sides[o]()
            self.shares[o] = n.send(route(o), n.landing(1 - self.box.core))

    def share_own(self):
        n = self.n

        def block():
            return self.full.at[n.z, n.other_y, self.box.span, :]

        self.own_y()
        self.shares[0] = n.send(
            lambda: (block(), block(), n.core_peer), n.landing(1 - self.box.core)
        )

    def finish(self):
        self.n.on_core(1 - self.box.core, *self.shares.values())


class SmallGather:
    def __init__(self, links, block, full):
        self.n, self.block, self.full = links, block, full

    def start(self):
        n = self.n

        def route(device):
            return lambda: (self.block, self.full.at[n.z, n.y, n.x, n.c], device)

        routes = [route(n.at_z[o]) for o in (1, 2, 3)]
        self.z_arrivals = n.send_all(routes, lambda: self.full.at[0:3, 0, 0, 0])
        self.own = n.local(self.block, self.full.at[n.z, n.y, n.x, n.c])

    def spread(self):
        n = self.n

        def block():
            return self.full.at[:, n.y, n.x, n.c]

        def route(peer):
            return lambda: (block(), block(), peer)

        self.z_arrivals()
        self.own.wait()
        routes = [route(peer) for peer in (n.x_peer, n.y_peer, n.diagonal)]
        self.sides = n.send_all(routes, lambda: self.full.at[0:3, :, :, 0])

    def share(self):
        n = self.n

        def block():
            return self.full.at[:, :, :, n.c]

        self.sides()
        self.core = n.send(lambda: (block(), block(), n.core_peer))

    def finish(self):
        self.core()


class Reduce:
    def __init__(self, links, box, early, grad, total, bufs):
        self.n, self.box, self.early, self.grad, self.total = links, box, early, grad, total
        self.from_core, self.held, self.z_early, self.sides_early, self.sides_late, self.z_late = bufs
        self.core, self.sides = {}, {}
        n = links
        self.mine, self.others = box.lanes_of(n.x), box.lanes_of(n.other_x)
        self.around = (
            (n.other_y, self.others, n.diagonal),
            (n.other_y, self.mine, n.y_peer),
            (n.y, self.others, n.x_peer),
        )
        self.early_landing = n.landing(box.core) if early else None
        self.late_landing = n.landing(box.core) if early < box.rows else None

    @staticmethod
    def buffers(box, early, z):
        w, late = box.half, max(box.rows - early, 16)
        return [
            ((z, 2, box.rows, box.lanes), BF16),
            ((z, 2, box.rows, box.lanes), BF16),
            ((3, 2, max(early, 16), box.lanes), BF16),
            ((3, max(early, 16), w), BF16),
            ((3, z, late, w), BF16),
            ((3, late, w), BF16),
        ]

    def spot(self, o):
        return slice(None) if o is None else self.n.turns[o]

    def to_z(self, o):
        n = self.n
        if o is None:
            return [(n.partners[k], k - 1, n.at_z[k]) for k in (3, 2, 1)]
        return [] if o == 3 else [(n.turns[o], n.slots[o], n.at_turn[o])]

    def rows(self, late):
        return slice(self.early, self.box.rows) if late else slice(0, self.early)

    def start(self, *parts):
        n = self.n

        def route(p):
            return lambda: (
                self.grad.at[p, :, self.box.span, :],
                self.from_core.at[p],
                n.core_peer,
            )

        for o in parts or (None,):
            self.core[o] = n.send(route(self.spot(o)), n.landing(self.box.core))

    def early_route(self, z, slot, device):
        return lambda: (self.held.at[z, :, self.rows(False), :], self.z_early.at[slot], device)

    def late_route(self, z, slot, device):
        return lambda: (
            self.held.at[z, self.n.y, self.rows(True), self.mine],
            self.z_late.at[slot],
            device,
        )

    def side_route(self, p, late, i):
        y, lanes, peer = self.around[i]
        land = self.sides_late if late else self.sides_early
        return lambda: (
            self.held.at[p, y, self.rows(late), lanes],
            land.at[i, p] if late else land.at[i],
            peer,
        )

    def pair(self, *parts):
        n = self.n
        for o in parts or (None,):
            p = self.spot(o)
            self.core[o]()
            self.held[p] = self.grad[p, :, self.box.span, :] + self.from_core[p]
            if self.early:
                for z, slot, device in self.to_z(o):
                    n.send(self.early_route(z, slot, device), self.early_landing)
            if self.early < self.box.rows:
                part = slice(None) if o is None else 0
                self.sides[o] = n.send_all(
                    [self.side_route(p, True, i) for i in range(3)],
                    lambda: self.sides_late.at[:, part],
                )

    def middle_early(self):
        n = self.n
        if not self.early:
            return
        n.arrival(self.early_landing, lambda: self.z_early)()
        at = (n.z, slice(None), self.rows(False), slice(None))
        summed = self.held[at].astype(F32)
        for i in range(3):
            summed = summed + self.z_early[i].astype(F32)
        self.held[at] = summed.astype(BF16)
        self.early_sides = n.send_all(
            [self.side_route(n.z, False, i) for i in range(3)], lambda: self.sides_early
        )

    def middle_late(self, *parts):
        n = self.n
        for o in parts or (None,):
            p = self.spot(o)
            self.sides[o]()
            at = (p, n.y, self.rows(True), self.mine)
            summed = self.held[at].astype(F32)
            for i in range(3):
                summed = summed + self.sides_late[i, p].astype(F32)
            self.held[at] = summed.astype(BF16)
            for z, slot, device in self.to_z(o):
                n.send(self.late_route(z, slot, device), self.late_landing)

    def owner(self):
        n, box = self.n, self.box
        if self.early:
            self.early_sides()
        if self.early < box.rows:
            n.arrival(self.late_landing, lambda: self.z_late)()
        for late, lands in ((False, self.sides_early), (True, self.z_late)):
            rows = self.rows(late)
            if rows.start < rows.stop:
                summed = self.held[n.z, n.y, rows, self.mine].astype(F32)
                for i in range(3):
                    summed = summed + lands[i].astype(F32)
                first = box.span.start
                at = (slice(first + rows.start, first + rows.stop), self.mine)
                self.total[at] = summed.astype(BF16)

        def route(peer):
            def block():
                return self.total.at[box.span, self.mine]

            return lambda: (block(), block(), peer)

        self.replica = n.send(route(n.x_peer))
        self.replicas = n.send_all(
            [route(n.x_core_peer), route(n.core_peer)],
            lambda: self.total.at[box.span, :],
            n.landing(1 - box.core),
        )

    def finish(self):
        n = self.n
        n.on_core(self.box.core, self.replica)
        n.on_core(1 - self.box.core, self.replicas)


class SmallSum:
    def __init__(self, links, block, land):
        self.n, self.block, self.land = links, block, land

    def half(self, z):
        return pl.ds(pl.multiple_of(z // 2 * 128, 128), 128)

    def cores(self):
        n = self.n
        self.arrivals = n.send(lambda: (self.block, self.land.at[0], n.core_peer))
        self.copies = n.pools[None][-1:]

    def add_core(self):
        self.arrivals()
        total = self.block[...] + self.land[0]
        self.n.sent(self.copies[0])
        self.block[...] = total

    def exchange(self, first, lanes, peers):
        n = self.n

        def route(i):
            return lambda: (
                self.block.at[:, lanes[i]],
                self.land.at[first + i, :, 0:128],
                peers[i],
            )

        self.arrivals = n.send_all(
            [route(i) for i in range(3)], lambda: self.land.at[first : first + 3, :, 0:128]
        )
        self.copies = n.pools[None][-3:]

    def over_z(self):
        n = self.n
        self.exchange(1, [self.half(z) for z in n.partners[1:]], n.at_z[1:])

    def over_sides(self):
        n = self.n
        self.exchange(4, [self.half(n.z)] * 3, (n.x_peer, n.y_peer, n.diagonal))

    def add(self, first):
        self.arrivals()
        parts = [self.land[i, :, 0:128] for i in range(first, first + 3)]
        mine = self.half(self.n.z)
        total = (self.block[:, mine] + parts[0]) + (parts[1] + parts[2])
        for copy in self.copies:
            self.n.sent(copy)
        self.block[:, mine] = total


def on_both(n, *steps):
    for core in (0, 1):
        n.on_core(
            core,
            *[functools.partial(getattr(pair[core], step), *rest) for pair, step, *rest in steps],
        )


def grad_and_start(k, n, a_t, g_w, pair):
    for steps, ready in (((0, 1), (0, 1)), ((2,), (2, 3))):
        for step in steps:
            kernel_grad(k, a_t, g_w, (1 - n.upper) * (2 - step) + n.upper * step)
        on_both(n, (pair[::-1], "start", *ready))


SHARDS = dict(
    first=(288, 256, 128),
    embed=(64, 256, 32),
    second=(288, 256, 128),
    mixed=(32, 768, 16),
    out=(32, 256, 16),
)
BOXES = {
    name: (Box(0, 0, cut, lanes), Box(1, cut, rows - cut, lanes))
    for name, (rows, lanes, cut) in SHARDS.items()
}
EARLY = dict(first=(32, 48), second=(32, 16), mixed=(0, 0), out=(0, 0))
SENDS = 24
LANDINGS = 10
CORE_LANDINGS = 67
LOCALS = 16


def whole_kernel(names, count, side, z_size, *refs):
    k = Refs(names, refs, count, side)
    n = Links(k.send_sems, k.recv_sems, k.local_sems)
    arrived = n.greet()
    vectors_copy = n.local(k.vectors_in, k.vectors)
    steps_copy = n.local(k.steps_in, k.steps)
    x_copy = n.local(k.x_in, k.x)
    table_copy = n.local(k.time_table, k.table)
    cot_copy = n.local(k.cot_in, k.cot)
    gathers = SimpleNamespace(**{
        name: tuple(
            Gather(
                n,
                box,
                getattr(k, "shard_" + name),
                getattr(k, "full_" + name),
                parts=name in ("first", "second"),
            )
            for box in boxes
        )
        for name, boxes in BOXES.items()
    })
    reduces = SimpleNamespace()
    for name, early in EARLY.items():
        pair = tuple(
            Reduce(
                n,
                box,
                early[box.core],
                getattr(k, "grad_" + name),
                getattr(k, "total_" + name),
                [getattr(k, f"reduce_{name}_{box.core}_{i}") for i in range(6)],
            )
            for box in BOXES[name]
        )
        setattr(reduces, name, pair)
    first, second = gathers.first, gathers.second

    arrived()
    on_both(n, (first, "start"), (first, "start_own"))
    vectors_copy.wait()
    width = k.vectors.shape[1]
    lane = lax.broadcasted_iota(jnp.int32, (width, 128), 1)
    row = lax.broadcasted_iota(jnp.int32, (width, 128), 0)
    place = jnp.where(lane == row + lax.rem(n.f * width, 128), 1.0, 0.0).astype(BF16)
    own_vec = dot(k.vectors[...], place).astype(BF16)
    k.vec_own[...] = jnp.concatenate([own_vec, jnp.zeros((4, 128), BF16)], axis=0)

    def vec_route(peer):
        return lambda: (k.vec_own, k.vec_all.at[n.z, n.y], peer)

    on_both(n, (gathers.embed, "start"))
    vec_arrival = n.send_all(
        [vec_route(peer) for peer in n.at_z[1:] + n.across_z], lambda: k.vec_room
    )
    on_both(n, (second, "start_own"))
    vec_own = n.local(k.vec_own, k.vec_all.at[n.z, n.y])
    own_first = n.local(k.shard_first, k.full_first.at[n.z, n.y])
    own_second = n.local(k.shard_second, k.full_second.at[n.z, n.y])
    start_compute(k)
    steps_copy.wait()
    table_copy.wait()
    for m in range(count):
        row = k.table[pl.ds(k.steps[m], 1), :]
        k.pre[m : m + 1, :] = row
        k.extra[m : m + 1, 0:HALF] = row[:, 0:HALF]
        k.extra[m + 4 : m + 5, 0:HALF] = row[:, HALF:TEMB]
        when = jnp.full((1, EXTRA - HALF), k.steps[m].astype(F32), F32)
        k.extra[m : m + 1, HALF:EXTRA] = when
        k.extra[m + 4 : m + 5, HALF:EXTRA] = when
    extras = SmallGather(n, k.extra, k.extra_all)
    on_both(n, (first, "spread", 1), (second, "start"), (first, "spread", 2, 3))
    vec_own.wait()
    x_copy.wait()
    vec_arrival()
    per_half = 2 * z_size // 2
    for half in range(2):
        total = k.vec_all[half * per_half // 2, 0].astype(F32)
        for i in range(half * per_half + 1, (half + 1) * per_half):
            total = total + k.vec_all[i // 2, i % 2].astype(F32)
        k.vec[:, half * 128 : (half + 1) * 128] = total
    on_both(n, (gathers.embed, "spread"), (gathers.mixed, "start"), (gathers.out, "start"))
    extras.start()
    on_both(n, (second, "spread", 1))
    each_map(k, first_norm)
    on_both(n, (first, "share_own"), (first, "share", 1, 2, 3), (second, "spread", 2, 3))
    for gather in first:
        gather.finish()
    own_first.wait()
    k.w_first = k.full_first.reshape(TAPS, WIDTH)
    k.w_second = k.full_second.reshape(TAPS, WIDTH)
    k.w_embed = k.full_embed.reshape(TEMB, WIDTH)
    k.w_mixed = k.full_mixed.reshape(WIDTH, 3 * WIDTH)
    k.w_out = k.full_out.reshape(WIDTH, WIDTH)
    each_map(k, first_conv)
    on_both(
        n,
        (gathers.mixed, "spread"),
        (gathers.out, "spread"),
        (gathers.embed, "share"),
        (second, "share_own"),
        (second, "share", 1),
    )
    for gather in gathers.embed:
        gather.finish()
    embed(k, k.pre[...])
    each_map(k, second_norm)
    on_both(n, (second, "share", 2, 3))
    for gather in second:
        gather.finish()
    own_second.wait()
    each_map(k, second_conv)
    on_both(n, (gathers.mixed, "share"), (gathers.out, "share"))
    extras.spread()
    each_map(k, third_norm)
    cot_copy.wait()
    for gather in gathers.mixed + gathers.out:
        gather.finish()
    each_map(k, *ATTENTION[1:])

    g_out = k.grad_out.reshape(WIDTH, WIDTH)
    g_mixed = k.grad_mixed.reshape(WIDTH, 3 * WIDTH)
    g_second = k.grad_second.reshape(TAPS, WIDTH)
    g_first = k.grad_first.reshape(TAPS, WIDTH)
    first, second, mixed, out = reduces.first, reduces.second, reduces.mixed, reduces.out
    g_out[...] = dot(k.att_t[...], k.cot[...]).astype(BF16)
    g_mixed[...] = dot(k.nrm_t[...], k.g_mixed[...]).astype(BF16)
    on_both(n, (out[::-1], "start"), (mixed[::-1], "start"))
    each_map(k, third_norm_back)
    on_both(n, (out, "pair"), (mixed, "pair"))
    grad_and_start(k, n, k.a2_t, g_second, second)
    on_both(n, (second, "pair", 0, 1))
    extras.share()
    each_map(k, second_conv_back)
    on_both(n, (second, "pair", 2, 3))
    each_map(k, second_norm_back)
    sends = SmallGather(n, k.g_proj, k.g_proj_all)
    sends.start()
    on_both(n, (out, "middle_late"), (mixed, "middle_late"))
    grad_and_start(k, n, k.a1_t, g_first, first)
    on_both(n, (first, "pair", 0, 1))
    each_map(k, first_conv_back)
    on_both(
        n,
        (first, "pair", 2, 3),
        (second, "middle_early"),
        (second, "middle_late", 0, 1, 2, 3),
    )
    each_map(k, first_norm_back)
    sums = SmallSum(n, k.sums, k.sums_land)
    sums.cores()
    on_both(n, (out, "owner"), (mixed, "owner"))
    sends.spread()
    sums.add_core()
    sums.over_z()
    on_both(
        n,
        (first, "middle_late", 0, 1),
        (first, "middle_early"),
        (first, "middle_late", 2, 3),
        (second, "owner"),
    )
    sums.add(1)
    sums.over_sides()
    on_both(n, (first, "owner"))
    sends.share()
    sends.finish()
    extras.finish()

    devices = 4 * 2 * z_size
    g_proj = k.g_proj_all[...].reshape(devices * 8, WIDTH)
    upper = lax.broadcasted_iota(jnp.int32, (devices * 8, 1), 0) % 8 < 4
    extra = k.extra_all[...].reshape(devices * 8, EXTRA)
    pre = extra[:, 0:HALF]
    sig = jax.nn.sigmoid(pre)
    e = pre * sig
    e_t = e.astype(BF16).T
    k.g_embed_all[0:HALF, :] = dot(e_t, jnp.where(upper, g_proj, 0.0).astype(BF16))
    k.g_embed_all[HALF:TEMB, :] = dot(e_t, jnp.where(upper, 0.0, g_proj).astype(BF16))
    g_e = dot_nt(g_proj.astype(BF16), k.w_embed[...])
    g_e = jnp.where(upper, g_e[:, 0:HALF], g_e[:, HALF:TEMB])
    k.g_pre[...] = g_e * (sig + e * (1.0 - sig))
    k.when[...] = extra[:, HALF:EXTRA].T[0:8, :]
    rows = TEMB // (2 * z_size)
    k.embed[...] = k.g_embed_all[pl.ds(pl.multiple_of(n.f * rows, rows), rows), :]
    sums.add(4)
    k.sums_total[...] = k.sums[...]
    for pair, total, result in (
        (out, k.total_out, k.out_total),
        (mixed, k.total_mixed, k.mixed_total),
        (second, k.total_second, k.second_total),
        (first, k.total_first, k.first_total),
    ):
        for part in pair:
            part.finish()
        result[...] = total[...]
    n.finish()


def finish_kernel(names, *refs):
    k = Refs(names, refs, 1, 1)
    stores = []

    def store(src, dst):
        copy = pltpu.make_async_copy(src, dst, k.sems.at[len(stores)])
        copy.start()
        stores.append(copy)

    store(k.out_done, k.out_final)
    store(k.image_grad_done, k.image_final)
    store(k.embed_done, k.embed_grad)
    for total, wide, out in (
        (k.out_total_done, k.out_wide, k.out_total_grad),
        (k.mixed_total_done, k.mixed_wide, k.mixed_total_grad),
        (k.second_total_done, k.second_wide, k.second_total_grad),
        (k.first_total_done, k.first_wide, k.first_total_grad),
    ):
        wide[...] = total[...].astype(F32)
        store(wide, out)
    width = k.vec_grad.shape[1]
    shift = lax.rem(WIDTH - lax.axis_index(FSDP) * width, WIDTH)
    k.vec_wide[...] = pltpu.roll(k.sums_total_done[...], shift, 1)[0 : k.vec_grad.shape[0], 0:width]
    store(k.vec_wide, k.vec_grad)
    high, mid, low = split3(k.g_pre_done[...])
    when = k.when_done[0:1, :]
    upper = lax.broadcasted_iota(jnp.int32, when.shape, 1) % 8 < 4
    halves = (jnp.where(upper, when, -1.0), jnp.where(upper, -1.0, when))
    steps = k.table.shape[0]
    chunk = 256
    for begin in range(0, steps, chunk):
        size = min(chunk, steps - begin)
        t = lax.broadcasted_iota(jnp.int32, (size, when.shape[1]), 0).astype(F32) + begin
        block = slice(begin, begin + size)
        for half, own in enumerate(halves):
            selector = jnp.where(t == own, 1.0, 0.0).astype(BF16)
            k.table[block, half * HALF : (half + 1) * HALF] = (
                dot(selector, high) + dot(selector, mid) + dot(selector, low)
            )
        store(k.table.at[block, :], k.table_grad.at[block, :])
    for copy in stores:
        copy.wait()


def fused(image, timesteps, time_table, conv_first, embed_weight, conv_second, qkv_weight, out_weight, vectors, cotangent):
    count, side = image.shape[:2]
    total = count * side * side
    z_size = lax.axis_size(FSDP) // 2
    slots = 4 * 2 * z_size * 8
    inputs = dict(
        x_in=image.reshape(total, WIDTH),
        cot_in=cotangent.reshape(total, WIDTH),
        steps_in=timesteps,
        time_table=time_table,
        shard_first=conv_first,
        shard_embed=embed_weight,
        shard_second=conv_second,
        shard_mixed=qkv_weight,
        shard_out=out_weight,
        vectors_in=vectors,
    )
    between = dict(
        g_pre=((slots, HALF), F32),
        when=((8, slots), F32),
        out=((total, WIDTH), BF16),
        image_grad=((total, WIDTH), BF16),
        embed=(embed_weight.shape, F32),
        out_total=(out_weight.shape, BF16),
        mixed_total=(qkv_weight.shape, BF16),
        second_total=(conv_second.shape, BF16),
        first_total=(conv_first.shape, BF16),
        sums_total=((16, WIDTH), F32),
    )
    scratch = scratch_of(count, side)
    for name in ("x", "cot"):
        scratch[name] = ((total, WIDTH), BF16)
    for name, (rows, lanes, _) in SHARDS.items():
        scratch["full_" + name] = ((z_size, 2, rows, lanes), BF16)
        if name not in EARLY:
            continue
        scratch["grad_" + name] = ((z_size, 2, rows, lanes), BF16)
        scratch["total_" + name] = ((rows, lanes), BF16)
        for box in BOXES[name]:
            bufs = Reduce.buffers(box, EARLY[name][box.core], z_size)
            for i, buf in enumerate(bufs):
                scratch[f"reduce_{name}_{box.core}_{i}"] = buf
    scratch.update(vectors=(vectors.shape, BF16))
    scratch.update(table=(time_table.shape, F32))
    scratch.update(pre=((8, TEMB), F32))
    scratch.update(extra=((8, EXTRA), F32))
    scratch.update(extra_all=((z_size, 2, 2, 2, 8, EXTRA), F32))
    scratch.update(g_proj_all=((z_size, 2, 2, 2, 8, WIDTH), F32))
    scratch.update(g_embed_all=((TEMB, WIDTH), F32))
    scratch.update(vec_own=((16, 128), BF16))
    scratch.update(vec_room=((2 * z_size - 1, 16, 128), BF16))
    scratch.update(vec_all=((z_size, 2, 16, 128), BF16))
    scratch.update(vec=((16, WIDTH), F32))
    scratch.update(sums_land=((7, 16, WIDTH), F32))
    sems = dict(send_sems=2 * SENDS, recv_sems=LANDINGS + CORE_LANDINGS, local_sems=LOCALS)
    names = list(inputs) + list(between) + list(scratch) + list(sems) + ["steps"]
    anywhere = pl.BlockSpec(memory_space=pl.ANY)
    results = pl.pallas_call(
        functools.partial(whole_kernel, names, count, side, z_size),
        out_shape=[pltpu.VMEM(*v) for v in between.values()],
        in_specs=[anywhere] * len(inputs),
        out_specs=[pl.BlockSpec(memory_space=pltpu.VMEM)] * len(between),
        scratch_shapes=[pltpu.VMEM(*v) for v in scratch.values()]
        + [pltpu.SemaphoreType.DMA((size,)) for size in sems.values()]
        + [pltpu.SMEM(timesteps.shape, jnp.int32)],
        compiler_params=pltpu.CompilerParams(
            collective_id=0, has_side_effects=True, vmem_limit_bytes=VMEM_BYTES
        ),
        name="block",
    )(*inputs.values())

    outputs = dict(
        out_final=((total, WIDTH), BF16),
        image_final=((total, WIDTH), BF16),
        table_grad=(time_table.shape, F32),
        first_total_grad=(conv_first.shape, F32),
        embed_grad=(embed_weight.shape, F32),
        second_total_grad=(conv_second.shape, F32),
        mixed_total_grad=(qkv_weight.shape, F32),
        out_total_grad=(out_weight.shape, F32),
        vec_grad=(vectors.shape, F32),
    )
    scratch = dict(
        table=(time_table.shape, F32),
        vec_wide=(vectors.shape, F32),
        out_wide=(out_weight.shape, F32),
        mixed_wide=(qkv_weight.shape, F32),
        second_wide=(conv_second.shape, F32),
        first_wide=(conv_first.shape, F32),
    )
    names = [name + "_done" for name in between] + list(outputs) + list(scratch) + ["sems"]
    results = pl.pallas_call(
        functools.partial(finish_kernel, names),
        out_shape=[jax.ShapeDtypeStruct(*v) for v in outputs.values()],
        in_specs=[pl.BlockSpec(memory_space=pltpu.VMEM)] * len(between),
        out_specs=[anywhere] * len(outputs),
        scratch_shapes=[pltpu.VMEM(*v) for v in scratch.values()]
        + [pltpu.SemaphoreType.DMA((16,))],
        compiler_params=pltpu.CompilerParams(vmem_limit_bytes=VMEM_BYTES),
        name="finish",
    )(*[pltpu.with_memory_space_constraint(r, pltpu.VMEM) for r in results])
    out, image_grad, *rest = results
    return (out.reshape(image.shape), image_grad.reshape(image.shape), *rest)


def local_kernel(names, count, side, *refs):
    k = Refs(names, refs, count, side)
    start_compute(k)
    embed(k, k.pre[...])
    each_map(k, first_norm, first_conv, second_norm, second_conv, *ATTENTION)
    k.grad_out[...] = dot(k.att_t[...], k.cot[...]).astype(BF16)
    k.grad_mixed[...] = dot(k.nrm_t[...], k.g_mixed[...]).astype(BF16)
    each_map(k, third_norm_back)
    for ky in range(3):
        kernel_grad(k, k.a2_t, k.grad_second, ky)
    each_map(k, second_conv_back, second_norm_back)
    for ky in range(3):
        kernel_grad(k, k.a1_t, k.grad_first, ky)
    each_map(k, first_conv_back, first_norm_back)
    k.vec_grad[...] = k.sums[...]
    k.g_proj_out[...] = k.g_proj[...]


def plain(image, timesteps, time_table, conv_first, embed_weight, conv_second, qkv_weight, out_weight, vectors, cotangent):
    count, side = image.shape[:2]
    total = count * side * side

    def whole(w, axis=0):
        return lax.all_gather(w, FSDP, axis=axis, tiled=True)

    pre = time_table[timesteps]
    w_embed = whole(embed_weight)
    inputs = dict(
        x=image.reshape(total, WIDTH),
        cot=cotangent.reshape(total, WIDTH),
        w_first=whole(conv_first),
        w_embed=w_embed,
        w_second=whole(conv_second),
        w_mixed=whole(qkv_weight),
        w_out=whole(out_weight),
        vec=jnp.pad(whole(vectors, 1).astype(F32), ((0, 4), (0, 0))),
        pre=jnp.pad(pre, ((0, 8 - count), (0, 0))),
    )
    outputs = dict(
        out=((total, WIDTH), BF16),
        image_grad=((total, WIDTH), BF16),
        grad_first=((TAPS, WIDTH), BF16),
        grad_second=((TAPS, WIDTH), BF16),
        grad_mixed=((WIDTH, 3 * WIDTH), BF16),
        grad_out=((WIDTH, WIDTH), BF16),
        vec_grad=((16, WIDTH), F32),
        g_proj_out=((8, WIDTH), F32),
    )
    scratch = scratch_of(count, side)
    names = list(inputs) + list(outputs) + list(scratch)
    vmem = pl.BlockSpec(memory_space=pltpu.VMEM)
    results = pl.pallas_call(
        functools.partial(local_kernel, names, count, side),
        out_shape=[jax.ShapeDtypeStruct(*v) for v in outputs.values()],
        in_specs=[vmem] * len(inputs),
        out_specs=[vmem] * len(outputs),
        scratch_shapes=[pltpu.VMEM(*v) for v in scratch.values()],
        compiler_params=pltpu.CompilerParams(vmem_limit_bytes=VMEM_BYTES),
        name="block_alone",
    )(*inputs.values())
    out, image_grad, g_first, g_second, g_mixed, g_out, g_vec, g_proj = results
    g_proj = g_proj[:count].astype(BF16)

    def owned(g, axis=0):
        own = lax.psum_scatter(g.astype(BF16), FSDP, scatter_dimension=axis, tiled=True)
        return lax.psum(own, DP).astype(F32)

    e = (pre * jax.nn.sigmoid(pre)).astype(BF16)
    g_embed = lax.dot_general(e, g_proj, TN, preferred_element_type=F32)
    sig = jax.nn.sigmoid(pre)
    g_pre = dot_nt(g_proj, w_embed) * (sig * (1.0 + pre * (1.0 - sig)))
    rows = lax.all_gather(g_pre, (FSDP, DP), axis=0, tiled=True)
    where = lax.all_gather(timesteps, (FSDP, DP), axis=0, tiled=True)
    table_grad = jnp.zeros(time_table.shape, F32).at[where].add(rows)
    return (
        out.reshape(image.shape),
        image_grad.reshape(image.shape),
        table_grad,
        owned(g_first),
        owned(g_embed),
        owned(g_second),
        owned(g_mixed),
        owned(g_out),
        owned(g_vec[: vectors.shape[0]], 1),
    )


def solution(mesh):
    placed = (
        P((FSDP, DP), None, None, None),
        P((FSDP, DP)),
        P(),
        P(FSDP, None),
        P(FSDP, None),
        P(FSDP, None),
        P(FSDP, None),
        P(FSDP, None),
        P(None, FSDP),
        P((FSDP, DP), None, None, None),
    )
    grid = (mesh.shape[FSDP], mesh.shape[DP])
    return jax.shard_map(
        fused if grid == (8, 4) else plain,
        mesh=mesh,
        in_specs=placed,
        out_specs=(
            P((FSDP, DP), None, None, None),
            P((FSDP, DP), None, None, None),
            P(),
            P(FSDP, None),
            P(FSDP, None),
            P(FSDP, None),
            P(FSDP, None),
            P(FSDP, None),
            P(None, FSDP),
        ),
        check_vma=False,
    )
```
